32 devices in a mesh: replica: 2 (over x), tp: 16 (over z, y, core).
Axes of the slice: x: 2, y: 2, z: 4, core: 2. Of those that a mesh axis runs over, the one named last changes fastest.
Arguments:
- residual: bfloat16 [64, 16384], P(('replica', 'tp')), parts along dimension 0
- queries: bfloat16 [64, 2048], P('replica', 'tp'), parts along dimension 0
- key_rows: bfloat16 [64, 1024], P('replica'), parts along dimension 0
- value_rows: bfloat16 [64, 1024], P('replica'), parts along dimension 0, may hold values from -6 to 6
- out_weight: bfloat16 [2048, 16384], P('tp'), may hold values from -0.125 to 0.125
- norm_gain: float32 [16384], replicated, may hold values from 0.1 to 1.9
- q_weight: bfloat16 [16384, 2048], P(None, 'tp'), may hold values from -0.046875 to 0.046875
Outputs:
- stream_codes: bfloat16 [64, 16384], P(('replica', 'tp')), parts along dimension 0
- stream_scales: float32 [64, 128], P(('replica', 'tp')), parts along dimension 0
- next_queries: bfloat16 [64, 2048], P('replica', 'tp'), parts along dimension 0
The draws below stay inside these ranges and needn't reach their ends.
There are 2 independent parts, one for each index of `replica`. The reference program is written for one: setup_inputs(seed, part) draws one part's arguments, and reference() takes and returns one part's arrays. A program takes and returns all parts, laid end to end along the dimension named above; an argument that names none is the same for every part. Nothing has to cross between parts.
All inputs are finite; a program needn't handle non-finite values. Where the reference program divides by a largest or mean magnitude, that divisor is 1e-20 or more.
Results may differ from the reference program's by a relative error of at most 0.013.
Values may be sent and summed in bfloat16 or wider, within the bound.
No kernel may reach another device: no remote copies, remote signals or barrier semaphores. Data moves between devices by JAX's collectives and lax.ppermute only.
A program may use at most 128 MiB of HBM per device.

```python
import jax
import jax.numpy as jnp
from jax import lax

D = 16384
HD = 128
KVH = 8
QB = 128
HEAD_DEV = 1
HEADS = 16
TOKENS = 32


def shared_keys(key):
    return jax.random.normal(key, (TOKENS, KVH * HD), jnp.float32)


def draw_key_rows(key, part):
    base = shared_keys(key)
    return base.astype(jnp.bfloat16)


def draw_queries(key, part):
    key = jax.random.fold_in(key, 12)
    drawn = jax.random.normal(key, (TOKENS, HEADS * HD), jnp.float32)
    return drawn.astype(jnp.bfloat16)


def draw_residual(key, part):
    key = jax.random.fold_in(key, 13)
    first = jax.random.fold_in(key, 0)
    drawn = jax.random.normal(first, (TOKENS, D), jnp.float32)
    return drawn.astype(jnp.bfloat16)


def level_of(key, extent, cuts, low, high):
    def one(dim, shards_of):
        heights = jax.random.uniform(jax.random.fold_in(jax.random.fold_in(key, 6), dim), (shards_of,), jnp.float32, low / len(cuts), high / len(cuts))
        return jnp.repeat(jnp.exp(heights), extent[dim] // shards_of).reshape((-1,) + (1,) * (len(extent) - dim - 1))

    gain = one(*cuts[0])
    for cut in cuts[1:]:
        gain = gain * one(*cut)
    return gain


def noise(own_key, dims, deviation, most, cuts=(), kind=jnp.bfloat16):
    result = deviation * jax.random.normal(own_key, dims, jnp.float32)
    if cuts:
        result = result * level_of(own_key, dims, cuts, -0.22, 0.18)
    return jnp.clip(result, -most, most).astype(kind)


def setup_inputs(seed: int = 0, part: int = 0) -> dict:
    key_of = jax.random.split(jax.random.key(seed), 8)
    part_keys = jax.random.split(jax.random.fold_in(key_of[7], part), 8)
    residual = draw_residual(jax.random.fold_in(jax.random.fold_in(key_of[7], part), 71), part)
    queries = draw_queries(jax.random.fold_in(jax.random.fold_in(key_of[7], part), 71), part)
    key_rows = draw_key_rows(jax.random.fold_in(jax.random.fold_in(key_of[7], part), 71), part)
    value_rows = noise(part_keys[3], (TOKENS, KVH * HD), 1.0, 6.0)
    out_weight = noise(key_of[4], (HEADS * HD, D), (HEADS * HD) ** -0.5, 0.125, ((0, 16),))
    norm_gain = jnp.clip(1.0 + 0.18 * jax.random.normal(key_of[5], (D,), jnp.float32), 0.1, 1.9)
    q_weight = noise(key_of[6], (D, HEADS * HD), D ** -0.5, 0.046875, ((1, 16),))
    return {"residual": residual, "queries": queries, "key_rows": key_rows, "value_rows": value_rows, "out_weight": out_weight, "norm_gain": norm_gain, "q_weight": q_weight}


epsilon = 1e-06

def encode(values_in):
    tok_rows = values_in.shape[0]
    grouped = values_in.reshape(tok_rows, D // QB, QB)
    peaks = lax.optimization_barrier(jnp.max(jnp.abs(grouped), axis=2)) + epsilon
    code_vals = (grouped / peaks[:, :, None]).astype(jnp.bfloat16).reshape(tok_rows, D)
    return (code_vals, peaks)

def decode(code_vals, peaks):
    tok_rows = code_vals.shape[0]
    grouped = code_vals.astype(jnp.float32).reshape(tok_rows, D // QB, QB)
    return (grouped * peaks[:, :, None]).reshape(tok_rows, D)

def reference(residual, queries, key_rows, value_rows, out_weight, norm_gain, q_weight):
    group = HEADS // KVH
    q_all = queries.astype(jnp.float32).reshape(TOKENS, HEADS, HD)
    k_all = jnp.repeat(key_rows.astype(jnp.float32).reshape(TOKENS, KVH, HD), group, axis=1)
    v_all = jnp.repeat(value_rows.astype(jnp.float32).reshape(TOKENS, KVH, HD), group, axis=1)
    scores = jnp.einsum('thd,shd->hts', q_all, k_all) / jnp.sqrt(jnp.float32(HD))
    positions = jnp.arange(TOKENS)
    visible = positions[None, :] <= positions[:, None]
    scores = jnp.where(visible[None], scores, jnp.float32(-1e+30))
    probs = jax.nn.softmax(scores, axis=-1).astype(jnp.bfloat16)
    context = jnp.einsum('hts,shd->thd', probs.astype(jnp.float32), v_all).astype(jnp.bfloat16)
    width_dev = HEAD_DEV * HD
    blocks_ctx = context.reshape(TOKENS, HEADS // HEAD_DEV, width_dev).transpose(1, 0, 2)
    blocks_w = out_weight.reshape(HEADS // HEAD_DEV, width_dev, D)

    def step(carry, pieces):
        partial_value = jnp.dot(pieces[0], pieces[1], preferred_element_type=jnp.float32)
        code_vals, peaks = encode(partial_value)
        return (carry + decode(code_vals, peaks), None)
    summed, unused = lax.scan(step, jnp.zeros((TOKENS, D), jnp.float32), (blocks_ctx, blocks_w))
    stream = residual.astype(jnp.float32) + summed
    stream_codes, stream_scales = encode(stream)
    decoded = decode(stream_codes, stream_scales)
    mean_sq = lax.optimization_barrier(jnp.mean(decoded * decoded, axis=1, keepdims=True))
    normed = (decoded * lax.rsqrt(mean_sq + 1e-05) * norm_gain[None, :]).astype(jnp.bfloat16)
    next_queries = jnp.dot(normed, q_weight, preferred_element_type=jnp.float32).astype(jnp.bfloat16)
    return (stream_codes, stream_scales, next_queries)
```

```python
import jax
import jax.numpy as jnp
from jax import lax
from jax.sharding import PartitionSpec as P

HD = 128
QB = 128
EPS = 1e-06


def on_device(residual, queries, key_rows, value_rows, out_weight, norm_gain, q_weight):
    n = lax.axis_size("tp")
    device = lax.axis_index("tp")
    core = device % 2
    chips = n // 2
    tokens = queries.shape[0]
    local = residual.shape[0]
    half = tokens // 2
    D = residual.shape[1]
    heads = queries.shape[1] // HD
    group = heads * n // (key_rows.shape[1] // HD)
    swap = [(i, i ^ 1) for i in range(n)]
    same_core = [[2 * i + c for i in range(chips)] for c in range(2)]

    row = jnp.arange(tokens)
    side = jnp.where(row < half, 1 - core, core)
    in_half = row % half
    token = in_half // local * (2 * local) + side * local + in_half % local
    pick = (token[:, None] == row[None, :]).astype(jnp.bfloat16)
    queries = jnp.dot(pick, queries, preferred_element_type=jnp.float32).astype(jnp.bfloat16)
    visible = row[None, :] <= token[:, None]
    contexts = []
    for h in range(heads):
        kv_start = (device * heads + h) // group * HD
        key_head = lax.dynamic_slice_in_dim(key_rows, kv_start, HD, 1)
        value_head = lax.dynamic_slice_in_dim(value_rows, kv_start, HD, 1)
        scores = lax.dot_general(
            queries[:, h * HD : (h + 1) * HD],
            key_head,
            (((1,), (1,)), ((), ())),
            preferred_element_type=jnp.float32,
        ) / jnp.sqrt(jnp.float32(HD))
        scores = jnp.where(visible, scores, jnp.float32(-1e30))
        probs = jax.nn.softmax(scores, axis=-1).astype(jnp.bfloat16)
        contexts.append(
            jnp.dot(probs, value_head, preferred_element_type=jnp.float32).astype(jnp.bfloat16)
        )
    context = jnp.concatenate(contexts, axis=1)
    sent = jnp.dot(context[:half], out_weight, preferred_element_type=jnp.float32)
    got = lax.ppermute(sent.astype(jnp.bfloat16), "tp", swap)
    kept = jnp.dot(context[half:], out_weight, preferred_element_type=jnp.float32)
    chip_sum = (kept + got.astype(jnp.float32)).astype(jnp.bfloat16)
    parts = lax.all_to_all(
        chip_sum.reshape(chips, local, D),
        "tp",
        split_axis=0,
        concat_axis=0,
        axis_index_groups=same_core,
        tiled=True,
    )
    summed = jnp.sum(parts.astype(jnp.float32), axis=0)
    stream = residual.astype(jnp.float32) + summed
    grouped = stream.reshape(local, D // QB, QB)
    scales = jnp.max(jnp.abs(grouped), axis=2) + EPS
    codes = (grouped / scales[:, :, None]).astype(jnp.bfloat16)
    decoded = (codes.astype(jnp.float32) * scales[:, :, None]).reshape(local, D)
    mean_sq = jnp.mean(decoded * decoded, axis=1, keepdims=True)
    normed = (decoded * lax.rsqrt(mean_sq + 1e-05) * norm_gain[None, :]).astype(jnp.bfloat16)
    mine = lax.all_to_all(
        jnp.broadcast_to(normed[None], (chips, local, D)),
        "tp",
        split_axis=0,
        concat_axis=0,
        axis_index_groups=same_core,
        tiled=True,
    ).reshape(half, D)
    other = lax.ppermute(mine, "tp", swap)
    out_mine = jnp.dot(mine, q_weight, preferred_element_type=jnp.float32).astype(jnp.bfloat16)
    out_other = jnp.dot(other, q_weight, preferred_element_type=jnp.float32).astype(jnp.bfloat16)
    out_mine = out_mine.reshape(chips, 1, local, -1)
    out_other = out_other.reshape(chips, 1, local, -1)
    first = jnp.where(core == 0, out_mine, out_other)
    second = jnp.where(core == 0, out_other, out_mine)
    next_queries = jnp.concatenate([first, second], axis=1).reshape(tokens, -1)
    return (codes.reshape(local, D), scales, next_queries)


def solution(mesh):
    in_specs = (
        P(("replica", "tp"), None),
        P("replica", "tp"),
        P("replica", None),
        P("replica", None),
        P("tp", None),
        P(),
        P(None, "tp"),
    )
    out_specs = (P(("replica", "tp"), None), P(("replica", "tp"), None), P("replica", "tp"))
    return jax.shard_map(
        on_device, mesh=mesh, in_specs=in_specs, out_specs=out_specs, check_vma=False
    )
```

```python
import jax
import jax.numpy as jnp
from jax import lax
from jax.sharding import PartitionSpec as P

HD = 128
QB = 128
EPS = 1e-06
F32 = jnp.float32
BF16 = jnp.bfloat16


def on_device(residual, queries, key_rows, value_rows, out_weight, norm_gain, q_weight):
    n = lax.axis_size("tp")
    device = lax.axis_index("tp")
    tokens = queries.shape[0]
    local = residual.shape[0]
    D = residual.shape[1]
    far = n // 4
    heads = queries.shape[1] // HD
    group = heads * n // (key_rows.shape[1] // HD)

    def swap(x, distance):
        return lax.ppermute(x, "tp", [(i, i ^ distance) for i in range(n)])

    row = jnp.arange(tokens)
    block = row // local
    distance = block % far * 4 + block // far % 2 * 2 + block // (2 * far)
    token = (device ^ distance) * local + row % local
    pick = (token[:, None] == row[None, :]).astype(BF16)
    queries = jnp.dot(pick, queries, preferred_element_type=F32).astype(BF16)
    visible = row[None, :] <= token[:, None]
    contexts = []
    for h in range(heads):
        kv_start = (device * heads + h) // group * HD
        key_head = lax.dynamic_slice_in_dim(key_rows, kv_start, HD, 1)
        value_head = lax.dynamic_slice_in_dim(value_rows, kv_start, HD, 1)
        scores = lax.dot_general(
            queries[:, h * HD : (h + 1) * HD],
            key_head,
            (((1,), (1,)), ((), ())),
            preferred_element_type=F32,
        ) / jnp.sqrt(F32(HD))
        scores = jnp.where(visible, scores, F32(-1e30))
        probs = jax.nn.softmax(scores, axis=-1).astype(BF16)
        contexts.append(jnp.dot(probs, value_head, preferred_element_type=F32).astype(BF16))
    context = jnp.concatenate(contexts, axis=1)
    half, quarter = tokens // 2, tokens // 4
    sent = jnp.dot(context[half:], out_weight, preferred_element_type=F32)
    got = swap(sent.astype(BF16), 1)
    kept = jnp.dot(context[:half], out_weight, preferred_element_type=F32)
    chip_sum = kept + got.astype(F32)
    got = swap(chip_sum[quarter:].astype(BF16), 2)
    pair_sum = chip_sum[:quarter] + got.astype(F32)
    stream = residual.astype(F32) + pair_sum[:local]
    arrived = [
        swap(pair_sum[f * local : (f + 1) * local].astype(BF16), 4 * f) for f in range(1, far)
    ]
    for piece in arrived:
        stream = stream + piece.astype(F32)
    grouped = stream.reshape(local, D // QB, QB)
    scales = jnp.max(jnp.abs(grouped), axis=2) + EPS
    codes = (grouped / scales[:, :, None]).astype(BF16)
    decoded = (codes.astype(F32) * scales[:, :, None]).reshape(local, D)
    mean_sq = jnp.mean(decoded * decoded, axis=1, keepdims=True)
    normed = (decoded * lax.rsqrt(mean_sq + 1e-05) * norm_gain[None, :]).astype(BF16)
    near = jnp.concatenate([normed] + [swap(normed, 4 * f) for f in range(1, far)], axis=0)
    mine = jnp.concatenate([near, swap(near, 2)], axis=0)
    other = swap(mine, 1)
    out_mine = jnp.dot(mine, q_weight, preferred_element_type=F32).astype(BF16)
    out_other = jnp.dot(other, q_weight, preferred_element_type=F32).astype(BF16)
    found = jnp.concatenate([out_mine, out_other], axis=0)
    next_queries = lax.dot_general(
        pick, found, (((0,), (0,)), ((), ())), preferred_element_type=F32
    ).astype(BF16)
    return (codes.reshape(local, D), scales, next_queries)


def solution(mesh):
    in_specs = (
        P(("replica", "tp"), None),
        P("replica", "tp"),
        P("replica", None),
        P("replica", None),
        P("tp", None),
        P(),
        P(None, "tp"),
    )
    out_specs = (P(("replica", "tp"), None), P(("replica", "tp"), None), P("replica", "tp"))
    return jax.shard_map(
        on_device, mesh=mesh, in_specs=in_specs, out_specs=out_specs, check_vma=False
    )
```

```python
import jax
import jax.numpy as jnp
from jax import lax
from jax.sharding import PartitionSpec as P

HD = 128
QB = 128
EPS = 1e-06
F32 = jnp.float32
BF16 = jnp.bfloat16


def on_device(residual, queries, key_rows, value_rows, out_weight, norm_gain, q_weight):
    n = lax.axis_size("tp")
    device = lax.axis_index("tp")
    tokens = queries.shape[0]
    local = residual.shape[0]
    D = residual.shape[1]
    heads = queries.shape[1] // HD
    group = heads * n // (key_rows.shape[1] // HD)
    late = [1 << b for b in range(3, n.bit_length() - 1)]
    orders = ([2, 4], [4, 2])
    cut = D // 2
    columns = ((0, cut), (cut, D))

    def swap(x, distance):
        return lax.ppermute(x, "tp", [(i, i ^ distance) for i in range(n)])

    row = jnp.arange(tokens)
    block = row // local

    def picker(order):
        bits = [1] + order + late
        distance = 0
        for place, bit in enumerate(bits):
            distance = distance + (block >> (len(bits) - 1 - place)) % 2 * bit
        token = (device ^ distance) * local + row % local
        return (token[:, None] == row[None, :]).astype(BF16)

    visible = row[None, :] <= row[:, None]
    contexts = []
    for h in range(heads):
        kv_start = (device * heads + h) // group * HD
        key_head = lax.dynamic_slice_in_dim(key_rows, kv_start, HD, 1)
        value_head = lax.dynamic_slice_in_dim(value_rows, kv_start, HD, 1)
        scores = lax.dot_general(
            queries[:, h * HD : (h + 1) * HD],
            key_head,
            (((1,), (1,)), ((), ())),
            preferred_element_type=F32,
        ) / jnp.sqrt(F32(HD))
        scores = jnp.where(visible, scores, F32(-1e30))
        probs = jax.nn.softmax(scores, axis=-1).astype(BF16)
        contexts.append(jnp.dot(probs, value_head, preferred_element_type=F32).astype(BF16))
    context = jnp.concatenate(contexts, axis=1)
    half, quarter, eighth = tokens // 2, tokens // 4, tokens // 8
    sums = []
    for order, (lo, hi) in zip(orders, columns):
        ordered = jnp.dot(picker(order), context, preferred_element_type=F32).astype(BF16)
        part = jnp.dot(ordered, out_weight[:, lo:hi], preferred_element_type=F32)
        got = swap(part[half:].astype(BF16), 1)
        chip_sum = part[:half] + got.astype(F32)
        got = swap(chip_sum[quarter:].astype(BF16), order[0])
        pair_sum = chip_sum[:quarter] + got.astype(F32)
        got = swap(pair_sum[eighth:].astype(BF16), order[1])
        sums.append(pair_sum[:eighth] + got.astype(F32))
    total = jnp.concatenate(sums, axis=1)
    for distance in late:
        kept = total.shape[0] // 2
        total = total[:kept] + swap(total[kept:].astype(BF16), distance).astype(F32)
    stream = residual.astype(F32) + total
    grouped = stream.reshape(local, D // QB, QB)
    scales = jnp.max(jnp.abs(grouped), axis=2) + EPS
    codes = (grouped / scales[:, :, None]).astype(BF16)
    decoded = (codes.astype(F32) * scales[:, :, None]).reshape(local, D)
    mean_sq = jnp.mean(decoded * decoded, axis=1, keepdims=True)
    normed = (decoded * lax.rsqrt(mean_sq + 1e-05) * norm_gain[None, :]).astype(BF16)
    for distance in late[::-1]:
        normed = jnp.concatenate([normed, swap(normed, distance)], axis=0)
    next_queries = 0
    for order, (lo, hi) in zip(orders, columns):
        held = normed[:, lo:hi]
        for distance in order[::-1]:
            held = jnp.concatenate([held, swap(held, distance)], axis=0)
        held = jnp.concatenate([held, swap(held, 1)], axis=0)
        found = jnp.dot(held, q_weight[lo:hi], preferred_element_type=F32)
        next_queries = next_queries + lax.dot_general(
            picker(order).astype(F32),
            found,
            (((0,), (0,)), ((), ())),
            precision=lax.Precision.HIGHEST,
        )
    return (codes.reshape(local, D), scales, next_queries.astype(BF16))


def solution(mesh):
    in_specs = (
        P(("replica", "tp"), None),
        P("replica", "tp"),
        P("replica", None),
        P("replica", None),
        P("tp", None),
        P(),
        P(None, "tp"),
    )
    out_specs = (P(("replica", "tp"), None), P(("replica", "tp"), None), P("replica", "tp"))
    return jax.shard_map(
        on_device, mesh=mesh, in_specs=in_specs, out_specs=out_specs, check_vma=False
    )
```

```python
import jax
import jax.numpy as jnp
from jax import lax
from jax.sharding import PartitionSpec as P

HD = 128
QB = 128
EPS = 1e-06
F32 = jnp.float32
BF16 = jnp.bfloat16


def on_device(residual, queries, key_rows, value_rows, out_weight, norm_gain, q_weight):
    n = lax.axis_size("tp")
    device = lax.axis_index("tp")
    core = device % 2
    tokens = queries.shape[0]
    local = residual.shape[0]
    D = residual.shape[1]
    heads = queries.shape[1] // HD
    group = heads * n // (key_rows.shape[1] // HD)
    levels = [(2, 4), (4, 2)] + [(1 << b, 1 << b) for b in range(3, n.bit_length() - 1)]
    bits = [(1, 1)] + levels

    def swap(x, level):
        return lax.ppermute(x, "tp", [(i, i ^ level[i % 2]) for i in range(n)])

    row = jnp.arange(tokens)
    block = row // local
    side = (core + block // (n // 2)) % 2
    distance = 0
    for place, (even, odd) in enumerate(bits):
        distance += (block >> (len(bits) - 1 - place)) % 2 * jnp.where(side == 0, even, odd)
    token = (device ^ distance) * local + row % local
    pick = (token[:, None] == row[None, :]).astype(BF16)
    queries = jnp.dot(pick, queries, preferred_element_type=F32).astype(BF16)
    visible = row[None, :] <= token[:, None]
    contexts = []
    for h in range(heads):
        kv_start = (device * heads + h) // group * HD
        key_head = lax.dynamic_slice_in_dim(key_rows, kv_start, HD, 1)
        value_head = lax.dynamic_slice_in_dim(value_rows, kv_start, HD, 1)
        scores = lax.dot_general(
            queries[:, h * HD : (h + 1) * HD],
            key_head,
            (((1,), (1,)), ((), ())),
            preferred_element_type=F32,
        ) / jnp.sqrt(F32(HD))
        scores = jnp.where(visible, scores, F32(-1e30))
        probs = jax.nn.softmax(scores, axis=-1).astype(BF16)
        contexts.append(jnp.dot(probs, value_head, preferred_element_type=F32).astype(BF16))
    context = jnp.concatenate(contexts, axis=1)
    half = tokens // 2
    sent = jnp.dot(context[half:], out_weight, preferred_element_type=F32)
    got = swap(sent.astype(BF16), bits[0])
    total = jnp.dot(context[:half], out_weight, preferred_element_type=F32)
    total = total + got.astype(F32)
    for level in levels[:-1]:
        kept = total.shape[0] // 2
        total = total[:kept] + swap(total[kept:].astype(BF16), level).astype(F32)
    total = jnp.concatenate([total[:local] + residual.astype(F32), total[local:]], axis=0)
    got = swap(total.astype(BF16), levels[-1]).astype(F32)
    stream = total + jnp.concatenate([got[local:], got[:local]], axis=0)
    rows = stream.shape[0]
    grouped = stream.reshape(rows, D // QB, QB)
    scales = jnp.max(jnp.abs(grouped), axis=2) + EPS
    codes = (grouped / scales[:, :, None]).astype(BF16)
    decoded = (codes.astype(F32) * scales[:, :, None]).reshape(rows, D)
    mean_sq = jnp.mean(decoded * decoded, axis=1, keepdims=True)
    held = (decoded * lax.rsqrt(mean_sq + 1e-05) * norm_gain[None, :]).astype(BF16)
    for level in levels[-2::-1]:
        held = jnp.concatenate([held, swap(held, level)], axis=0)
    other = swap(held, bits[0])
    out_mine = jnp.dot(held, q_weight, preferred_element_type=F32).astype(BF16)
    out_other = jnp.dot(other, q_weight, preferred_element_type=F32).astype(BF16)
    found = jnp.concatenate([out_mine, out_other], axis=0)
    next_queries = lax.dot_general(
        pick, found, (((0,), (0,)), ((), ())), preferred_element_type=F32
    ).astype(BF16)
    return (codes.reshape(rows, D)[:local], scales[:local], next_queries)


def solution(mesh):
    in_specs = (
        P(("replica", "tp"), None),
        P("replica", "tp"),
        P("replica", None),
        P("replica", None),
        P("tp", None),
        P(),
        P(None, "tp"),
    )
    out_specs = (P(("replica", "tp"), None), P(("replica", "tp"), None), P("replica", "tp"))
    return jax.shard_map(
        on_device, mesh=mesh, in_specs=in_specs, out_specs=out_specs, check_vma=False
    )
```

```python
import jax
import jax.numpy as jnp
from jax import lax
from jax.sharding import PartitionSpec as P

HD = 128
QB = 128
EPS = 1e-06
F32 = jnp.float32
BF16 = jnp.bfloat16


def on_device(residual, queries, key_rows, value_rows, out_weight, norm_gain, q_weight):
    n = lax.axis_size("tp")
    device = lax.axis_index("tp")
    tokens = queries.shape[0]
    local = residual.shape[0]
    D = residual.shape[1]
    heads = queries.shape[1] // HD
    group = heads * n // (key_rows.shape[1] // HD)
    square = (4, 2, 6)
    levels = [1 << b for b in range(3, n.bit_length() - 1)]
    bits = [1, 2, 4] + levels

    def swap(x, distance):
        return lax.ppermute(x, "tp", [(i, i ^ distance) for i in range(n)])

    row = jnp.arange(tokens)
    block = row // local
    distance = 0
    for place, bit in enumerate(bits):
        distance += (block >> (len(bits) - 1 - place)) % 2 * bit
    token = (device ^ distance) * local + row % local
    pick = (token[:, None] == row[None, :]).astype(BF16)
    queries = jnp.dot(pick, queries, preferred_element_type=F32).astype(BF16)
    visible = row[None, :] <= token[:, None]
    contexts = []
    for h in range(heads):
        kv_start = (device * heads + h) // group * HD
        key_head = lax.dynamic_slice_in_dim(key_rows, kv_start, HD, 1)
        value_head = lax.dynamic_slice_in_dim(value_rows, kv_start, HD, 1)
        scores = lax.dot_general(
            queries[:, h * HD : (h + 1) * HD],
            key_head,
            (((1,), (1,)), ((), ())),
            preferred_element_type=F32,
        ) / jnp.sqrt(F32(HD))
        scores = jnp.where(visible, scores, F32(-1e30))
        probs = jax.nn.softmax(scores, axis=-1).astype(BF16)
        contexts.append(jnp.dot(probs, value_head, preferred_element_type=F32).astype(BF16))
    context = jnp.concatenate(contexts, axis=1)
    half = tokens // 2
    sent = jnp.dot(context[half:], out_weight, preferred_element_type=F32)
    got = swap(sent.astype(BF16), 1)
    total = jnp.dot(context[:half], out_weight, preferred_element_type=F32)
    total = total + got.astype(F32)
    part = half // 4
    arrived = [
        swap(total[k * part : (k + 1) * part].astype(BF16), d) for k, d in enumerate(square, 1)
    ]
    total = total[:part]
    for piece in arrived:
        total = total + piece.astype(F32)
    for level in levels[:-1]:
        kept = total.shape[0] // 2
        total = total[:kept] + swap(total[kept:].astype(BF16), level).astype(F32)
    total = jnp.concatenate([total[:local] + residual.astype(F32), total[local:]], axis=0)
    got = swap(total.astype(BF16), levels[-1]).astype(F32)
    stream = total + jnp.concatenate([got[local:], got[:local]], axis=0)
    rows = stream.shape[0]
    grouped = stream.reshape(rows, D // QB, QB)
    scales = jnp.max(jnp.abs(grouped), axis=2) + EPS
    codes = (grouped / scales[:, :, None]).astype(BF16)
    decoded = (codes.astype(F32) * scales[:, :, None]).reshape(rows, D)
    mean_sq = jnp.mean(decoded * decoded, axis=1, keepdims=True)
    held = (decoded * lax.rsqrt(mean_sq + 1e-05) * norm_gain[None, :]).astype(BF16)
    for level in levels[-2::-1]:
        held = jnp.concatenate([held, swap(held, level)], axis=0)
    held = jnp.concatenate([held] + [swap(held, d) for d in square], axis=0)
    other = swap(held, 1)
    out_mine = jnp.dot(held, q_weight, preferred_element_type=F32).astype(BF16)
    out_other = jnp.dot(other, q_weight, preferred_element_type=F32).astype(BF16)
    found = jnp.concatenate([out_mine, out_other], axis=0)
    next_queries = lax.dot_general(
        pick, found, (((0,), (0,)), ((), ())), preferred_element_type=F32
    ).astype(BF16)
    return (codes.reshape(rows, D)[:local], scales[:local], next_queries)


def solution(mesh):
    in_specs = (
        P(("replica", "tp"), None),
        P("replica", "tp"),
        P("replica", None),
        P("replica", None),
        P("tp", None),
        P(),
        P(None, "tp"),
    )
    out_specs = (P(("replica", "tp"), None), P(("replica", "tp"), None), P("replica", "tp"))
    return jax.shard_map(
        on_device, mesh=mesh, in_specs=in_specs, out_specs=out_specs, check_vma=False
    )
```

```python
import functools

import jax
import jax.numpy as jnp
from jax import lax
from jax.experimental import pallas as pl
from jax.experimental.pallas import tpu as pltpu
from jax.sharding import PartitionSpec as P

HD = 128
QB = 128
EPS = 1e-06
F32 = jnp.float32
BF16 = jnp.bfloat16
CHUNKS = 8


def late_levels(n):
    return [1 << b for b in range(3, n.bit_length() - 1)]


def owner_token(row, device, n, local):
    bits = [(1, 1), (2, 4), (4, 2)] + [(d, d) for d in late_levels(n)]
    block = row // local
    side = (device + block // (n // 2)) % 2
    distance = jnp.zeros_like(row)
    for place, (even, odd) in enumerate(bits):
        bit = (block >> (len(bits) - 1 - place)) % 2
        distance = distance + bit * jnp.where(side == 0, even, odd)
    return (device ^ distance) * local + row % local


def project_kernel(n, local, queries, keys, values, weight, sent, kept, held, sems):
    device = lax.axis_index("tp")
    tokens = queries.shape[0]
    heads = queries.shape[1] // HD
    group = heads * n // (keys.shape[1] // HD)
    width = held.shape[1] // CHUNKS
    copies = []
    for c in range(CHUNKS):
        part = pl.ds(c * width, width)
        copies.append(pltpu.make_async_copy(weight.at[:, part], held.at[:, part], sems.at[c]))
        copies[-1].start()
    row = lax.broadcasted_iota(jnp.int32, (tokens, tokens), 0)
    col = lax.broadcasted_iota(jnp.int32, (tokens, tokens), 1)
    token = owner_token(row, device, n, local)
    pick = (token == col).astype(F32).astype(BF16)
    ordered = jnp.dot(pick, queries[...], preferred_element_type=F32).astype(BF16)
    contexts = []
    for h in range(heads):
        at = pl.ds(pl.multiple_of(lax.div(device * heads + h, group) * HD, HD), HD)
        scores = lax.dot_general(
            ordered[:, h * HD : (h + 1) * HD],
            keys[:, at],
            (((1,), (1,)), ((), ())),
            preferred_element_type=F32,
        ) / jnp.sqrt(F32(HD))
        scores = jnp.where(col <= token, scores, F32(-1e30))
        weights = jnp.exp(scores - jnp.max(scores, axis=1, keepdims=True))
        probs = (weights / jnp.sum(weights, axis=1, keepdims=True)).astype(BF16)
        contexts.append(
            jnp.dot(probs, values[:, at], preferred_element_type=F32).astype(BF16)
        )
    context = contexts[0] if heads == 1 else jnp.concatenate(contexts, axis=1)
    half = tokens // 2
    for c in range(CHUNKS):
        part = pl.ds(c * width, width)
        copies[c].wait()
        partial = jnp.dot(context, held[:, part], preferred_element_type=F32)
        kept[:, part] = partial[:half]
        sent[:, part] = partial[half:].astype(BF16)


def project(n, local, queries, keys, values, weight):
    tokens, D = queries.shape[0], weight.shape[1]
    half = tokens // 2
    whole = pl.BlockSpec(memory_space=pltpu.VMEM)
    return pl.pallas_call(
        functools.partial(project_kernel, n, local),
        out_shape=[
            jax.ShapeDtypeStruct((half, D), BF16),
            jax.ShapeDtypeStruct((half, D), F32),
        ],
        in_specs=[whole, whole, whole, pl.BlockSpec(memory_space=pltpu.HBM)],
        out_specs=[whole, whole],
        scratch_shapes=[
            pltpu.VMEM(weight.shape, BF16),
            pltpu.SemaphoreType.DMA((CHUNKS,)),
        ],
        compiler_params=pltpu.CompilerParams(vmem_limit_bytes=24 << 20),
        cost_estimate=pl.CostEstimate(
            flops=2 * tokens * weight.size, bytes_accessed=2 * weight.size, transcendentals=0
        ),
        name="project",
    )(queries, keys, values, weight)


def on_device(residual, queries, key_rows, value_rows, out_weight, norm_gain, q_weight):
    n = lax.axis_size("tp")
    device = lax.axis_index("tp")
    tokens = queries.shape[0]
    local = residual.shape[0]
    D = residual.shape[1]
    levels = late_levels(n)
    square = [(1, (4, 2)), (2, (2, 4)), (3, (6, 6))]

    def swap(x, even, odd):
        return lax.ppermute(x, "tp", [(i, i ^ (odd if i % 2 else even)) for i in range(n)])

    half = tokens // 2
    sent, total = project(n, local, queries, key_rows, value_rows, out_weight)
    total = total + swap(sent, 1, 1).astype(F32)
    part = half // 4
    arrived = [
        swap(total[k * part : (k + 1) * part].astype(BF16), *distance)
        for k, distance in square[::-1]
    ]
    total = total[:part]
    for piece in arrived:
        total = total + piece.astype(F32)
    for level in levels[:-1]:
        kept = total.shape[0] // 2
        total = total[:kept] + swap(total[kept:].astype(BF16), level, level).astype(F32)
    total = jnp.concatenate([total[:local] + residual.astype(F32), total[local:]], axis=0)
    got = swap(total.astype(BF16), levels[-1], levels[-1]).astype(F32)
    stream = total + jnp.concatenate([got[local:], got[:local]], axis=0)
    rows = stream.shape[0]
    grouped = stream.reshape(rows, D // QB, QB)
    scales = jnp.max(jnp.abs(grouped), axis=2) + EPS
    codes = (grouped / scales[:, :, None]).astype(BF16)
    decoded = (codes.astype(F32) * scales[:, :, None]).reshape(rows, D)
    mean_sq = jnp.mean(decoded * decoded, axis=1, keepdims=True)
    held = (decoded * lax.rsqrt(mean_sq + 1e-05) * norm_gain[None, :]).astype(BF16)
    for level in levels[-2::-1]:
        held = jnp.concatenate([held, swap(held, level, level)], axis=0)
    arrived = [swap(held, *distance) for _, distance in square[::-1]]
    held = jnp.concatenate([held] + arrived[::-1], axis=0)
    other = swap(held, 1, 1)
    out_mine = jnp.dot(held, q_weight, preferred_element_type=F32).astype(BF16)
    out_other = jnp.dot(other, q_weight, preferred_element_type=F32).astype(BF16)
    found = jnp.concatenate([out_mine, out_other], axis=0)
    row = jnp.arange(tokens)
    pick = (owner_token(row, device, n, local)[:, None] == row[None, :]).astype(BF16)
    next_queries = lax.dot_general(
        pick, found, (((0,), (0,)), ((), ())), preferred_element_type=F32
    ).astype(BF16)
    return (codes.reshape(rows, D)[:local], scales[:local], next_queries)


def solution(mesh):
    in_specs = (
        P(("replica", "tp"), None),
        P("replica", "tp"),
        P("replica", None),
        P("replica", None),
        P("tp", None),
        P(),
        P(None, "tp"),
    )
    out_specs = (P(("replica", "tp"), None), P(("replica", "tp"), None), P("replica", "tp"))
    return jax.shard_map(
        on_device, mesh=mesh, in_specs=in_specs, out_specs=out_specs, check_vma=False
    )
```

```python
import functools

import jax
import jax.numpy as jnp
from jax import lax
from jax.experimental import pallas as pl
from jax.experimental.pallas import tpu as pltpu
from jax.sharding import PartitionSpec as P

HD = 128
QB = 128
EPS = 1e-06
F32 = jnp.float32
BF16 = jnp.bfloat16
CHUNKS = 8
VMEM = 32 << 20


def late_levels(n):
    return [1 << b for b in range(3, n.bit_length() - 1)]


def owner_token(row, device, n, local):
    bits = [(1, 1), (2, 4), (6, 6)] + [(d, d) for d in late_levels(n)]
    block = row // local
    side = (device + block // (n // 2)) % 2
    distance = jnp.zeros_like(row)
    for place, (even, odd) in enumerate(bits):
        bit = (block >> (len(bits) - 1 - place)) % 2
        distance = distance ^ (bit * jnp.where(side == 0, even, odd))
    return (device ^ distance) * local + row % local


def project_kernel(
    n, local, queries, keys, values, weight, sent, kept, query, key, value, held, small, sems
):
    device = lax.axis_index("tp")
    tokens = queries.shape[0]
    heads = queries.shape[1] // HD
    group = heads * n // (keys.shape[1] // HD)
    width = held.shape[1] // CHUNKS
    fetches = [pltpu.make_async_copy(queries, query, small.at[0])]
    for h in range(heads):
        at = pl.ds(pl.multiple_of(lax.div(device * heads + h, group) * HD, HD), HD)
        fetches.append(pltpu.make_async_copy(keys.at[:, at], key.at[h], small.at[1 + 2 * h]))
        fetches.append(pltpu.make_async_copy(values.at[:, at], value.at[h], small.at[2 + 2 * h]))
    for fetch in fetches:
        fetch.start()
    copies = []
    for c in range(CHUNKS):
        part = pl.ds(c * width, width)
        copies.append(pltpu.make_async_copy(weight.at[:, part], held.at[:, part], sems.at[c]))
        copies[-1].start()
    row = lax.broadcasted_iota(jnp.int32, (tokens, tokens), 0)
    col = lax.broadcasted_iota(jnp.int32, (tokens, tokens), 1)
    token = owner_token(row, device, n, local)
    pick = (token == col).astype(F32).astype(BF16)
    for fetch in fetches:
        fetch.wait()
    ordered = jnp.dot(pick, query[...], preferred_element_type=F32).astype(BF16)
    contexts = []
    for h in range(heads):
        scores = lax.dot_general(
            ordered[:, h * HD : (h + 1) * HD],
            key[h],
            (((1,), (1,)), ((), ())),
            preferred_element_type=F32,
        ) / jnp.sqrt(F32(HD))
        scores = jnp.where(col <= token, scores, F32(-1e30))
        weights = jnp.exp(scores - jnp.max(scores, axis=1, keepdims=True))
        probs = (weights / jnp.sum(weights, axis=1, keepdims=True)).astype(BF16)
        contexts.append(
            jnp.dot(probs, value[h], preferred_element_type=F32).astype(BF16)
        )
    context = contexts[0] if heads == 1 else jnp.concatenate(contexts, axis=1)
    half = tokens // 2
    for c in range(CHUNKS):
        part = pl.ds(c * width, width)
        copies[c].wait()
        partial = jnp.dot(context, held[:, part], preferred_element_type=F32)
        kept[:, part] = partial[:half]
        sent[:, part] = partial[half:].astype(BF16)


def project(n, local, queries, keys, values, weight):
    tokens, D = queries.shape[0], weight.shape[1]
    half = tokens // 2
    heads = queries.shape[1] // HD
    operands = [
        pltpu.with_memory_space_constraint(x, pltpu.HBM) for x in (queries, keys, values, weight)
    ]
    whole = pl.BlockSpec(memory_space=pltpu.VMEM)
    return pl.pallas_call(
        functools.partial(project_kernel, n, local),
        out_shape=[
            jax.ShapeDtypeStruct((half, D), BF16),
            jax.ShapeDtypeStruct((half, D), F32),
        ],
        in_specs=[pl.BlockSpec(memory_space=pltpu.HBM)] * 4,
        out_specs=[whole, whole],
        scratch_shapes=[
            pltpu.VMEM(queries.shape, BF16),
            pltpu.VMEM((heads, tokens, HD), BF16),
            pltpu.VMEM((heads, tokens, HD), BF16),
            pltpu.VMEM(weight.shape, BF16),
            pltpu.SemaphoreType.DMA((1 + 2 * heads,)),
            pltpu.SemaphoreType.DMA((CHUNKS,)),
        ],
        compiler_params=pltpu.CompilerParams(vmem_limit_bytes=VMEM),
        cost_estimate=pl.CostEstimate(
            flops=2 * tokens * weight.size, bytes_accessed=2 * weight.size, transcendentals=0
        ),
        name="project",
    )(*operands)


def on_device(residual, queries, key_rows, value_rows, out_weight, norm_gain, q_weight):
    n = lax.axis_size("tp")
    device = lax.axis_index("tp")
    tokens = queries.shape[0]
    local = residual.shape[0]
    D = residual.shape[1]
    levels = late_levels(n)
    square = [(1, (6, 6)), (2, (2, 4)), (3, (4, 2))]

    def swap(x, even, odd):
        return lax.ppermute(x, "tp", [(i, i ^ (odd if i % 2 else even)) for i in range(n)])

    half = tokens // 2
    sent, total = project(n, local, queries, key_rows, value_rows, out_weight)
    total = total + swap(sent, 1, 1).astype(F32)
    part = half // 4
    arrived = [
        swap(total[k * part : (k + 1) * part].astype(BF16), *distance)
        for k, distance in square
    ]
    total = total[:part]
    for piece in arrived:
        total = total + piece.astype(F32)
    for level in levels[:-1]:
        kept = total.shape[0] // 2
        total = total[:kept] + swap(total[kept:].astype(BF16), level, level).astype(F32)
    total = jnp.concatenate([total[:local] + residual.astype(F32), total[local:]], axis=0)
    got = swap(total.astype(BF16), levels[-1], levels[-1]).astype(F32)
    stream = total + jnp.concatenate([got[local:], got[:local]], axis=0)
    rows = stream.shape[0]
    grouped = stream.reshape(rows, D // QB, QB)
    scales = jnp.max(jnp.abs(grouped), axis=2) + EPS
    codes = (grouped / scales[:, :, None]).astype(BF16)
    decoded = (codes.astype(F32) * scales[:, :, None]).reshape(rows, D)
    mean_sq = jnp.mean(decoded * decoded, axis=1, keepdims=True)
    held = (decoded * lax.rsqrt(mean_sq + 1e-05) * norm_gain[None, :]).astype(BF16)
    for level in levels[-2::-1]:
        held = jnp.concatenate([held, swap(held, level, level)], axis=0)
    held = jnp.concatenate([held] + [swap(held, *distance) for _, distance in square], axis=0)
    other = swap(held, 1, 1)
    out_mine = jnp.dot(held, q_weight, preferred_element_type=F32).astype(BF16)
    out_other = jnp.dot(other, q_weight, preferred_element_type=F32).astype(BF16)
    found = jnp.concatenate([out_mine, out_other], axis=0)
    row = jnp.arange(tokens)
    pick = (owner_token(row, device, n, local)[:, None] == row[None, :]).astype(BF16)
    next_queries = lax.dot_general(
        pick, found, (((0,), (0,)), ((), ())), preferred_element_type=F32
    ).astype(BF16)
    return (codes.reshape(rows, D)[:local], scales[:local], next_queries)


def solution(mesh):
    in_specs = (
        P(("replica", "tp"), None),
        P("replica", "tp"),
        P("replica", None),
        P("replica", None),
        P("tp", None),
        P(),
        P(None, "tp"),
    )
    out_specs = (P(("replica", "tp"), None), P(("replica", "tp"), None), P("replica", "tp"))
    return jax.shard_map(
        on_device, mesh=mesh, in_specs=in_specs, out_specs=out_specs, check_vma=False
    )
```

```python
import functools

import jax
import jax.numpy as jnp
from jax import lax
from jax.experimental import pallas as pl
from jax.experimental.pallas import tpu as pltpu
from jax.sharding import PartitionSpec as P

HD = 128
QB = 128
EPS = 1e-06
F32 = jnp.float32
BF16 = jnp.bfloat16
PIECES = 4
VMEM_LIMIT = 24 << 20


def late_levels(n):
    return [1 << b for b in range(3, n.bit_length() - 1)]


def owner_token(row, device, n, local):
    bits = [1, 2, 6] + late_levels(n)
    shift = local.bit_length() - 1
    block = row >> shift
    distance = jnp.zeros_like(row)
    for place, bit in enumerate(bits):
        distance = distance ^ (((block >> (len(bits) - 1 - place)) & 1) * bit)
    return ((device ^ distance) << shift) | (row & (local - 1))


def attend_kernel(
    n, local, queries, keys, values, weight, context, held, query, key, value, small, large
):
    device = lax.axis_index("tp")
    tokens = queries.shape[0]
    heads = queries.shape[1] // HD
    group = heads * n // (keys.shape[1] // HD)
    copies = [pltpu.make_async_copy(queries, query, small.at[0])]
    for h in range(heads):
        at = pl.ds(pl.multiple_of(lax.div(device * heads + h, group) * HD, HD), HD)
        copies.append(pltpu.make_async_copy(keys.at[:, at], key.at[h], small.at[1 + 2 * h]))
        copies.append(pltpu.make_async_copy(values.at[:, at], value.at[h], small.at[2 + 2 * h]))
    depth = held.shape[0] // PIECES
    late = []
    for c in range(PIECES):
        part = pl.ds(c * depth, depth)
        late.append(pltpu.make_async_copy(weight.at[part], held.at[part], large.at[c]))
    for copy in copies + late:
        copy.start()
    row = lax.broadcasted_iota(jnp.int32, (tokens, tokens), 0)
    col = lax.broadcasted_iota(jnp.int32, (tokens, tokens), 1)
    token = owner_token(row, device, n, local)
    pick = (token == col).astype(F32).astype(BF16)
    for copy in copies:
        copy.wait()
    ordered = jnp.dot(pick, query[...], preferred_element_type=F32).astype(BF16)
    for h in range(heads):
        scores = lax.dot_general(
            ordered[:, h * HD : (h + 1) * HD],
            key[h],
            (((1,), (1,)), ((), ())),
            preferred_element_type=F32,
        ) / jnp.sqrt(F32(HD))
        scores = jnp.where(col <= token, scores, F32(-1e30))
        weights = jnp.exp(scores - jnp.max(scores, axis=1, keepdims=True))
        probs = (weights / jnp.sum(weights, axis=1, keepdims=True)).astype(BF16)
        context[:, h * HD : (h + 1) * HD] = jnp.dot(
            probs, value[h], preferred_element_type=F32
        ).astype(BF16)
    for copy in late:
        copy.wait()


def in_hbm(*arrays):
    return [pltpu.with_memory_space_constraint(x, pltpu.HBM) for x in arrays]


def attend(n, local, queries, keys, values, weight):
    tokens = queries.shape[0]
    heads = queries.shape[1] // HD
    whole = pl.BlockSpec(memory_space=pltpu.VMEM)
    return pl.pallas_call(
        functools.partial(attend_kernel, n, local),
        out_shape=[
            jax.ShapeDtypeStruct(queries.shape, BF16),
            pltpu.VMEM(weight.shape, BF16),
        ],
        in_specs=[pl.BlockSpec(memory_space=pltpu.HBM)] * 4,
        out_specs=[whole, whole],
        scratch_shapes=[
            pltpu.VMEM(queries.shape, BF16),
            pltpu.VMEM((heads, tokens, HD), BF16),
            pltpu.VMEM((heads, tokens, HD), BF16),
            pltpu.SemaphoreType.DMA((1 + 2 * heads,)),
            pltpu.SemaphoreType.DMA((PIECES,)),
        ],
        compiler_params=pltpu.CompilerParams(vmem_limit_bytes=VMEM_LIMIT),
        cost_estimate=pl.CostEstimate(
            flops=0, bytes_accessed=2 * weight.size, transcendentals=0
        ),
        name="attend",
    )(*in_hbm(queries, keys, values, weight))


def fetch_kernel(source, target, sems):
    depth = source.shape[0] // PIECES
    copies = []
    for c in range(PIECES):
        part = pl.ds(c * depth, depth)
        copies.append(pltpu.make_async_copy(source.at[part], target.at[part], sems.at[c]))
        copies[-1].start()
    for copy in copies:
        copy.wait()


def fetch(weight):
    return pl.pallas_call(
        fetch_kernel,
        out_shape=pltpu.VMEM(weight.shape, BF16),
        in_specs=[pl.BlockSpec(memory_space=pltpu.HBM)],
        out_specs=pl.BlockSpec(memory_space=pltpu.VMEM),
        scratch_shapes=[pltpu.SemaphoreType.DMA((PIECES,))],
        compiler_params=pltpu.CompilerParams(vmem_limit_bytes=VMEM_LIMIT),
        cost_estimate=pl.CostEstimate(
            flops=0, bytes_accessed=4 * weight.size, transcendentals=0
        ),
        name="fetch",
    )(*in_hbm(weight))


def on_device(residual, queries, key_rows, value_rows, out_weight, norm_gain, q_weight):
    n = lax.axis_size("tp")
    device = lax.axis_index("tp")
    tokens = queries.shape[0]
    local = residual.shape[0]
    D = residual.shape[1]
    levels = late_levels(n)
    square = (6, 2, 4)

    def swap(x, distance):
        return lax.ppermute(x, "tp", [(i, i ^ distance) for i in range(n)])

    half = tokens // 2
    context, weight = attend(n, local, queries, key_rows, value_rows, out_weight)
    sent = jnp.dot(context[half:], weight, preferred_element_type=F32).astype(BF16)
    got = swap(sent, 1)
    total = jnp.dot(context[:half], weight, preferred_element_type=F32)
    total = lax.optimization_barrier(total) + got.astype(F32)
    part = half // 4
    pieces = [total[k * part : (k + 1) * part].astype(BF16) for k in range(1, 4)]
    arrived = [swap(piece, distance) for piece, distance in zip(pieces, square)]
    arrived[0], q_weight = lax.optimization_barrier((arrived[0], q_weight))
    total, q_weight = lax.optimization_barrier(
        (total[:part] + arrived[0].astype(F32), fetch(q_weight))
    )
    for piece in arrived[1:]:
        total = total + piece.astype(F32)
    for level in levels[:-1]:
        kept = total.shape[0] // 2
        total = total[:kept] + swap(total[kept:].astype(BF16), level).astype(F32)
    total = jnp.concatenate([total[:local] + residual.astype(F32), total[local:]], axis=0)
    got = swap(total.astype(BF16), levels[-1]).astype(F32)
    stream = total + jnp.concatenate([got[local:], got[:local]], axis=0)
    rows = stream.shape[0]
    grouped = stream.reshape(rows, D // QB, QB)
    scales = jnp.max(jnp.abs(grouped), axis=2) + EPS
    codes = (grouped / scales[:, :, None]).astype(BF16)
    decoded = (codes.astype(F32) * scales[:, :, None]).reshape(rows, D)
    mean_sq = jnp.mean(decoded * decoded, axis=1, keepdims=True)
    held = (decoded * lax.rsqrt(mean_sq + 1e-05) * norm_gain[None, :]).astype(BF16)
    for level in levels[-2::-1]:
        held = jnp.concatenate([held, swap(held, level)], axis=0)
    held = jnp.concatenate([held] + [swap(held, distance) for distance in square], axis=0)
    other = swap(held, 1)
    out_mine = jnp.dot(held, q_weight, preferred_element_type=F32).astype(BF16)
    out_other = jnp.dot(other, q_weight, preferred_element_type=F32).astype(BF16)
    found = jnp.concatenate([out_mine, out_other], axis=0)
    row = jnp.arange(tokens)
    pick = (owner_token(row, device, n, local)[:, None] == row[None, :]).astype(BF16)
    next_queries = lax.dot_general(
        pick, found, (((0,), (0,)), ((), ())), preferred_element_type=F32
    ).astype(BF16)
    return (codes.reshape(rows, D)[:local], scales[:local], next_queries)


def solution(mesh):
    in_specs = (
        P(("replica", "tp"), None),
        P("replica", "tp"),
        P("replica", None),
        P("replica", None),
        P("tp", None),
        P(),
        P(None, "tp"),
    )
    out_specs = (P(("replica", "tp"), None), P(("replica", "tp"), None), P("replica", "tp"))
    return jax.shard_map(
        on_device, mesh=mesh, in_specs=in_specs, out_specs=out_specs, check_vma=False
    )
```

```python
import functools

import jax
import jax.numpy as jnp
from jax import lax
from jax.experimental import pallas as pl
from jax.experimental.pallas import tpu as pltpu
from jax.sharding import PartitionSpec as P

HD = 128
QB = 128
EPS = 1e-06
F32 = jnp.float32
BF16 = jnp.bfloat16
PIECES = 4
STEPS = 8
VMEM_LIMIT = 24 << 20


def late_levels(n):
    return [1 << b for b in range(3, n.bit_length() - 1)]


def owner_token(row, device, n, local):
    bits = [1, 2, 6] + late_levels(n)
    shift = local.bit_length() - 1
    block = row >> shift
    distance = jnp.zeros_like(row)
    for place, bit in enumerate(bits):
        distance = distance ^ (((block >> (len(bits) - 1 - place)) & 1) * bit)
    return ((device ^ distance) << shift) | (row & (local - 1))


def attend_kernel(
    n, local, queries, keys, values, weight, context, held, query, key, value, small, large
):
    device = lax.axis_index("tp")
    tokens = queries.shape[0]
    heads = queries.shape[1] // HD
    group = heads * n // (keys.shape[1] // HD)
    copies = [pltpu.make_async_copy(queries, query, small.at[0])]
    for h in range(heads):
        at = pl.ds(pl.multiple_of(lax.div(device * heads + h, group) * HD, HD), HD)
        copies.append(pltpu.make_async_copy(keys.at[:, at], key.at[h], small.at[1 + 2 * h]))
        copies.append(pltpu.make_async_copy(values.at[:, at], value.at[h], small.at[2 + 2 * h]))
    depth = held.shape[0] // PIECES
    late = []
    for c in range(PIECES):
        part = pl.ds(c * depth, depth)
        late.append(pltpu.make_async_copy(weight.at[part], held.at[part], large.at[c]))
    for copy in copies + late:
        copy.start()
    row = lax.broadcasted_iota(jnp.int32, (tokens, tokens), 0)
    col = lax.broadcasted_iota(jnp.int32, (tokens, tokens), 1)
    token = owner_token(row, device, n, local)
    pick = (token == col).astype(F32).astype(BF16)
    for copy in copies:
        copy.wait()
    ordered = jnp.dot(pick, query[...], preferred_element_type=F32).astype(BF16)
    for h in range(heads):
        scores = lax.dot_general(
            ordered[:, h * HD : (h + 1) * HD],
            key[h],
            (((1,), (1,)), ((), ())),
            preferred_element_type=F32,
        ) / jnp.sqrt(F32(HD))
        scores = jnp.where(col <= token, scores, F32(-1e30))
        weights = jnp.exp(scores - jnp.max(scores, axis=1, keepdims=True))
        probs = (weights / jnp.sum(weights, axis=1, keepdims=True)).astype(BF16)
        context[:, h * HD : (h + 1) * HD] = jnp.dot(
            probs, value[h], preferred_element_type=F32
        ).astype(BF16)
    for copy in late:
        copy.wait()


def in_hbm(*arrays):
    return [pltpu.with_memory_space_constraint(x, pltpu.HBM) for x in arrays]


def attend(n, local, queries, keys, values, weight):
    tokens = queries.shape[0]
    heads = queries.shape[1] // HD
    whole = pl.BlockSpec(memory_space=pltpu.VMEM)
    return pl.pallas_call(
        functools.partial(attend_kernel, n, local),
        out_shape=[
            jax.ShapeDtypeStruct(queries.shape, BF16),
            pltpu.VMEM(weight.shape, BF16),
        ],
        in_specs=[pl.BlockSpec(memory_space=pltpu.HBM)] * 4,
        out_specs=[whole, whole],
        scratch_shapes=[
            pltpu.VMEM(queries.shape, BF16),
            pltpu.VMEM((heads, tokens, HD), BF16),
            pltpu.VMEM((heads, tokens, HD), BF16),
            pltpu.SemaphoreType.DMA((1 + 2 * heads,)),
            pltpu.SemaphoreType.DMA((PIECES,)),
        ],
        compiler_params=pltpu.CompilerParams(vmem_limit_bytes=VMEM_LIMIT),
        cost_estimate=pl.CostEstimate(
            flops=0, bytes_accessed=2 * weight.size, transcendentals=0
        ),
        name="attend",
    )(*in_hbm(queries, keys, values, weight))


def times(rows, weight):
    depth = weight.shape[0] // STEPS
    total = jnp.zeros((rows.shape[0], weight.shape[1]), F32)
    for c in range(STEPS):
        part = pl.ds(c * depth, depth)
        total += jnp.dot(rows[:, part], weight[part], preferred_element_type=F32)
    return total


def first_dot_kernel(rows, weight, out):
    out[...] = times(rows, weight).astype(BF16)


def last_dot_kernel(n, local, rows, weight, near, out):
    device = lax.axis_index("tp")
    tokens, half = out.shape[0], rows.shape[0]
    row = lax.broadcasted_iota(jnp.int32, (tokens, half), 1) ^ (3 * half // 4)
    token = lax.broadcasted_iota(jnp.int32, (tokens, half), 0)
    far = times(rows, weight).astype(BF16)
    total = jnp.zeros(out.shape, F32)
    for start, values in ((0, near[...]), (half, far)):
        pick = (owner_token(row + start, device, n, local) == token).astype(F32).astype(BF16)
        total += jnp.dot(pick, values, preferred_element_type=F32)
    out[...] = total.astype(BF16)


def small_call(kernel, shape, name, *operands):
    spec = pl.BlockSpec(memory_space=pltpu.VMEM)
    return pl.pallas_call(
        kernel,
        out_shape=jax.ShapeDtypeStruct(shape, BF16),
        in_specs=[spec] * len(operands),
        out_specs=spec,
        compiler_params=pltpu.CompilerParams(vmem_limit_bytes=VMEM_LIMIT),
        cost_estimate=pl.CostEstimate(
            flops=2 * operands[0].size * operands[1].shape[1],
            bytes_accessed=2 * operands[1].size,
            transcendentals=0,
        ),
        name=name,
    )(*operands)


def on_device(residual, queries, key_rows, value_rows, out_weight, norm_gain, q_weight):
    n = lax.axis_size("tp")
    device = lax.axis_index("tp")
    tokens = queries.shape[0]
    local = residual.shape[0]
    D = residual.shape[1]
    levels = late_levels(n)
    square = (6, 2, 4)

    def swap(x, distance):
        return lax.ppermute(x, "tp", [(i, i ^ distance) for i in range(n)])

    half = tokens // 2
    context, weight = attend(n, local, queries, key_rows, value_rows, out_weight)
    sent = jnp.dot(context[half:], weight, preferred_element_type=F32).astype(BF16)
    got = swap(sent, 1)
    total = jnp.dot(context[:half], weight, preferred_element_type=F32)
    total = lax.optimization_barrier(total) + got.astype(F32)
    part = half // 4
    pieces = [total[k * part : (k + 1) * part].astype(BF16) for k in range(1, 4)]
    arrived = [swap(piece, distance) for piece, distance in zip(pieces, square)]
    total = total[:part]
    for piece in arrived:
        total = total + piece.astype(F32)
    for level in levels[:-1]:
        kept = total.shape[0] // 2
        total = total[:kept] + swap(total[kept:].astype(BF16), level).astype(F32)
    total = jnp.concatenate([total[:local] + residual.astype(F32), total[local:]], axis=0)
    got = swap(total.astype(BF16), levels[-1]).astype(F32)
    stream = total + jnp.concatenate([got[local:], got[:local]], axis=0)
    rows = stream.shape[0]
    grouped = stream.reshape(rows, D // QB, QB)
    scales = jnp.max(jnp.abs(grouped), axis=2) + EPS
    codes = (grouped / scales[:, :, None]).astype(BF16)
    decoded = (codes.astype(F32) * scales[:, :, None]).reshape(rows, D)
    mean_sq = jnp.mean(decoded * decoded, axis=1, keepdims=True)
    held = (decoded * lax.rsqrt(mean_sq + 1e-05) * norm_gain[None, :]).astype(BF16)
    for level in levels[-2::-1]:
        held = jnp.concatenate([held, swap(held, level)], axis=0)
    arrived = [swap(held, distance) for distance in square]
    held = jnp.concatenate(arrived[::-1] + [held], axis=0)
    other = swap(held, 1)
    near = small_call(first_dot_kernel, (half, q_weight.shape[1]), "first_dot", held, q_weight)
    last = functools.partial(last_dot_kernel, n, local)
    shape = (tokens, q_weight.shape[1])
    next_queries = small_call(last, shape, "last_dot", other, q_weight, near)
    return (codes.reshape(rows, D)[:local], scales[:local], next_queries)


def solution(mesh):
    in_specs = (
        P(("replica", "tp"), None),
        P("replica", "tp"),
        P("replica", None),
        P("replica", None),
        P("tp", None),
        P(),
        P(None, "tp"),
    )
    out_specs = (P(("replica", "tp"), None), P(("replica", "tp"), None), P("replica", "tp"))
    return jax.shard_map(
        on_device, mesh=mesh, in_specs=in_specs, out_specs=out_specs, check_vma=False
    )
```

```python
import functools

import jax
import jax.numpy as jnp
from jax import lax
from jax.experimental import pallas as pl
from jax.experimental.pallas import tpu as pltpu
from jax.sharding import PartitionSpec as P

HD = 128
QB = 128
EPS = 1e-06
F32 = jnp.float32
BF16 = jnp.bfloat16
PIECES = 4
STEPS = 8
VMEM_LIMIT = 24 << 20


def late_levels(n):
    return [1 << b for b in range(3, n.bit_length() - 1)]


def owner_token(row, device, n, local):
    bits = [2, 6] + late_levels(n)
    shift = local.bit_length() - 2
    block = row >> shift
    distance = block >> (len(bits) + 1)
    part = (block >> len(bits)) & 1
    for place, bit in enumerate(bits):
        distance = distance ^ (((block >> (len(bits) - 1 - place)) & 1) * bit)
    own = (part << shift) | (row & (local // 2 - 1))
    return ((device ^ distance) << (shift + 1)) | own


def attend_kernel(
    n, local, queries, keys, values, weight, old, context, held, fresh, query, key, value, small, large
):
    device = lax.axis_index("tp")
    tokens = queries.shape[0]
    heads = queries.shape[1] // HD
    group = heads * n // (keys.shape[1] // HD)
    copies = [pltpu.make_async_copy(queries, query, small.at[0])]
    for h in range(heads):
        at = pl.ds(pl.multiple_of(lax.div(device * heads + h, group) * HD, HD), HD)
        copies.append(pltpu.make_async_copy(keys.at[:, at], key.at[h], small.at[1 + 2 * h]))
        copies.append(pltpu.make_async_copy(values.at[:, at], value.at[h], small.at[2 + 2 * h]))
    depth = held.shape[0] // PIECES
    late = [pltpu.make_async_copy(old, fresh, small.at[1 + 2 * heads])]
    for c in range(PIECES):
        part = pl.ds(c * depth, depth)
        late.append(pltpu.make_async_copy(weight.at[part], held.at[part], large.at[c]))
    for copy in copies + late:
        copy.start()
    row = lax.broadcasted_iota(jnp.int32, (tokens, tokens), 0)
    col = lax.broadcasted_iota(jnp.int32, (tokens, tokens), 1)
    token = owner_token(row, device, n, local)
    pick = (token == col).astype(F32).astype(BF16)
    for copy in copies:
        copy.wait()
    ordered = jnp.dot(pick, query[...], preferred_element_type=F32).astype(BF16)
    for h in range(heads):
        scores = lax.dot_general(
            ordered[:, h * HD : (h + 1) * HD],
            key[h],
            (((1,), (1,)), ((), ())),
            preferred_element_type=F32,
        ) / jnp.sqrt(F32(HD))
        scores = jnp.where(col <= token, scores, F32(-1e30))
        weights = jnp.exp(scores - jnp.max(scores, axis=1, keepdims=True))
        probs = (weights / jnp.sum(weights, axis=1, keepdims=True)).astype(BF16)
        context[:, h * HD : (h + 1) * HD] = jnp.dot(
            probs, value[h], preferred_element_type=F32
        ).astype(BF16)
    for copy in late:
        copy.wait()


def in_hbm(*arrays):
    return [pltpu.with_memory_space_constraint(x, pltpu.HBM) for x in arrays]


def attend(n, local, queries, keys, values, weight, old):
    tokens = queries.shape[0]
    heads = queries.shape[1] // HD
    whole = pl.BlockSpec(memory_space=pltpu.VMEM)
    return pl.pallas_call(
        functools.partial(attend_kernel, n, local),
        out_shape=[
            jax.ShapeDtypeStruct(queries.shape, BF16),
            pltpu.VMEM(weight.shape, BF16),
            pltpu.VMEM(old.shape, BF16),
        ],
        in_specs=[pl.BlockSpec(memory_space=pltpu.HBM)] * 5,
        out_specs=[whole] * 3,
        scratch_shapes=[
            pltpu.VMEM(queries.shape, BF16),
            pltpu.VMEM((heads, tokens, HD), BF16),
            pltpu.VMEM((heads, tokens, HD), BF16),
            pltpu.SemaphoreType.DMA((2 + 2 * heads,)),
            pltpu.SemaphoreType.DMA((PIECES,)),
        ],
        compiler_params=pltpu.CompilerParams(vmem_limit_bytes=VMEM_LIMIT),
        cost_estimate=pl.CostEstimate(
            flops=0, bytes_accessed=2 * weight.size, transcendentals=0
        ),
        name="attend",
    )(*in_hbm(queries, keys, values, weight, old))


def times(rows, weight):
    depth = weight.shape[0] // STEPS
    total = jnp.zeros((rows.shape[0], weight.shape[1]), F32)
    for c in range(STEPS):
        part = pl.ds(c * depth, depth)
        total += jnp.dot(rows[:, part], weight[part], preferred_element_type=F32)
    return total


def first_dot_kernel(rows, weight, out):
    out[...] = times(rows, weight).astype(BF16)


def last_dot_kernel(n, local, rows, weight, early, near, out):
    device = lax.axis_index("tp")
    tokens, quarter = out.shape[0], rows.shape[0]
    token = lax.broadcasted_iota(jnp.int32, (tokens, quarter), 0)
    row = lax.broadcasted_iota(jnp.int32, (tokens, quarter), 1) ^ (3 * quarter // 4)
    far = times(rows, weight).astype(BF16)
    total = jnp.zeros(out.shape, F32)
    for start, values in (
        (0, early[:quarter]),
        (2 * quarter, early[quarter:]),
        (quarter, near[...]),
        (3 * quarter, far),
    ):
        pick = (owner_token(row + start, device, n, local) == token).astype(F32).astype(BF16)
        total += jnp.dot(pick, values, preferred_element_type=F32)
    out[...] = total.astype(BF16)


def small_call(kernel, shape, name, *operands):
    spec = pl.BlockSpec(memory_space=pltpu.VMEM)
    return pl.pallas_call(
        kernel,
        out_shape=jax.ShapeDtypeStruct(shape, BF16),
        in_specs=[spec] * len(operands),
        out_specs=spec,
        compiler_params=pltpu.CompilerParams(vmem_limit_bytes=VMEM_LIMIT),
        cost_estimate=pl.CostEstimate(
            flops=2 * operands[0].size * operands[1].shape[1],
            bytes_accessed=2 * operands[1].size,
            transcendentals=0,
        ),
        name=name,
    )(*operands)


def on_device(residual, queries, key_rows, value_rows, out_weight, norm_gain, q_weight):
    n = lax.axis_size("tp")
    device = lax.axis_index("tp")
    tokens = queries.shape[0]
    local = residual.shape[0]
    D = residual.shape[1]
    levels = late_levels(n)
    square = (6, 2, 4)

    def swap(x, distance):
        return lax.ppermute(x, "tp", [(i, i ^ distance) for i in range(n)])

    half, quarter = tokens // 2, tokens // 4
    context, weight, fresh = attend(
        n, local, queries, key_rows, value_rows, out_weight, residual
    )

    def project(start):
        rows = context[start : start + quarter]
        return lax.optimization_barrier(jnp.dot(rows, weight, preferred_element_type=F32))

    got = [swap(project(half + h * quarter).astype(BF16), 1) for h in range(2)]
    kept = [project(h * quarter) for h in range(2)]

    def after(values, earlier):
        return list(lax.optimization_barrier((*values, *earlier))[: len(values)])

    def reduce(total, old, earlier):
        part = total.shape[0] // 4
        pieces = [total[k * part : (k + 1) * part].astype(BF16) for k in range(1, 4)]
        arrived = [swap(piece, distance) for piece, distance in zip(pieces, square)]
        arrived = after(arrived[::-1], earlier)
        total = total[:part]
        for piece in arrived:
            total = total + piece.astype(F32)
        for level in levels[:-1]:
            rest = total.shape[0] // 2
            total = total[:rest] + swap(total[rest:].astype(BF16), level).astype(F32)
        own = old.shape[0]
        return jnp.concatenate([total[:own] + old.astype(F32), total[own:]], axis=0)

    def finish(total, own, earlier):
        (arrived,) = after([swap(total.astype(BF16), levels[-1])], earlier)
        arrived = arrived.astype(F32)
        stream = total + jnp.concatenate([arrived[own:], arrived[:own]], axis=0)
        rows = stream.shape[0]
        grouped = stream.reshape(rows, D // QB, QB)
        scales = jnp.max(jnp.abs(grouped), axis=2) + EPS
        codes = (grouped / scales[:, :, None]).astype(BF16)
        decoded = (codes.astype(F32) * scales[:, :, None]).reshape(rows, D)
        mean_sq = jnp.mean(decoded * decoded, axis=1, keepdims=True)
        normed = (decoded * lax.rsqrt(mean_sq + 1e-05) * norm_gain[None, :]).astype(BF16)
        return codes.reshape(rows, D)[:own], scales[:own], normed

    def gather(held, earlier):
        for level in levels[-2::-1]:
            held = jnp.concatenate([held, swap(held, level)], axis=0)
        arrived = after([swap(held, distance) for distance in square[::-1]], earlier)
        return jnp.concatenate(arrived + [held], axis=0)

    part = local // 2
    codes, scales, normed, sums, held = [], [], [], [], []
    for h in range(2):
        old = (residual, fresh)[h][h * part : (h + 1) * part]
        sums.append(reduce(kept[h] + got[h].astype(F32), old, sums[:h]))
    for h in range(2):
        out = finish(sums[h], part, normed[:h])
        codes.append(out[0])
        scales.append(out[1])
        normed.append(out[2])
    for h in range(2):
        held.append(gather(normed[h], held[:h]))
    early = jnp.concatenate([held[0], swap(held[0], 1)], axis=0)
    early = small_call(first_dot_kernel, (half, q_weight.shape[1]), "early_dot", early, q_weight)
    other = swap(held[1], 1)
    shape = (quarter, q_weight.shape[1])
    near = small_call(first_dot_kernel, shape, "near_dot", held[1], q_weight)
    last = functools.partial(last_dot_kernel, n, local)
    shape = (tokens, q_weight.shape[1])
    next_queries = small_call(last, shape, "last_dot", other, q_weight, early, near)
    return jnp.concatenate(codes, axis=0), jnp.concatenate(scales, axis=0), next_queries


def solution(mesh):
    in_specs = (
        P(("replica", "tp"), None),
        P("replica", "tp"),
        P("replica", None),
        P("replica", None),
        P("tp", None),
        P(),
        P(None, "tp"),
    )
    out_specs = (P(("replica", "tp"), None), P(("replica", "tp"), None), P("replica", "tp"))
    return jax.shard_map(
        on_device, mesh=mesh, in_specs=in_specs, out_specs=out_specs, check_vma=False
    )
```

```python
import functools

import jax
import jax.numpy as jnp
from jax import lax
from jax.experimental import pallas as pl
from jax.experimental.pallas import tpu as pltpu
from jax.sharding import PartitionSpec as P

HD = 128
QB = 128
EPS = 1e-06
F32 = jnp.float32
BF16 = jnp.bfloat16
PIECES = 4
STEPS = 8
VMEM_LIMIT = 24 << 20


def late_levels(n):
    return [1 << b for b in range(3, n.bit_length() - 1)]


def owner_token(row, device, n, local):
    bits = late_levels(n)
    shift = local.bit_length() - 2
    block = row >> shift
    distance = block >> (len(bits) + 3)
    part = (block >> (len(bits) + 2)) & 1
    place = (block >> len(bits)) & 3
    for order, bit in enumerate(bits):
        distance = distance ^ (((block >> (len(bits) - 1 - order)) & 1) * bit)
    own = (part << shift) | (row & (local // 2 - 1))
    owner = ((device ^ distance) & ~6) | (place << 1)
    return (owner << (shift + 1)) | own


def attend_kernel(
    n, local, queries, keys, values, weight, old, context, held, fresh, query, key, value, small, large
):
    device = lax.axis_index("tp")
    tokens = queries.shape[0]
    heads = queries.shape[1] // HD
    group = heads * n // (keys.shape[1] // HD)
    copies = [pltpu.make_async_copy(queries, query, small.at[0])]
    for h in range(heads):
        at = pl.ds(pl.multiple_of(lax.div(device * heads + h, group) * HD, HD), HD)
        copies.append(pltpu.make_async_copy(keys.at[:, at], key.at[h], small.at[1 + 2 * h]))
        copies.append(pltpu.make_async_copy(values.at[:, at], value.at[h], small.at[2 + 2 * h]))
    depth = held.shape[0] // PIECES
    late = [pltpu.make_async_copy(old, fresh, small.at[1 + 2 * heads])]
    for c in range(PIECES):
        part = pl.ds(c * depth, depth)
        late.append(pltpu.make_async_copy(weight.at[part], held.at[part], large.at[c]))
    for copy in copies + late:
        copy.start()
    row = lax.broadcasted_iota(jnp.int32, (tokens, tokens), 0)
    col = lax.broadcasted_iota(jnp.int32, (tokens, tokens), 1)
    token = owner_token(row, device, n, local)
    pick = (token == col).astype(F32).astype(BF16)
    for copy in copies:
        copy.wait()
    ordered = jnp.dot(pick, query[...], preferred_element_type=F32).astype(BF16)
    for h in range(heads):
        scores = lax.dot_general(
            ordered[:, h * HD : (h + 1) * HD],
            key[h],
            (((1,), (1,)), ((), ())),
            preferred_element_type=F32,
        ) / jnp.sqrt(F32(HD))
        scores = jnp.where(col <= token, scores, F32(-1e30))
        weights = jnp.exp(scores - jnp.max(scores, axis=1, keepdims=True))
        probs = (weights / jnp.sum(weights, axis=1, keepdims=True)).astype(BF16)
        context[:, h * HD : (h + 1) * HD] = jnp.dot(
            probs, value[h], preferred_element_type=F32
        ).astype(BF16)
    for copy in late:
        copy.wait()


def in_hbm(*arrays):
    return [pltpu.with_memory_space_constraint(x, pltpu.HBM) for x in arrays]


def attend(n, local, queries, keys, values, weight, old):
    tokens = queries.shape[0]
    heads = queries.shape[1] // HD
    whole = pl.BlockSpec(memory_space=pltpu.VMEM)
    return pl.pallas_call(
        functools.partial(attend_kernel, n, local),
        out_shape=[
            jax.ShapeDtypeStruct(queries.shape, BF16),
            pltpu.VMEM(weight.shape, BF16),
            pltpu.VMEM(old.shape, BF16),
        ],
        in_specs=[pl.BlockSpec(memory_space=pltpu.HBM)] * 5,
        out_specs=[whole] * 3,
        scratch_shapes=[
            pltpu.VMEM(queries.shape, BF16),
            pltpu.VMEM((heads, tokens, HD), BF16),
            pltpu.VMEM((heads, tokens, HD), BF16),
            pltpu.SemaphoreType.DMA((2 + 2 * heads,)),
            pltpu.SemaphoreType.DMA((PIECES,)),
        ],
        compiler_params=pltpu.CompilerParams(vmem_limit_bytes=VMEM_LIMIT),
        cost_estimate=pl.CostEstimate(
            flops=0, bytes_accessed=2 * weight.size, transcendentals=0
        ),
        name="attend",
    )(*in_hbm(queries, keys, values, weight, old))


def times(rows, weight):
    depth = weight.shape[0] // STEPS
    total = jnp.zeros((rows.shape[0], weight.shape[1]), F32)
    for c in range(STEPS):
        part = pl.ds(c * depth, depth)
        total += jnp.dot(rows[:, part], weight[part], preferred_element_type=F32)
    return total


def first_dot_kernel(early, near, weight, out):
    split = early.shape[0]
    out[:split] = times(early, weight)
    out[split:] = times(near, weight)


def last_dot_kernel(n, local, rows, before, weight, out):
    device = lax.axis_index("tp")
    tokens, quarter = out.shape[0], rows.shape[0]
    token = lax.broadcasted_iota(jnp.int32, (tokens, quarter), 0)
    row = lax.broadcasted_iota(jnp.int32, (tokens, quarter), 1)
    total = jnp.zeros(out.shape, F32)
    for start, values in (
        (0, before[:quarter]),
        (2 * quarter, before[quarter : 2 * quarter]),
        (quarter, before[2 * quarter :]),
        (3 * quarter, times(rows, weight)),
    ):
        pick = (owner_token(row + start, device, n, local) == token).astype(F32).astype(BF16)
        total += jnp.dot(pick, values.astype(BF16), preferred_element_type=F32)
    out[...] = total.astype(BF16)


def small_call(kernel, shape, dtype, name, *operands):
    spec = pl.BlockSpec(memory_space=pltpu.VMEM)
    return pl.pallas_call(
        kernel,
        out_shape=jax.ShapeDtypeStruct(shape, dtype),
        in_specs=[spec] * len(operands),
        out_specs=spec,
        compiler_params=pltpu.CompilerParams(vmem_limit_bytes=VMEM_LIMIT),
        cost_estimate=pl.CostEstimate(
            flops=2 * operands[0].size * operands[-1].shape[1],
            bytes_accessed=2 * operands[-1].size,
            transcendentals=0,
        ),
        name=name,
    )(*operands)


def on_device(residual, queries, key_rows, value_rows, out_weight, norm_gain, q_weight):
    n = lax.axis_size("tp")
    device = lax.axis_index("tp")
    tokens = queries.shape[0]
    local = residual.shape[0]
    D = residual.shape[1]
    levels = late_levels(n)
    squares = [[b + c + 2 * k for k in range(4)] for b in range(0, n, 8) for c in range(2)]

    def exchange(x):
        return lax.all_to_all(x, "tp", 0, 0, axis_index_groups=squares, tiled=True)

    def swap(x, distance):
        return lax.ppermute(x, "tp", [(i, i ^ distance) for i in range(n)])

    half, quarter = tokens // 2, tokens // 4
    context, weight, fresh = attend(
        n, local, queries, key_rows, value_rows, out_weight, residual
    )

    def project(start):
        rows = context[start : start + quarter]
        return lax.optimization_barrier(jnp.dot(rows, weight, preferred_element_type=F32))

    got = [swap(project(half + h * quarter).astype(BF16), 1) for h in range(2)]
    kept = [project(h * quarter) for h in range(2)]

    def after(values, earlier):
        return list(lax.optimization_barrier((*values, *earlier))[: len(values)])

    def reduce(total, old, earlier):
        pieces = total.astype(BF16).reshape(4, total.shape[0] // 4, D)
        (arrived,) = after([exchange(pieces)], earlier)
        total = jnp.sum(arrived.astype(F32), axis=0)
        for level in levels[:-1]:
            rest = total.shape[0] // 2
            total = total[:rest] + swap(total[rest:].astype(BF16), level).astype(F32)
        own = old.shape[0]
        return jnp.concatenate([total[:own] + old.astype(F32), total[own:]], axis=0)

    def finish(total, own, earlier):
        (arrived,) = after([swap(total.astype(BF16), levels[-1])], earlier)
        arrived = arrived.astype(F32)
        stream = total + jnp.concatenate([arrived[own:], arrived[:own]], axis=0)
        rows = stream.shape[0]
        grouped = stream.reshape(rows, D // QB, QB)
        scales = jnp.max(jnp.abs(grouped), axis=2) + EPS
        codes = (grouped / scales[:, :, None]).astype(BF16)
        decoded = (codes.astype(F32) * scales[:, :, None]).reshape(rows, D)
        mean_sq = jnp.mean(decoded * decoded, axis=1, keepdims=True)
        normed = (decoded * lax.rsqrt(mean_sq + 1e-05) * norm_gain[None, :]).astype(BF16)
        return codes.reshape(rows, D)[:own], scales[:own], normed

    def gather(held, earlier):
        for level in levels[-2::-1]:
            held = jnp.concatenate([held, swap(held, level)], axis=0)
        copies = jnp.broadcast_to(held[None], (4, *held.shape))
        (arrived,) = after([exchange(copies)], earlier)
        return arrived.reshape(-1, D)

    part = local // 2
    codes, scales, normed, sums, held = [], [], [], [], []
    for h in range(2):
        old = (residual, fresh)[h][h * part : (h + 1) * part]
        sums.append(reduce(kept[h] + got[h].astype(F32), old, sums[:h]))
    for h in range(2):
        out = finish(sums[h], part, normed[:h])
        codes.append(out[0])
        scales.append(out[1])
        normed.append(out[2])
    for h in range(2):
        held.append(gather(normed[h], held[:h]))
    early = jnp.concatenate([held[0], swap(held[0], 1)], axis=0)
    other = swap(held[1], 1)
    width = q_weight.shape[1]
    shape = (3 * quarter, width)
    before = small_call(first_dot_kernel, shape, F32, "first_dots", early, held[1], q_weight)
    last = functools.partial(last_dot_kernel, n, local)
    next_queries = small_call(last, (tokens, width), BF16, "last_dot", other, before, q_weight)
    return jnp.concatenate(codes, axis=0), jnp.concatenate(scales, axis=0), next_queries


def solution(mesh):
    in_specs = (
        P(("replica", "tp"), None),
        P("replica", "tp"),
        P("replica", None),
        P("replica", None),
        P("tp", None),
        P(),
        P(None, "tp"),
    )
    out_specs = (P(("replica", "tp"), None), P(("replica", "tp"), None), P("replica", "tp"))
    return jax.shard_map(
        on_device, mesh=mesh, in_specs=in_specs, out_specs=out_specs, check_vma=False
    )
```

```python
import functools

import jax
import jax.numpy as jnp
from jax import lax
from jax.experimental import pallas as pl
from jax.experimental.pallas import tpu as pltpu
from jax.sharding import PartitionSpec as P

HD = 128
QB = 128
EPS = 1e-06
F32 = jnp.float32
BF16 = jnp.bfloat16
PIECES = 4
STEPS = 8
VMEM_LIMIT = 24 << 20
SMALL_LIMIT = 16 << 20


def late_levels(n):
    return [1 << b for b in range(3, n.bit_length() - 1)]


def owner_token(row, device, n):
    bits = [2, 6] + late_levels(n)
    distance = row >> (len(bits) + 1)
    which = (row >> len(bits)) & 1
    block = row ^ which
    for place, bit in enumerate(bits):
        distance = distance ^ (((block >> (len(bits) - 1 - place)) & 1) * bit)
    return ((device ^ distance) << 1) | which


def attend_kernel(
    n, queries, keys, values, weight, context, held, query, key, value, small, large
):
    device = lax.axis_index("tp")
    tokens = queries.shape[0]
    heads = queries.shape[1] // HD
    group = heads * n // (keys.shape[1] // HD)
    copies = [pltpu.make_async_copy(queries, query, small.at[0])]
    for h in range(heads):
        at = pl.ds(pl.multiple_of(lax.div(device * heads + h, group) * HD, HD), HD)
        copies.append(pltpu.make_async_copy(keys.at[:, at], key.at[h], small.at[1 + 2 * h]))
        copies.append(pltpu.make_async_copy(values.at[:, at], value.at[h], small.at[2 + 2 * h]))
    depth = held.shape[0] // PIECES
    late = []
    for c in range(PIECES):
        part = pl.ds(c * depth, depth)
        late.append(pltpu.make_async_copy(weight.at[part], held.at[part], large.at[c]))
    for copy in copies + late:
        copy.start()
    row = lax.broadcasted_iota(jnp.int32, (tokens, tokens), 0)
    col = lax.broadcasted_iota(jnp.int32, (tokens, tokens), 1)
    token = owner_token(row, device, n)
    pick = (token == col).astype(F32).astype(BF16)
    for copy in copies:
        copy.wait()
    ordered = jnp.dot(pick, query[...], preferred_element_type=F32).astype(BF16)
    for h in range(heads):
        scores = lax.dot_general(
            ordered[:, h * HD : (h + 1) * HD],
            key[h],
            (((1,), (1,)), ((), ())),
            preferred_element_type=F32,
        ) / jnp.sqrt(F32(HD))
        scores = jnp.where(col <= token, scores, F32(-1e30))
        weights = jnp.exp(scores - jnp.max(scores, axis=1, keepdims=True))
        probs = (weights / jnp.sum(weights, axis=1, keepdims=True)).astype(BF16)
        context[:, h * HD : (h + 1) * HD] = jnp.dot(
            probs, value[h], preferred_element_type=F32
        ).astype(BF16)
    for copy in late:
        copy.wait()


def in_hbm(*arrays):
    return [pltpu.with_memory_space_constraint(x, pltpu.HBM) for x in arrays]


def attend(n, queries, keys, values, weight):
    tokens = queries.shape[0]
    heads = queries.shape[1] // HD
    whole = pl.BlockSpec(memory_space=pltpu.VMEM)
    return pl.pallas_call(
        functools.partial(attend_kernel, n),
        out_shape=[
            jax.ShapeDtypeStruct(queries.shape, BF16),
            pltpu.VMEM(weight.shape, BF16),
        ],
        in_specs=[pl.BlockSpec(memory_space=pltpu.HBM)] * 4,
        out_specs=[whole] * 2,
        scratch_shapes=[
            pltpu.VMEM(queries.shape, BF16),
            pltpu.VMEM((heads, tokens, HD), BF16),
            pltpu.VMEM((heads, tokens, HD), BF16),
            pltpu.SemaphoreType.DMA((1 + 2 * heads,)),
            pltpu.SemaphoreType.DMA((PIECES,)),
        ],
        compiler_params=pltpu.CompilerParams(vmem_limit_bytes=VMEM_LIMIT),
        cost_estimate=pl.CostEstimate(
            flops=0, bytes_accessed=2 * weight.size, transcendentals=0
        ),
        name="attend",
    )(*in_hbm(queries, keys, values, weight))


def parts(ref):
    width = ref.shape[1] // STEPS
    return [pl.ds(c * width, width) for c in range(STEPS)]


def split_kernel(which, kept, got, own, *pieces):
    rows = got.shape[0]
    part = rows // 4
    for at in parts(got):
        total = kept[which * rows : (which + 1) * rows, at] + got[:, at].astype(F32)
        own[:, at] = total[:part]
        for k, piece in enumerate(pieces, 1):
            piece[:, at] = total[k * part : (k + 1) * part].astype(BF16)


def settle_kernel(which, own, old, *refs):
    *arrived, total, turned = refs
    for at in parts(own):
        value = own[:, at]
        for piece in arrived:
            value = value + piece[:, at].astype(F32)
        row = lax.broadcasted_iota(jnp.int32, value.shape, 0)
        value = value + jnp.where(row == which, old[:, at].astype(F32), F32(0))
        total[:, at] = value
        turned[:, at] = jnp.concatenate([value[1:], value[:1]], axis=0).astype(BF16)


def encode_kernel(total, arrived, gain, *refs):
    *before, normed, codes, scales, decoded = refs
    blocks = total.shape[1] // QB
    row = lax.broadcasted_iota(jnp.int32, (total.shape[0], QB), 0)
    lane = lax.broadcasted_iota(jnp.int32, (total.shape[0], blocks), 1)
    all_scales = jnp.zeros(scales.shape, F32)
    squares = jnp.zeros(row.shape, F32)
    for b in range(blocks):
        at = pl.ds(b * QB, QB)
        stream = total[:, at] + arrived[:, at].astype(F32)
        scale = jnp.max(jnp.abs(stream), axis=1, keepdims=True) + EPS
        code = (stream / scale).astype(BF16).astype(F32)
        value = code * scale
        squares += value * value
        decoded[:, at] = value
        if before:
            code = jnp.where(row == 0, before[0][:, at].astype(F32), code)
        codes[:, at] = code.astype(BF16)
        all_scales = jnp.where(lane == b, scale, all_scales)
    if before:
        all_scales = jnp.where(
            lax.broadcasted_iota(jnp.int32, scales.shape, 0) == 0, before[1][...], all_scales
        )
    scales[...] = all_scales
    mean_sq = jnp.sum(squares, axis=1, keepdims=True) / total.shape[1]
    factor = lax.rsqrt(mean_sq + 1e-05)
    for at in parts(total):
        normed[:, at] = (decoded[:, at] * factor * gain[:, at]).astype(BF16)


def times(rows, weight):
    depth = weight.shape[0] // STEPS
    count = sum(r.shape[0] for r in rows)
    total = jnp.zeros((count, weight.shape[1]), F32)
    for c in range(STEPS):
        part = pl.ds(c * depth, depth)
        block = jnp.concatenate([r[:, part] for r in rows], axis=0)
        total += jnp.dot(block, weight[part], preferred_element_type=F32)
    return total


def first_dots_kernel(early, early_other, near, weight, out):
    out[...] = times([early, early_other, near], weight)


def last_dot_kernel(n, rows, before, weight, out):
    device = lax.axis_index("tp")
    tokens, quarter = out.shape[0], rows.shape[0]
    token = lax.broadcasted_iota(jnp.int32, (tokens, quarter), 0)
    row = lax.broadcasted_iota(jnp.int32, (tokens, quarter), 1) ^ (3 * quarter // 4)
    total = jnp.zeros(out.shape, F32)
    for start, values in (
        (0, before[:quarter]),
        (2 * quarter, before[quarter : 2 * quarter]),
        (quarter, before[2 * quarter :]),
        (3 * quarter, times([rows], weight)),
    ):
        pick = (owner_token(row + start, device, n) == token).astype(F32).astype(BF16)
        total += jnp.dot(pick, values.astype(BF16), preferred_element_type=F32)
    out[...] = total.astype(BF16)


def local_call(kernel, shapes, name, *operands, scratch=()):
    spec = pl.BlockSpec(memory_space=pltpu.VMEM)
    return pl.pallas_call(
        kernel,
        out_shape=[jax.ShapeDtypeStruct(shape, dtype) for shape, dtype in shapes],
        in_specs=[spec] * len(operands),
        out_specs=[spec] * len(shapes),
        scratch_shapes=list(scratch),
        compiler_params=pltpu.CompilerParams(vmem_limit_bytes=SMALL_LIMIT),
        cost_estimate=pl.CostEstimate(
            flops=0, bytes_accessed=sum(2 * x.size for x in operands), transcendentals=0
        ),
        name=name,
    )(*operands)


def on_device(residual, queries, key_rows, value_rows, out_weight, norm_gain, q_weight):
    n = lax.axis_size("tp")
    tokens = queries.shape[0]
    D = residual.shape[1]
    levels = late_levels(n)
    square = (6, 2, 4)

    def swap(x, distance):
        return lax.ppermute(x, "tp", [(i, i ^ distance) for i in range(n)])

    half, quarter = tokens // 2, tokens // 4
    part, pair = quarter // 4, (2, D)
    gain = norm_gain.reshape(1, D)
    context, weight = attend(n, queries, key_rows, value_rows, out_weight)
    sent = jnp.dot(context[half:], weight, preferred_element_type=F32).astype(BF16)
    got = [swap(sent[:quarter], 1), swap(sent[quarter:], 1)]
    kept = jnp.dot(context[:half], weight, preferred_element_type=F32)

    def reduce(which):
        shapes = [((part, D), F32)] + [((part, D), BF16)] * 3
        kernel = functools.partial(split_kernel, which)
        total, *pieces = local_call(kernel, shapes, f"split{which}", kept, got[which])
        arrived = [swap(piece, distance) for piece, distance in zip(pieces, square)]
        if len(levels) > 1:
            for piece in arrived:
                total = total + piece.astype(F32)
            arrived = []
        for level in levels[:-1]:
            rest = total.shape[0] // 2
            total = total[:rest] + swap(total[rest:].astype(BF16), level).astype(F32)
        kernel = functools.partial(settle_kernel, which)
        shapes = [(pair, F32), (pair, BF16)]
        return local_call(kernel, shapes, f"settle{which}", total, residual, *arrived)

    def gather(held):
        for level in levels[-2::-1]:
            held = jnp.concatenate([held, swap(held, level)], axis=0)
        arrived = [swap(held, distance) for distance in square]
        return jnp.concatenate(arrived[::-1] + [held], axis=0)

    sums = [reduce(which) for which in range(2)]
    sums = [(total, swap(turned, levels[-1])) for total, turned in sums]
    outs, held = [], []
    for which in range(2):
        shapes = [(pair, BF16), (pair, BF16), ((2, D // QB), F32)]
        normed, *outs = local_call(
            encode_kernel,
            shapes,
            f"encode{which}",
            *sums[which],
            gain,
            *outs,
            scratch=[pltpu.VMEM(pair, F32)],
        )
        held.append(gather(normed))
    others = [swap(rows, 1) for rows in held]
    width = q_weight.shape[1]
    shapes = [((3 * quarter, width), F32)]
    (before,) = local_call(
        first_dots_kernel, shapes, "first_dots", held[0], others[0], held[1], q_weight
    )
    kernel = functools.partial(last_dot_kernel, n)
    shapes = [((tokens, width), BF16)]
    (next_queries,) = local_call(kernel, shapes, "last_dot", others[1], before, q_weight)
    return (*outs, next_queries)


def solution(mesh):
    in_specs = (
        P(("replica", "tp"), None),
        P("replica", "tp"),
        P("replica", None),
        P("replica", None),
        P("tp", None),
        P(),
        P(None, "tp"),
    )
    out_specs = (P(("replica", "tp"), None), P(("replica", "tp"), None), P("replica", "tp"))
    return jax.shard_map(
        on_device, mesh=mesh, in_specs=in_specs, out_specs=out_specs, check_vma=False
    )
```

```python
import functools

import jax
import jax.numpy as jnp
from jax import lax
from jax.experimental import pallas as pl
from jax.experimental.pallas import tpu as pltpu
from jax.sharding import PartitionSpec as P

HD = 128
QB = 128
EPS = 1e-06
F32 = jnp.float32
BF16 = jnp.bfloat16
PIECES = 4
STEPS = 8
VMEM_LIMIT = 24 << 20
SMALL_LIMIT = 16 << 20


def late_levels(n):
    return [1 << b for b in range(3, n.bit_length() - 1)]


def owner_token(row, device, n):
    bits = [2, 6] + late_levels(n)
    distance = row >> (len(bits) + 1)
    which = (row >> len(bits)) & 1
    block = row ^ which
    for place, bit in enumerate(bits):
        distance = distance ^ (((block >> (len(bits) - 1 - place)) & 1) * bit)
    return ((device ^ distance) << 1) | which


def attend_kernel(
    n, queries, keys, values, weight, context, held, query, key, value, small, large
):
    device = lax.axis_index("tp")
    tokens = queries.shape[0]
    heads = queries.shape[1] // HD
    group = heads * n // (keys.shape[1] // HD)
    copies = [pltpu.make_async_copy(queries, query, small.at[0])]
    for h in range(heads):
        at = pl.ds(pl.multiple_of(lax.div(device * heads + h, group) * HD, HD), HD)
        copies.append(pltpu.make_async_copy(keys.at[:, at], key.at[h], small.at[1 + 2 * h]))
        copies.append(pltpu.make_async_copy(values.at[:, at], value.at[h], small.at[2 + 2 * h]))
    depth = held.shape[0] // PIECES
    late = []
    for c in range(PIECES):
        part = pl.ds(c * depth, depth)
        late.append(pltpu.make_async_copy(weight.at[part], held.at[part], large.at[c]))
    for copy in copies + late:
        copy.start()
    row = lax.broadcasted_iota(jnp.int32, (tokens, tokens), 0)
    col = lax.broadcasted_iota(jnp.int32, (tokens, tokens), 1)
    token = owner_token(row, device, n)
    pick = (token == col).astype(F32).astype(BF16)
    for copy in copies:
        copy.wait()
    ordered = jnp.dot(pick, query[...], preferred_element_type=F32).astype(BF16)
    for h in range(heads):
        scores = lax.dot_general(
            ordered[:, h * HD : (h + 1) * HD],
            key[h],
            (((1,), (1,)), ((), ())),
            preferred_element_type=F32,
        ) / jnp.sqrt(F32(HD))
        scores = jnp.where(col <= token, scores, F32(-1e30))
        weights = jnp.exp(scores - jnp.max(scores, axis=1, keepdims=True))
        probs = (weights / jnp.sum(weights, axis=1, keepdims=True)).astype(BF16)
        context[:, h * HD : (h + 1) * HD] = jnp.dot(
            probs, value[h], preferred_element_type=F32
        ).astype(BF16)
    for copy in late:
        copy.wait()


def in_hbm(*arrays):
    return [pltpu.with_memory_space_constraint(x, pltpu.HBM) for x in arrays]


def attend(n, queries, keys, values, weight):
    tokens = queries.shape[0]
    heads = queries.shape[1] // HD
    whole = pl.BlockSpec(memory_space=pltpu.VMEM)
    return pl.pallas_call(
        functools.partial(attend_kernel, n),
        out_shape=[
            jax.ShapeDtypeStruct(queries.shape, BF16),
            pltpu.VMEM(weight.shape, BF16),
        ],
        in_specs=[pl.BlockSpec(memory_space=pltpu.HBM)] * 4,
        out_specs=[whole] * 2,
        scratch_shapes=[
            pltpu.VMEM(queries.shape, BF16),
            pltpu.VMEM((heads, tokens, HD), BF16),
            pltpu.VMEM((heads, tokens, HD), BF16),
            pltpu.SemaphoreType.DMA((1 + 2 * heads,)),
            pltpu.SemaphoreType.DMA((PIECES,)),
        ],
        compiler_params=pltpu.CompilerParams(vmem_limit_bytes=VMEM_LIMIT),
        cost_estimate=pl.CostEstimate(
            flops=0, bytes_accessed=2 * weight.size, transcendentals=0
        ),
        name="attend",
    )(*in_hbm(queries, keys, values, weight))


def parts(ref):
    width = ref.shape[1] // STEPS
    return [pl.ds(c * width, width) for c in range(STEPS)]


def split_kernel(which, kept, got, own, *pieces):
    rows = got.shape[0]
    part = rows // 4
    for at in parts(got):
        total = kept[which * rows : (which + 1) * rows, at] + got[:, at].astype(F32)
        own[:, at] = total[:part]
        for k, piece in enumerate(pieces, 1):
            piece[:, at] = total[k * part : (k + 1) * part].astype(BF16)


def settle_kernel(which, own, old, *refs):
    *arrived, total, turned = refs
    for at in parts(own):
        value = own[:, at]
        for piece in arrived:
            value = value + piece[:, at].astype(F32)
        row = lax.broadcasted_iota(jnp.int32, value.shape, 0)
        value = value + jnp.where(row == which, old[:, at].astype(F32), F32(0))
        total[:, at] = value
        turned[:, at] = jnp.concatenate([value[1:], value[:1]], axis=0).astype(BF16)


def encode_kernel(total, arrived, gain, *refs):
    *before, normed, codes, scales, decoded = refs
    blocks = total.shape[1] // QB
    row = lax.broadcasted_iota(jnp.int32, (total.shape[0], QB), 0)
    lane = lax.broadcasted_iota(jnp.int32, (total.shape[0], blocks), 1)
    all_scales = jnp.zeros(scales.shape, F32)
    squares = jnp.zeros(row.shape, F32)
    for b in range(blocks):
        at = pl.ds(b * QB, QB)
        stream = total[:, at] + arrived[:, at].astype(F32)
        scale = jnp.max(jnp.abs(stream), axis=1, keepdims=True) + EPS
        code = (stream / scale).astype(BF16).astype(F32)
        value = code * scale
        squares += value * value
        decoded[:, at] = value
        if before:
            code = jnp.where(row == 0, before[0][:, at].astype(F32), code)
        codes[:, at] = code.astype(BF16)
        all_scales = jnp.where(lane == b, scale, all_scales)
    if before:
        all_scales = jnp.where(
            lax.broadcasted_iota(jnp.int32, scales.shape, 0) == 0, before[1][...], all_scales
        )
    scales[...] = all_scales
    mean_sq = jnp.sum(squares, axis=1, keepdims=True) / total.shape[1]
    factor = lax.rsqrt(mean_sq + 1e-05)
    for at in parts(total):
        normed[:, at] = (decoded[:, at] * factor * gain[:, at]).astype(BF16)


def times(rows, weight):
    depth = weight.shape[0] // STEPS
    count = sum(r.shape[0] for r in rows)
    total = jnp.zeros((count, weight.shape[1]), F32)
    for c in range(STEPS):
        part = pl.ds(c * depth, depth)
        block = jnp.concatenate([r[:, part] for r in rows], axis=0)
        total += jnp.dot(block, weight[part], preferred_element_type=F32)
    return total


def first_dots_kernel(*refs):
    *rows, weight, codes, scales, out, codes_out, scales_out, sems = refs
    copies = [
        pltpu.make_async_copy(codes, codes_out, sems.at[0]),
        pltpu.make_async_copy(scales, scales_out, sems.at[1]),
    ]
    for copy in copies:
        copy.start()
    out[...] = times(rows, weight)
    for copy in copies:
        copy.wait()


def last_dot_kernel(n, *refs):
    *rows, before, weight, out = refs
    device = lax.axis_index("tp")
    tokens = out.shape[0]
    quarter = tokens // 4
    token = lax.broadcasted_iota(jnp.int32, (tokens, quarter), 0)
    row = lax.broadcasted_iota(jnp.int32, (tokens, quarter), 1) ^ (3 * quarter // 4)
    total = jnp.zeros(out.shape, F32)
    for start, values in (
        (0, before[:quarter]),
        (2 * quarter, before[quarter : 2 * quarter]),
        (quarter, before[2 * quarter :]),
        (3 * quarter, times(rows, weight)),
    ):
        pick = (owner_token(row + start, device, n) == token).astype(F32).astype(BF16)
        total += jnp.dot(pick, values.astype(BF16), preferred_element_type=F32)
    out[...] = total.astype(BF16)


def local_call(kernel, shapes, name, *operands, scratch=()):
    spec = pl.BlockSpec(memory_space=pltpu.VMEM)
    spaces = [space[0] if space else pltpu.VMEM for _, _, *space in shapes]
    return pl.pallas_call(
        kernel,
        out_shape=[
            (space[0] if space else jax.ShapeDtypeStruct)(shape, dtype)
            for shape, dtype, *space in shapes
        ],
        in_specs=[spec] * len(operands),
        out_specs=[pl.BlockSpec(memory_space=space) for space in spaces],
        scratch_shapes=list(scratch),
        compiler_params=pltpu.CompilerParams(vmem_limit_bytes=SMALL_LIMIT),
        cost_estimate=pl.CostEstimate(
            flops=0, bytes_accessed=sum(2 * x.size for x in operands), transcendentals=0
        ),
        name=name,
    )(*operands)


def on_device(residual, queries, key_rows, value_rows, out_weight, norm_gain, q_weight):
    n = lax.axis_size("tp")
    tokens = queries.shape[0]
    D = residual.shape[1]
    levels = late_levels(n)
    square = (6, 2, 4)

    def swap(x, distance):
        return lax.ppermute(x, "tp", [(i, i ^ distance) for i in range(n)])

    half, quarter = tokens // 2, tokens // 4
    part, pair = quarter // 4, (2, D)
    gain = norm_gain.reshape(1, D)
    context, weight = attend(n, queries, key_rows, value_rows, out_weight)
    sent = jnp.dot(context[half:], weight, preferred_element_type=F32).astype(BF16)
    got = [swap(sent[:quarter], 1), swap(sent[quarter:], 1)]
    kept = jnp.dot(context[:half], weight, preferred_element_type=F32)

    def reduce(which):
        shapes = [((part, D), F32)] + [((part, D), BF16)] * 3
        kernel = functools.partial(split_kernel, which)
        total, *pieces = local_call(kernel, shapes, f"split{which}", kept, got[which])
        arrived = [swap(piece, distance) for piece, distance in zip(pieces, square)]
        if len(levels) > 1:
            for piece in arrived:
                total = total + piece.astype(F32)
            arrived = []
        for level in levels[:-1]:
            rest = total.shape[0] // 2
            total = total[:rest] + swap(total[rest:].astype(BF16), level).astype(F32)
        kernel = functools.partial(settle_kernel, which)
        shapes = [(pair, F32), (pair, BF16)]
        return local_call(kernel, shapes, f"settle{which}", total, residual, *arrived)

    def gather(held):
        for level in levels[-2::-1]:
            held = jnp.concatenate([held, swap(held, level)], axis=0)
        return [swap(held, distance) for distance in square][::-1] + [held]

    sums = [reduce(which) for which in range(2)]
    sums = [(total, swap(turned, levels[-1])) for total, turned in sums]
    outs, held = [], []
    for which in range(2):
        shapes = [(pair, BF16), (pair, BF16, pltpu.VMEM), ((2, D // QB), F32, pltpu.VMEM)]
        normed, *outs = local_call(
            encode_kernel,
            shapes,
            f"encode{which}",
            *sums[which],
            gain,
            *outs,
            scratch=[pltpu.VMEM(pair, F32)],
        )
        held.append(gather(normed))
    early, near = (jnp.concatenate(pieces, axis=0) for pieces in held)
    early_other, near_other = swap(early, 1), swap(near, 1)
    width = q_weight.shape[1]
    shapes = [((3 * quarter, width), F32)] + [(x.shape, x.dtype, pltpu.HBM) for x in outs]
    before, *outs = local_call(
        first_dots_kernel,
        shapes,
        "first_dots",
        *(early, early_other, near, q_weight, *outs),
        scratch=[pltpu.SemaphoreType.DMA((2,))],
    )
    kernel = functools.partial(last_dot_kernel, n)
    shapes = [((tokens, width), BF16)]
    (next_queries,) = local_call(kernel, shapes, "last_dot", near_other, before, q_weight)
    return (*outs, next_queries)


def solution(mesh):
    in_specs = (
        P(("replica", "tp"), None),
        P("replica", "tp"),
        P("replica", None),
        P("replica", None),
        P("tp", None),
        P(),
        P(None, "tp"),
    )
    out_specs = (P(("replica", "tp"), None), P(("replica", "tp"), None), P("replica", "tp"))
    return jax.shard_map(
        on_device, mesh=mesh, in_specs=in_specs, out_specs=out_specs, check_vma=False
    )
```

```python
import functools

import jax
import jax.numpy as jnp
from jax import lax
from jax.experimental import pallas as pl
from jax.experimental.pallas import tpu as pltpu
from jax.sharding import PartitionSpec as P

HD = 128
QB = 128
EPS = 1e-06
F32 = jnp.float32
BF16 = jnp.bfloat16
PIECES = 4
STEPS = 8
VMEM_LIMIT = 24 << 20
SMALL_LIMIT = 16 << 20


def late_levels(n):
    return [1 << b for b in range(3, n.bit_length() - 1)]


def owner_token(row, device, n):
    bits = [2, 6] + late_levels(n)
    distance = row >> (len(bits) + 1)
    which = (row >> len(bits)) & 1
    block = row ^ which
    for place, bit in enumerate(bits):
        distance = distance ^ (((block >> (len(bits) - 1 - place)) & 1) * bit)
    return ((device ^ distance) << 1) | which


def attend_kernel(
    n, queries, keys, values, weight, context, held, query, key, value, small, large
):
    device = lax.axis_index("tp")
    tokens = queries.shape[0]
    heads = queries.shape[1] // HD
    group = heads * n // (keys.shape[1] // HD)
    copies = [pltpu.make_async_copy(queries, query, small.at[0])]
    for h in range(heads):
        at = pl.ds(pl.multiple_of(lax.div(device * heads + h, group) * HD, HD), HD)
        copies.append(pltpu.make_async_copy(keys.at[:, at], key.at[h], small.at[1 + 2 * h]))
        copies.append(pltpu.make_async_copy(values.at[:, at], value.at[h], small.at[2 + 2 * h]))
    depth = held.shape[0] // PIECES
    late = []
    for c in range(PIECES):
        part = pl.ds(c * depth, depth)
        late.append(pltpu.make_async_copy(weight.at[part], held.at[part], large.at[c]))
    for copy in copies + late:
        copy.start()
    row = lax.broadcasted_iota(jnp.int32, (tokens, tokens), 0)
    col = lax.broadcasted_iota(jnp.int32, (tokens, tokens), 1)
    token = owner_token(row, device, n)
    pick = (token == col).astype(F32).astype(BF16)
    for copy in copies:
        copy.wait()
    ordered = jnp.dot(pick, query[...], preferred_element_type=F32).astype(BF16)
    for h in range(heads):
        scores = lax.dot_general(
            ordered[:, h * HD : (h + 1) * HD],
            key[h],
            (((1,), (1,)), ((), ())),
            preferred_element_type=F32,
        ) / jnp.sqrt(F32(HD))
        scores = jnp.where(col <= token, scores, F32(-1e30))
        weights = jnp.exp(scores - jnp.max(scores, axis=1, keepdims=True))
        probs = (weights / jnp.sum(weights, axis=1, keepdims=True)).astype(BF16)
        context[:, h * HD : (h + 1) * HD] = jnp.dot(
            probs, value[h], preferred_element_type=F32
        ).astype(BF16)
    for copy in late:
        copy.wait()


def in_hbm(*arrays):
    return [pltpu.with_memory_space_constraint(x, pltpu.HBM) for x in arrays]


def attend(n, queries, keys, values, weight):
    tokens = queries.shape[0]
    heads = queries.shape[1] // HD
    whole = pl.BlockSpec(memory_space=pltpu.VMEM)
    return pl.pallas_call(
        functools.partial(attend_kernel, n),
        out_shape=[
            jax.ShapeDtypeStruct(queries.shape, BF16),
            pltpu.VMEM(weight.shape, BF16),
        ],
        in_specs=[pl.BlockSpec(memory_space=pltpu.HBM)] * 4,
        out_specs=[whole] * 2,
        scratch_shapes=[
            pltpu.VMEM(queries.shape, BF16),
            pltpu.VMEM((heads, tokens, HD), BF16),
            pltpu.VMEM((heads, tokens, HD), BF16),
            pltpu.SemaphoreType.DMA((1 + 2 * heads,)),
            pltpu.SemaphoreType.DMA((PIECES,)),
        ],
        compiler_params=pltpu.CompilerParams(vmem_limit_bytes=VMEM_LIMIT),
        cost_estimate=pl.CostEstimate(
            flops=0, bytes_accessed=2 * weight.size, transcendentals=0
        ),
        name="attend",
    )(*in_hbm(queries, keys, values, weight))


def parts(ref):
    width = ref.shape[1] // STEPS
    return [pl.ds(c * width, width) for c in range(STEPS)]


def split_kernel(which, kept, got, own, *pieces):
    rows = got.shape[0]
    part = rows // 4
    for at in parts(got):
        total = kept[which * rows : (which + 1) * rows, at] + got[:, at].astype(F32)
        own[:, at] = total[:part]
        for k, piece in enumerate(pieces, 1):
            piece[:, at] = total[k * part : (k + 1) * part].astype(BF16)


def settle_kernel(which, own, old, *refs):
    *arrived, total, turned = refs
    for at in parts(own):
        value = own[:, at]
        for piece in arrived:
            value = value + piece[:, at].astype(F32)
        row = lax.broadcasted_iota(jnp.int32, value.shape, 0)
        value = value + jnp.where(row == which, old[:, at].astype(F32), F32(0))
        total[:, at] = value
        turned[:, at] = jnp.concatenate([value[1:], value[:1]], axis=0).astype(BF16)


def encode_kernel(total, arrived, gain, *refs):
    if len(refs) > 4:
        first, *before, normed, codes, scales, joint, decoded = refs
    else:
        before, (normed, codes, scales, decoded) = (), refs
    blocks = total.shape[1] // QB
    row = lax.broadcasted_iota(jnp.int32, (total.shape[0], QB), 0)
    lane = lax.broadcasted_iota(jnp.int32, (total.shape[0], blocks), 1)
    all_scales = jnp.zeros(scales.shape, F32)
    squares = jnp.zeros(row.shape, F32)
    for b in range(blocks):
        at = pl.ds(b * QB, QB)
        stream = total[:, at] + arrived[:, at].astype(F32)
        scale = jnp.max(jnp.abs(stream), axis=1, keepdims=True) + EPS
        code = (stream / scale).astype(BF16).astype(F32)
        value = code * scale
        squares += value * value
        decoded[:, at] = value
        if before:
            code = jnp.where(row == 0, before[0][:, at].astype(F32), code)
        codes[:, at] = code.astype(BF16)
        all_scales = jnp.where(lane == b, scale, all_scales)
    if before:
        all_scales = jnp.where(
            lax.broadcasted_iota(jnp.int32, scales.shape, 0) == 0, before[1][...], all_scales
        )
    scales[...] = all_scales
    mean_sq = jnp.sum(squares, axis=1, keepdims=True) / total.shape[1]
    factor = lax.rsqrt(mean_sq + 1e-05)
    for at in parts(total):
        value = decoded[:, at] * factor * gain[:, at]
        normed[:, at] = value.astype(BF16)
        if before:
            joint[:, at] = jnp.concatenate([first[:, at].astype(F32), value], axis=0).astype(BF16)


def times(rows, weight):
    depth = weight.shape[0] // STEPS
    count = sum(r.shape[0] for r in rows)
    total = jnp.zeros((count, weight.shape[1]), F32)
    for c in range(STEPS):
        part = pl.ds(c * depth, depth)
        block = jnp.concatenate([r[:, part] for r in rows], axis=0)
        total += jnp.dot(block, weight[part], preferred_element_type=F32)
    return total


def first_dots_kernel(*refs):
    *rows, weight, codes, scales, out, codes_out, scales_out, sems = refs
    copies = [
        pltpu.make_async_copy(codes, codes_out, sems.at[0]),
        pltpu.make_async_copy(scales, scales_out, sems.at[1]),
    ]
    for copy in copies:
        copy.start()
    out[...] = times(rows, weight)
    for copy in copies:
        copy.wait()


def last_dot_kernel(n, orders, *refs):
    *rows, before, weight, out = refs
    device = lax.axis_index("tp")
    tokens = out.shape[0]
    part = tokens // 16
    total = jnp.zeros(out.shape, F32)
    groups = [(0, 0), (1, 0), (0, 1), (1, 1)]
    start = 0
    for side, order in groups:
        count = len(orders[order]) * part
        if (side, order) == groups[-1]:
            values = times(rows, weight)
        else:
            values = before[start : start + count]
            start += count
        at = lax.broadcasted_iota(jnp.int32, (tokens, count), 1)
        row = at & (part - 1)
        for k, (which, place) in enumerate(orders[order]):
            here = (at >> (part.bit_length() - 1)) == k
            row = row + jnp.where(here, (8 * side + 4 * which + place) * part, 0)
        token = lax.broadcasted_iota(jnp.int32, (tokens, count), 0)
        pick = (owner_token(row, device, n) == token).astype(F32).astype(BF16)
        total += jnp.dot(pick, values.astype(BF16), preferred_element_type=F32)
    out[...] = total.astype(BF16)


def local_call(kernel, shapes, name, *operands, scratch=()):
    spec = pl.BlockSpec(memory_space=pltpu.VMEM)
    spaces = [space[0] if space else pltpu.VMEM for _, _, *space in shapes]
    return pl.pallas_call(
        kernel,
        out_shape=[
            (space[0] if space else jax.ShapeDtypeStruct)(shape, dtype)
            for shape, dtype, *space in shapes
        ],
        in_specs=[spec] * len(operands),
        out_specs=[pl.BlockSpec(memory_space=space) for space in spaces],
        scratch_shapes=list(scratch),
        compiler_params=pltpu.CompilerParams(vmem_limit_bytes=SMALL_LIMIT),
        cost_estimate=pl.CostEstimate(
            flops=0, bytes_accessed=sum(2 * x.size for x in operands), transcendentals=0
        ),
        name=name,
    )(*operands)


def on_device(residual, queries, key_rows, value_rows, out_weight, norm_gain, q_weight):
    n = lax.axis_size("tp")
    tokens = queries.shape[0]
    D = residual.shape[1]
    levels = late_levels(n)
    square = (6, 2, 4)

    def swap(x, distance):
        return lax.ppermute(x, "tp", [(i, i ^ distance) for i in range(n)])

    half, quarter = tokens // 2, tokens // 4
    part, pair = quarter // 4, (2, D)
    gain = norm_gain.reshape(1, D)
    context, weight = attend(n, queries, key_rows, value_rows, out_weight)
    sent = jnp.dot(context[half:], weight, preferred_element_type=F32).astype(BF16)
    got = [swap(sent[:quarter], 1), swap(sent[quarter:], 1)]
    kept = jnp.dot(context[:half], weight, preferred_element_type=F32)

    def reduce(which):
        shapes = [((part, D), F32)] + [((part, D), BF16)] * 3
        kernel = functools.partial(split_kernel, which)
        total, *pieces = local_call(kernel, shapes, f"split{which}", kept, got[which])
        arrived = [swap(piece, distance) for piece, distance in zip(pieces, square)]
        if len(levels) > 1:
            for piece in arrived:
                total = total + piece.astype(F32)
            arrived = []
        for level in levels[:-1]:
            rest = total.shape[0] // 2
            total = total[:rest] + swap(total[rest:].astype(BF16), level).astype(F32)
        kernel = functools.partial(settle_kernel, which)
        shapes = [(pair, F32), (pair, BF16)]
        return local_call(kernel, shapes, f"settle{which}", total, residual, *arrived)

    def widen(held):
        for level in levels[-2::-1]:
            held = jnp.concatenate([held, swap(held, level)], axis=0)
        return held

    sums = [reduce(which) for which in range(2)]
    sums = [(total, swap(turned, levels[-1])) for total, turned in sums]
    shapes = [(pair, BF16), (pair, BF16, pltpu.VMEM), ((2, D // QB), F32, pltpu.VMEM)]
    scratch = [pltpu.VMEM(pair, F32)]
    first = local_call(encode_kernel, shapes, "encode0", *sums[0], gain, scratch=scratch)
    shapes.append(((4, D), BF16))
    second = local_call(encode_kernel, shapes, "encode1", *sums[1], gain, *first, scratch=scratch)
    held = [widen(first[0]), widen(second[0])]
    joint = second[3] if len(levels) == 1 else jnp.concatenate(held, axis=0)
    diagonal, near, far = square
    early = [swap(held[0], near), swap(held[0], diagonal), held[0]]
    early = jnp.concatenate(early, axis=0)
    late = [swap(held[1], near), swap(joint, far), swap(held[1], diagonal), held[1]]
    late = jnp.concatenate(late, axis=0)
    orders = [(0, 2), (0, 1), (0, 0)], [(1, 2), (0, 3), (1, 3), (1, 1), (1, 0)]
    early_other = swap(early, 1)
    late, _ = lax.optimization_barrier((late, early_other))
    late_other = swap(late, 1)
    width = q_weight.shape[1]
    outs = second[1:3]
    shapes = [((half + 3 * part, width), F32)] + [(x.shape, x.dtype, pltpu.HBM) for x in outs]
    before, *outs = local_call(
        first_dots_kernel,
        shapes,
        "first_dots",
        *(early, early_other, late, q_weight, *outs),
        scratch=[pltpu.SemaphoreType.DMA((2,))],
    )
    kernel = functools.partial(last_dot_kernel, n, orders)
    shapes = [((tokens, width), BF16)]
    (next_queries,) = local_call(kernel, shapes, "last_dot", late_other, before, q_weight)
    return (*outs, next_queries)


def solution(mesh):
    in_specs = (
        P(("replica", "tp"), None),
        P("replica", "tp"),
        P("replica", None),
        P("replica", None),
        P("tp", None),
        P(),
        P(None, "tp"),
    )
    out_specs = (P(("replica", "tp"), None), P(("replica", "tp"), None), P("replica", "tp"))
    return jax.shard_map(
        on_device, mesh=mesh, in_specs=in_specs, out_specs=out_specs, check_vma=False
    )
```

```python
import functools

import jax
import jax.numpy as jnp
from jax import lax
from jax.experimental import pallas as pl
from jax.experimental.pallas import tpu as pltpu
from jax.sharding import PartitionSpec as P

HD = 128
QB = 128
EPS = 1e-06
F32 = jnp.float32
BF16 = jnp.bfloat16
PIECES = 4
STEPS = 8
VMEM_LIMIT = 24 << 20
SMALL_LIMIT = 16 << 20


def late_levels(n):
    return [1 << b for b in range(3, n.bit_length() - 1)]


def owner_token(row, device, n):
    bits = [2, 6] + late_levels(n)
    distance = row >> (len(bits) + 1)
    which = (row >> len(bits)) & 1
    block = row ^ which
    for place, bit in enumerate(bits):
        distance = distance ^ (((block >> (len(bits) - 1 - place)) & 1) * bit)
    return ((device ^ distance) << 1) | which


def attend_kernel(
    n, queries, keys, values, weight, context, held, query, key, value, small, large
):
    device = lax.axis_index("tp")
    tokens = queries.shape[0]
    heads = queries.shape[1] // HD
    group = heads * n // (keys.shape[1] // HD)
    copies = [pltpu.make_async_copy(queries, query, small.at[0])]
    for h in range(heads):
        at = pl.ds(pl.multiple_of(lax.div(device * heads + h, group) * HD, HD), HD)
        copies.append(pltpu.make_async_copy(keys.at[:, at], key.at[h], small.at[1 + 2 * h]))
        copies.append(pltpu.make_async_copy(values.at[:, at], value.at[h], small.at[2 + 2 * h]))
    depth = held.shape[0] // PIECES
    late = []
    for c in range(PIECES):
        part = pl.ds(c * depth, depth)
        late.append(pltpu.make_async_copy(weight.at[part], held.at[part], large.at[c]))
    for copy in copies + late:
        copy.start()
    row = lax.broadcasted_iota(jnp.int32, (tokens, tokens), 0)
    col = lax.broadcasted_iota(jnp.int32, (tokens, tokens), 1)
    token = owner_token(row, device, n)
    pick = (token == col).astype(F32).astype(BF16)
    for copy in copies:
        copy.wait()
    ordered = jnp.dot(pick, query[...], preferred_element_type=F32).astype(BF16)
    for h in range(heads):
        scores = lax.dot_general(
            ordered[:, h * HD : (h + 1) * HD],
            key[h],
            (((1,), (1,)), ((), ())),
            preferred_element_type=F32,
        ) / jnp.sqrt(F32(HD))
        scores = jnp.where(col <= token, scores, F32(-1e30))
        weights = jnp.exp(scores - jnp.max(scores, axis=1, keepdims=True))
        probs = (weights / jnp.sum(weights, axis=1, keepdims=True)).astype(BF16)
        context[:, h * HD : (h + 1) * HD] = jnp.dot(
            probs, value[h], preferred_element_type=F32
        ).astype(BF16)
    for copy in late:
        copy.wait()


def in_hbm(*arrays):
    return [pltpu.with_memory_space_constraint(x, pltpu.HBM) for x in arrays]


def attend(n, queries, keys, values, weight):
    tokens = queries.shape[0]
    heads = queries.shape[1] // HD
    whole = pl.BlockSpec(memory_space=pltpu.VMEM)
    return pl.pallas_call(
        functools.partial(attend_kernel, n),
        out_shape=[
            jax.ShapeDtypeStruct(queries.shape, BF16),
            pltpu.VMEM(weight.shape, BF16),
        ],
        in_specs=[pl.BlockSpec(memory_space=pltpu.HBM)] * 4,
        out_specs=[whole] * 2,
        scratch_shapes=[
            pltpu.VMEM(queries.shape, BF16),
            pltpu.VMEM((heads, tokens, HD), BF16),
            pltpu.VMEM((heads, tokens, HD), BF16),
            pltpu.SemaphoreType.DMA((1 + 2 * heads,)),
            pltpu.SemaphoreType.DMA((PIECES,)),
        ],
        compiler_params=pltpu.CompilerParams(vmem_limit_bytes=VMEM_LIMIT),
        cost_estimate=pl.CostEstimate(
            flops=0, bytes_accessed=2 * weight.size, transcendentals=0
        ),
        name="attend",
    )(*in_hbm(queries, keys, values, weight))


def parts(ref):
    width = ref.shape[1] // STEPS
    return [pl.ds(c * width, width) for c in range(STEPS)]


def split_kernel(which, kept, got, own, *pieces):
    rows = got.shape[0]
    part = rows // 4
    for at in parts(got):
        total = kept[which * rows : (which + 1) * rows, at] + got[:, at].astype(F32)
        own[:, at] = total[:part]
        for k, piece in enumerate(pieces, 1):
            piece[:, at] = total[k * part : (k + 1) * part].astype(BF16)


def settle_kernel(which, own, old, *refs):
    *arrived, total, turned = refs
    for at in parts(own):
        value = own[:, at]
        for piece in arrived:
            value = value + piece[:, at].astype(F32)
        row = lax.broadcasted_iota(jnp.int32, value.shape, 0)
        value = value + jnp.where(row == which, old[:, at].astype(F32), F32(0))
        total[:, at] = value
        turned[:, at] = jnp.concatenate([value[1:], value[:1]], axis=0).astype(BF16)


def encode_kernel(total, arrived, gain, *refs):
    if len(refs) > 4:
        first, *before, normed, codes, scales, joint, decoded = refs
    else:
        before, (normed, codes, scales, decoded) = (), refs
    blocks = total.shape[1] // QB
    row = lax.broadcasted_iota(jnp.int32, (total.shape[0], QB), 0)
    lane = lax.broadcasted_iota(jnp.int32, (total.shape[0], blocks), 1)
    all_scales = jnp.zeros(scales.shape, F32)
    squares = jnp.zeros(row.shape, F32)
    for b in range(blocks):
        at = pl.ds(b * QB, QB)
        stream = total[:, at] + arrived[:, at].astype(F32)
        scale = jnp.max(jnp.abs(stream), axis=1, keepdims=True) + EPS
        code = (stream / scale).astype(BF16).astype(F32)
        value = code * scale
        squares += value * value
        decoded[:, at] = value
        if before:
            code = jnp.where(row == 0, before[0][:, at].astype(F32), code)
        codes[:, at] = code.astype(BF16)
        all_scales = jnp.where(lane == b, scale, all_scales)
    if before:
        all_scales = jnp.where(
            lax.broadcasted_iota(jnp.int32, scales.shape, 0) == 0, before[1][...], all_scales
        )
    scales[...] = all_scales
    mean_sq = jnp.sum(squares, axis=1, keepdims=True) / total.shape[1]
    factor = lax.rsqrt(mean_sq + 1e-05)
    for at in parts(total):
        value = decoded[:, at] * factor * gain[:, at]
        normed[:, at] = value.astype(BF16)
        if before:
            joint[:, at] = jnp.concatenate([first[:, at].astype(F32), value], axis=0).astype(BF16)


def times(rows, weight):
    depth = weight.shape[0] // STEPS
    count = sum(r.shape[0] for r in rows)
    total = jnp.zeros((count, weight.shape[1]), F32)
    for c in range(STEPS):
        part = pl.ds(c * depth, depth)
        block = jnp.concatenate([r[:, part] for r in rows], axis=0)
        total += jnp.dot(block, weight[part], preferred_element_type=F32)
    return total


def first_dots_kernel(*refs):
    *rows, weight, codes, scales, out, codes_out, scales_out, sems = refs
    copies = [
        pltpu.make_async_copy(codes, codes_out, sems.at[0]),
        pltpu.make_async_copy(scales, scales_out, sems.at[1]),
    ]
    for copy in copies:
        copy.start()
    out[...] = times(rows, weight)
    for copy in copies:
        copy.wait()


def last_dot_kernel(n, orders, *refs):
    *rows, before, weight, out = refs
    device = lax.axis_index("tp")
    tokens = out.shape[0]
    part = tokens // 16
    total = jnp.zeros(out.shape, F32)
    groups = [(side, order) for order in range(len(orders)) for side in range(2)]
    start = 0
    for side, order in groups:
        count = len(orders[order]) * part
        if (side, order) == groups[-1]:
            values = times(rows, weight)
        else:
            values = before[start : start + count]
            start += count
        at = lax.broadcasted_iota(jnp.int32, (tokens, count), 1)
        row = at & (part - 1)
        for k, (which, place) in enumerate(orders[order]):
            here = (at >> (part.bit_length() - 1)) == k
            row = row + jnp.where(here, (8 * side + 4 * which + place) * part, 0)
        token = lax.broadcasted_iota(jnp.int32, (tokens, count), 0)
        pick = (owner_token(row, device, n) == token).astype(F32).astype(BF16)
        total += jnp.dot(pick, values.astype(BF16), preferred_element_type=F32)
    out[...] = total.astype(BF16)


def local_call(kernel, shapes, name, *operands, scratch=()):
    spec = pl.BlockSpec(memory_space=pltpu.VMEM)
    spaces = [space[0] if space else pltpu.VMEM for _, _, *space in shapes]
    return pl.pallas_call(
        kernel,
        out_shape=[
            (space[0] if space else jax.ShapeDtypeStruct)(shape, dtype)
            for shape, dtype, *space in shapes
        ],
        in_specs=[spec] * len(operands),
        out_specs=[pl.BlockSpec(memory_space=space) for space in spaces],
        scratch_shapes=list(scratch),
        compiler_params=pltpu.CompilerParams(vmem_limit_bytes=SMALL_LIMIT),
        cost_estimate=pl.CostEstimate(
            flops=0, bytes_accessed=sum(2 * x.size for x in operands), transcendentals=0
        ),
        name=name,
    )(*operands)


def on_device(residual, queries, key_rows, value_rows, out_weight, norm_gain, q_weight):
    n = lax.axis_size("tp")
    tokens = queries.shape[0]
    D = residual.shape[1]
    levels = late_levels(n)
    square = (6, 2, 4)

    def swap(x, distance):
        return lax.ppermute(x, "tp", [(i, i ^ distance) for i in range(n)])

    half, quarter = tokens // 2, tokens // 4
    part, pair = quarter // 4, (2, D)
    gain = norm_gain.reshape(1, D)
    context, weight = attend(n, queries, key_rows, value_rows, out_weight)
    sent = jnp.dot(context[half:], weight, preferred_element_type=F32).astype(BF16)
    got = [swap(sent[:quarter], 1), swap(sent[quarter:], 1)]
    kept = jnp.dot(context[:half], weight, preferred_element_type=F32)

    def reduce(which):
        shapes = [((part, D), F32)] + [((part, D), BF16)] * 3
        kernel = functools.partial(split_kernel, which)
        total, *pieces = local_call(kernel, shapes, f"split{which}", kept, got[which])
        arrived = [swap(piece, distance) for piece, distance in zip(pieces, square)]
        if len(levels) > 1:
            for piece in arrived:
                total = total + piece.astype(F32)
            arrived = []
        for level in levels[:-1]:
            rest = total.shape[0] // 2
            total = total[:rest] + swap(total[rest:].astype(BF16), level).astype(F32)
        kernel = functools.partial(settle_kernel, which)
        shapes = [(pair, F32), (pair, BF16)]
        return local_call(kernel, shapes, f"settle{which}", total, residual, *arrived)

    def widen(held):
        for level in levels[-2::-1]:
            held = jnp.concatenate([held, swap(held, level)], axis=0)
        return held

    sums = [reduce(which) for which in range(2)]
    sums = [(total, swap(turned, levels[-1])) for total, turned in sums]
    shapes = [(pair, BF16), (pair, BF16, pltpu.VMEM), ((2, D // QB), F32, pltpu.VMEM)]
    scratch = [pltpu.VMEM(pair, F32)]
    first = local_call(encode_kernel, shapes, "encode0", *sums[0], gain, scratch=scratch)
    shapes.append(((4, D), BF16))
    second = local_call(encode_kernel, shapes, "encode1", *sums[1], gain, *first, scratch=scratch)
    held = [widen(first[0]), widen(second[0])]
    joint = second[3] if len(levels) == 1 else jnp.concatenate(held, axis=0)
    diagonal, near, far = square
    early = [swap(held[0], near), swap(held[0], diagonal), held[0]]
    early = jnp.concatenate(early, axis=0)
    both = swap(joint, far)
    late = [swap(held[1], near), swap(held[1], diagonal), held[1]]
    late = jnp.concatenate(late, axis=0)
    early_other = swap(early, 1)
    late, _ = lax.optimization_barrier((late, early_other))
    both_other, late_other = swap(both, 1), swap(late, 1)
    orders = [(0, 2), (0, 1), (0, 0)], [(1, 2), (1, 1), (1, 0)], [(0, 3), (1, 3)]
    width = q_weight.shape[1]
    outs = second[1:3]
    shapes = [((half + 6 * part, width), F32)] + [(x.shape, x.dtype, pltpu.HBM) for x in outs]
    before, *outs = local_call(
        first_dots_kernel,
        shapes,
        "first_dots",
        *(early, early_other, late, late_other, both, q_weight, *outs),
        scratch=[pltpu.SemaphoreType.DMA((2,))],
    )
    kernel = functools.partial(last_dot_kernel, n, orders)
    shapes = [((tokens, width), BF16)]
    (next_queries,) = local_call(kernel, shapes, "last_dot", both_other, before, q_weight)
    return (*outs, next_queries)


def solution(mesh):
    in_specs = (
        P(("replica", "tp"), None),
        P("replica", "tp"),
        P("replica", None),
        P("replica", None),
        P("tp", None),
        P(),
        P(None, "tp"),
    )
    out_specs = (P(("replica", "tp"), None), P(("replica", "tp"), None), P("replica", "tp"))
    return jax.shard_map(
        on_device, mesh=mesh, in_specs=in_specs, out_specs=out_specs, check_vma=False
    )
```

```python
import functools

import jax
import jax.numpy as jnp
from jax import lax
from jax.experimental import pallas as pl
from jax.experimental.pallas import tpu as pltpu
from jax.sharding import PartitionSpec as P

HD = 128
QB = 128
EPS = 1e-06
F32 = jnp.float32
BF16 = jnp.bfloat16
PIECES = 16
STEPS = 8
VMEM_LIMIT = 24 << 20
SMALL_LIMIT = 16 << 20


def late_levels(n):
    return [1 << b for b in range(3, n.bit_length() - 1)]


def owner_token(row, device, n):
    bits = [2, 6] + late_levels(n)
    distance = row >> (len(bits) + 1)
    which = (row >> len(bits)) & 1
    block = row ^ which
    for place, bit in enumerate(bits):
        distance = distance ^ (((block >> (len(bits) - 1 - place)) & 1) * bit)
    return ((device ^ distance) << 1) | which


def attend_kernel(
    n, queries, keys, values, weight, context, held, query, key, value, small, large
):
    device = lax.axis_index("tp")
    tokens = queries.shape[0]
    heads = queries.shape[1] // HD
    group = heads * n // (keys.shape[1] // HD)
    copies = [pltpu.make_async_copy(queries, query, small.at[0])]
    for h in range(heads):
        at = pl.ds(pl.multiple_of(lax.div(device * heads + h, group) * HD, HD), HD)
        copies.append(pltpu.make_async_copy(keys.at[:, at], key.at[h], small.at[1 + 2 * h]))
        copies.append(pltpu.make_async_copy(values.at[:, at], value.at[h], small.at[2 + 2 * h]))
    depth = held.shape[0] // PIECES
    late = []
    for c in range(PIECES):
        part = pl.ds(c * depth, depth)
        late.append(pltpu.make_async_copy(weight.at[part], held.at[part], large.at[c]))
    for copy in copies + late:
        copy.start()
    row = lax.broadcasted_iota(jnp.int32, (tokens, tokens), 0)
    col = lax.broadcasted_iota(jnp.int32, (tokens, tokens), 1)
    token = owner_token(row, device, n)
    pick = (token == col).astype(F32).astype(BF16)
    for copy in copies:
        copy.wait()
    ordered = jnp.dot(pick, query[...], preferred_element_type=F32).astype(BF16)
    for h in range(heads):
        scores = lax.dot_general(
            ordered[:, h * HD : (h + 1) * HD],
            key[h],
            (((1,), (1,)), ((), ())),
            preferred_element_type=F32,
        ) / jnp.sqrt(F32(HD))
        scores = jnp.where(col <= token, scores, F32(-1e30))
        weights = jnp.exp(scores - jnp.max(scores, axis=1, keepdims=True))
        probs = (weights / jnp.sum(weights, axis=1, keepdims=True)).astype(BF16)
        context[:, h * HD : (h + 1) * HD] = jnp.dot(
            probs, value[h], preferred_element_type=F32
        ).astype(BF16)
    for copy in late:
        copy.wait()


def in_hbm(*arrays):
    return [pltpu.with_memory_space_constraint(x, pltpu.HBM) for x in arrays]


def attend(n, queries, keys, values, weight):
    tokens = queries.shape[0]
    heads = queries.shape[1] // HD
    whole = pl.BlockSpec(memory_space=pltpu.VMEM)
    return pl.pallas_call(
        functools.partial(attend_kernel, n),
        out_shape=[
            jax.ShapeDtypeStruct(queries.shape, BF16),
            pltpu.VMEM(weight.shape, BF16),
        ],
        in_specs=[pl.BlockSpec(memory_space=pltpu.HBM)] * 4,
        out_specs=[whole] * 2,
        scratch_shapes=[
            pltpu.VMEM(queries.shape, BF16),
            pltpu.VMEM((heads, tokens, HD), BF16),
            pltpu.VMEM((heads, tokens, HD), BF16),
            pltpu.SemaphoreType.DMA((1 + 2 * heads,)),
            pltpu.SemaphoreType.DMA((PIECES,)),
        ],
        compiler_params=pltpu.CompilerParams(vmem_limit_bytes=VMEM_LIMIT),
        cost_estimate=pl.CostEstimate(
            flops=0, bytes_accessed=2 * weight.size, transcendentals=0
        ),
        name="attend",
    )(*in_hbm(queries, keys, values, weight))


def parts(ref):
    width = ref.shape[1] // STEPS
    return [pl.ds(c * width, width) for c in range(STEPS)]


def split_kernel(which, kept, got, own, *pieces):
    rows = got.shape[0]
    part = rows // 4
    for at in parts(got):
        total = kept[which * rows : (which + 1) * rows, at] + got[:, at].astype(F32)
        own[:, at] = total[:part]
        for k, piece in enumerate(pieces, 1):
            piece[:, at] = total[k * part : (k + 1) * part].astype(BF16)


def settle_kernel(which, own, old, *refs):
    *arrived, total, turned = refs
    for at in parts(own):
        value = own[:, at]
        for piece in arrived:
            value = value + piece[:, at].astype(F32)
        row = lax.broadcasted_iota(jnp.int32, value.shape, 0)
        value = value + jnp.where(row == which, old[:, at].astype(F32), F32(0))
        total[:, at] = value
        turned[:, at] = jnp.concatenate([value[1:], value[:1]], axis=0).astype(BF16)


def encode_kernel(total, arrived, gain, *refs):
    if len(refs) > 4:
        first, *before, normed, codes, scales, joint, decoded = refs
    else:
        before, (normed, codes, scales, decoded) = (), refs
    blocks = total.shape[1] // QB
    row = lax.broadcasted_iota(jnp.int32, (total.shape[0], QB), 0)
    lane = lax.broadcasted_iota(jnp.int32, (total.shape[0], blocks), 1)
    all_scales = jnp.zeros(scales.shape, F32)
    squares = jnp.zeros(row.shape, F32)
    for b in range(blocks):
        at = pl.ds(b * QB, QB)
        stream = total[:, at] + arrived[:, at].astype(F32)
        scale = jnp.max(jnp.abs(stream), axis=1, keepdims=True) + EPS
        code = (stream / scale).astype(BF16).astype(F32)
        value = code * scale
        squares += value * value
        decoded[:, at] = value
        if before:
            code = jnp.where(row == 0, before[0][:, at].astype(F32), code)
        codes[:, at] = code.astype(BF16)
        all_scales = jnp.where(lane == b, scale, all_scales)
    if before:
        all_scales = jnp.where(
            lax.broadcasted_iota(jnp.int32, scales.shape, 0) == 0, before[1][...], all_scales
        )
    scales[...] = all_scales
    mean_sq = jnp.sum(squares, axis=1, keepdims=True) / total.shape[1]
    factor = lax.rsqrt(mean_sq + 1e-05)
    for at in parts(total):
        value = decoded[:, at] * factor * gain[:, at]
        normed[:, at] = value.astype(BF16)
        if before:
            joint[:, at] = jnp.concatenate([first[:, at].astype(F32), value], axis=0).astype(BF16)


def times(rows, weight):
    depth = weight.shape[0] // STEPS
    count = sum(r.shape[0] for r in rows)
    total = jnp.zeros((count, weight.shape[1]), F32)
    for c in range(STEPS):
        part = pl.ds(c * depth, depth)
        block = jnp.concatenate([r[:, part] for r in rows], axis=0)
        total += jnp.dot(block, weight[part], preferred_element_type=F32)
    return total


def placed(n, tokens, values, side, order):
    count = values.shape[0]
    part = count // len(order)
    at = lax.broadcasted_iota(jnp.int32, (tokens, count), 1)
    row = at & (part - 1)
    for k, (which, place) in enumerate(order):
        here = (at >> (part.bit_length() - 1)) == k
        row = row + jnp.where(here, (8 * side + 4 * which + place) * part, 0)
    token = lax.broadcasted_iota(jnp.int32, (tokens, count), 0)
    pick = (owner_token(row, lax.axis_index("tp"), n) == token).astype(F32).astype(BF16)
    return jnp.dot(pick, values.astype(BF16), preferred_element_type=F32)


def first_dots_kernel(n, groups, *refs):
    *rows, weight, codes, scales, out, codes_out, scales_out, sems = refs
    copies = [
        pltpu.make_async_copy(codes, codes_out, sems.at[0]),
        pltpu.make_async_copy(scales, scales_out, sems.at[1]),
    ]
    for copy in copies:
        copy.start()
    values = times(rows, weight)
    total = jnp.zeros(out.shape, F32)
    start = 0
    for ref, (side, order) in zip(rows, groups):
        stop = start + ref.shape[0]
        total += placed(n, out.shape[0], values[start:stop], side, order)
        start = stop
    out[...] = total
    for copy in copies:
        copy.wait()


def last_dot_kernel(n, group, rows, before, weight, out):
    values = times([rows], weight)
    out[...] = (before[...] + placed(n, out.shape[0], values, *group)).astype(BF16)


def local_call(kernel, shapes, name, *operands, scratch=()):
    spec = pl.BlockSpec(memory_space=pltpu.VMEM)
    spaces = [space[0] if space else pltpu.VMEM for _, _, *space in shapes]
    return pl.pallas_call(
        kernel,
        out_shape=[
            (space[0] if space else jax.ShapeDtypeStruct)(shape, dtype)
            for shape, dtype, *space in shapes
        ],
        in_specs=[spec] * len(operands),
        out_specs=[pl.BlockSpec(memory_space=space) for space in spaces],
        scratch_shapes=list(scratch),
        compiler_params=pltpu.CompilerParams(vmem_limit_bytes=SMALL_LIMIT),
        cost_estimate=pl.CostEstimate(
            flops=0, bytes_accessed=sum(2 * x.size for x in operands), transcendentals=0
        ),
        name=name,
    )(*operands)


def on_device(residual, queries, key_rows, value_rows, out_weight, norm_gain, q_weight):
    n = lax.axis_size("tp")
    tokens = queries.shape[0]
    D = residual.shape[1]
    levels = late_levels(n)
    square = (6, 2, 4)

    def swap(x, distance):
        return lax.ppermute(x, "tp", [(i, i ^ distance) for i in range(n)])

    half, quarter = tokens // 2, tokens // 4
    part, pair = quarter // 4, (2, D)
    gain = norm_gain.reshape(1, D)
    context, weight = attend(n, queries, key_rows, value_rows, out_weight)
    sent = jnp.dot(context[half:], weight, preferred_element_type=F32).astype(BF16)
    got = [swap(sent[:quarter], 1), swap(sent[quarter:], 1)]
    kept = jnp.dot(context[:half], weight, preferred_element_type=F32)

    def reduce(which):
        shapes = [((part, D), F32)] + [((part, D), BF16)] * 3
        kernel = functools.partial(split_kernel, which)
        total, *pieces = local_call(kernel, shapes, f"split{which}", kept, got[which])
        arrived = [swap(piece, distance) for piece, distance in zip(pieces, square)]
        if len(levels) > 1:
            for piece in arrived:
                total = total + piece.astype(F32)
            arrived = []
        for level in levels[:-1]:
            rest = total.shape[0] // 2
            total = total[:rest] + swap(total[rest:].astype(BF16), level).astype(F32)
        kernel = functools.partial(settle_kernel, which)
        shapes = [(pair, F32), (pair, BF16)]
        return local_call(kernel, shapes, f"settle{which}", total, residual, *arrived)

    def widen(held):
        for level in levels[-2::-1]:
            held = jnp.concatenate([held, swap(held, level)], axis=0)
        return held

    sums = [reduce(which) for which in range(2)]
    sums = [(total, swap(turned, levels[-1])) for total, turned in sums]
    shapes = [(pair, BF16), (pair, BF16, pltpu.VMEM), ((2, D // QB), F32, pltpu.VMEM)]
    scratch = [pltpu.VMEM(pair, F32)]
    first = local_call(encode_kernel, shapes, "encode0", *sums[0], gain, scratch=scratch)
    shapes.append(((4, D), BF16))
    second = local_call(encode_kernel, shapes, "encode1", *sums[1], gain, *first, scratch=scratch)
    held = [widen(first[0]), widen(second[0])]
    joint = second[3] if len(levels) == 1 else jnp.concatenate(held, axis=0)
    diagonal, near, far = square
    early = [swap(held[0], near), swap(held[0], diagonal), held[0]]
    early = jnp.concatenate(early, axis=0)
    both = swap(joint, far)
    late = [swap(held[1], near), swap(held[1], diagonal), held[1]]
    late = jnp.concatenate(late, axis=0)
    early_other = swap(early, 1)
    late, _ = lax.optimization_barrier((late, early_other))
    both_other, late_other = swap(both, 1), swap(late, 1)
    orders = [(0, 2), (0, 1), (0, 0)], [(1, 2), (1, 1), (1, 0)], [(0, 3), (1, 3)]
    groups = [(side, order) for order in orders for side in range(2)]
    shape = (tokens, q_weight.shape[1])
    outs = second[1:3]
    shapes = [(shape, F32)] + [(x.shape, x.dtype, pltpu.HBM) for x in outs]
    before, *outs = local_call(
        functools.partial(first_dots_kernel, n, groups[:-1]),
        shapes,
        "first_dots",
        *(early, early_other, late, late_other, both, q_weight, *outs),
        scratch=[pltpu.SemaphoreType.DMA((2,))],
    )
    kernel = functools.partial(last_dot_kernel, n, groups[-1])
    (next_queries,) = local_call(
        kernel, [(shape, BF16)], "last_dot", both_other, before, q_weight
    )
    return (*outs, next_queries)


def solution(mesh):
    in_specs = (
        P(("replica", "tp"), None),
        P("replica", "tp"),
        P("replica", None),
        P("replica", None),
        P("tp", None),
        P(),
        P(None, "tp"),
    )
    out_specs = (P(("replica", "tp"), None), P(("replica", "tp"), None), P("replica", "tp"))
    return jax.shard_map(
        on_device, mesh=mesh, in_specs=in_specs, out_specs=out_specs, check_vma=False
    )
```

```python
import functools

import jax
import jax.numpy as jnp
from jax import lax
from jax.experimental import pallas as pl
from jax.experimental.pallas import tpu as pltpu
from jax.sharding import PartitionSpec as P

HD = 128
QB = 128
EPS = 1e-06
F32 = jnp.float32
BF16 = jnp.bfloat16
PIECES = 4
STEPS = 8
VMEM_LIMIT = 24 << 20
SMALL_LIMIT = 16 << 20


def late_levels(n):
    return [1 << b for b in range(3, n.bit_length() - 1)]


def owner_token(row, device, n):
    bits = [2, 6] + late_levels(n)
    distance = row >> (len(bits) + 1)
    which = (row >> len(bits)) & 1
    block = row ^ which
    for place, bit in enumerate(bits):
        distance = distance ^ (((block >> (len(bits) - 1 - place)) & 1) * bit)
    return ((device ^ distance) << 1) | which


def attend_kernel(
    n, queries, keys, values, weight, context, held, query, key, value, small, large
):
    device = lax.axis_index("tp")
    tokens = queries.shape[0]
    heads = queries.shape[1] // HD
    group = heads * n // (keys.shape[1] // HD)
    copies = [pltpu.make_async_copy(queries, query, small.at[0])]
    for h in range(heads):
        at = pl.ds(pl.multiple_of(lax.div(device * heads + h, group) * HD, HD), HD)
        copies.append(pltpu.make_async_copy(keys.at[:, at], key.at[h], small.at[1 + 2 * h]))
        copies.append(pltpu.make_async_copy(values.at[:, at], value.at[h], small.at[2 + 2 * h]))
    depth = held.shape[0] // PIECES
    late = []
    for c in range(PIECES):
        part = pl.ds(c * depth, depth)
        late.append(pltpu.make_async_copy(weight.at[part], held.at[part], large.at[c]))
    for copy in copies + late:
        copy.start()
    row = lax.broadcasted_iota(jnp.int32, (tokens, tokens), 0)
    col = lax.broadcasted_iota(jnp.int32, (tokens, tokens), 1)
    token = owner_token(row, device, n)
    pick = (token == col).astype(F32).astype(BF16)
    for copy in copies:
        copy.wait()
    ordered = jnp.dot(pick, query[...], preferred_element_type=F32).astype(BF16)
    for h in range(heads):
        scores = lax.dot_general(
            ordered[:, h * HD : (h + 1) * HD],
            key[h],
            (((1,), (1,)), ((), ())),
            preferred_element_type=F32,
        ) / jnp.sqrt(F32(HD))
        scores = jnp.where(col <= token, scores, F32(-1e30))
        weights = jnp.exp(scores - jnp.max(scores, axis=1, keepdims=True))
        probs = (weights / jnp.sum(weights, axis=1, keepdims=True)).astype(BF16)
        context[:, h * HD : (h + 1) * HD] = jnp.dot(
            probs, value[h], preferred_element_type=F32
        ).astype(BF16)
    for copy in late:
        copy.wait()


def in_hbm(*arrays):
    return [pltpu.with_memory_space_constraint(x, pltpu.HBM) for x in arrays]


def attend(n, queries, keys, values, weight):
    tokens = queries.shape[0]
    heads = queries.shape[1] // HD
    whole = pl.BlockSpec(memory_space=pltpu.VMEM)
    return pl.pallas_call(
        functools.partial(attend_kernel, n),
        out_shape=[
            jax.ShapeDtypeStruct(queries.shape, BF16),
            pltpu.VMEM(weight.shape, BF16),
        ],
        in_specs=[pl.BlockSpec(memory_space=pltpu.HBM)] * 4,
        out_specs=[whole] * 2,
        scratch_shapes=[
            pltpu.VMEM(queries.shape, BF16),
            pltpu.VMEM((heads, tokens, HD), BF16),
            pltpu.VMEM((heads, tokens, HD), BF16),
            pltpu.SemaphoreType.DMA((1 + 2 * heads,)),
            pltpu.SemaphoreType.DMA((PIECES,)),
        ],
        compiler_params=pltpu.CompilerParams(vmem_limit_bytes=VMEM_LIMIT),
        cost_estimate=pl.CostEstimate(
            flops=0, bytes_accessed=2 * weight.size, transcendentals=0
        ),
        name="attend",
    )(*in_hbm(queries, keys, values, weight))


def parts(ref):
    width = ref.shape[1] // STEPS
    return [pl.ds(c * width, width) for c in range(STEPS)]


def split_kernel(which, kept, got, own, *pieces):
    rows = got.shape[0]
    part = rows // 4
    for at in parts(got):
        total = kept[which * rows : (which + 1) * rows, at] + got[:, at].astype(F32)
        own[:, at] = total[:part]
        for k, piece in enumerate(pieces, 1):
            piece[:, at] = total[k * part : (k + 1) * part].astype(BF16)


def settle_kernel(which, own, old, *refs):
    *arrived, total, turned = refs
    for at in parts(own):
        value = own[:, at]
        for piece in arrived:
            value = value + piece[:, at].astype(F32)
        row = lax.broadcasted_iota(jnp.int32, value.shape, 0)
        value = value + jnp.where(row == which, old[:, at].astype(F32), F32(0))
        total[:, at] = value
        turned[:, at] = jnp.concatenate([value[1:], value[:1]], axis=0).astype(BF16)


def encode_kernel(total, arrived, gain, *refs):
    if len(refs) > 4:
        _, *before, normed, codes, scales, decoded = refs
    else:
        before, (normed, codes, scales, decoded) = (), refs
    blocks = total.shape[1] // QB
    row = lax.broadcasted_iota(jnp.int32, (total.shape[0], QB), 0)
    lane = lax.broadcasted_iota(jnp.int32, (total.shape[0], blocks), 1)
    all_scales = jnp.zeros(scales.shape, F32)
    squares = jnp.zeros(row.shape, F32)
    for b in range(blocks):
        at = pl.ds(b * QB, QB)
        stream = total[:, at] + arrived[:, at].astype(F32)
        scale = jnp.max(jnp.abs(stream), axis=1, keepdims=True) + EPS
        code = (stream / scale).astype(BF16).astype(F32)
        value = code * scale
        squares += value * value
        decoded[:, at] = value
        if before:
            code = jnp.where(row == 0, before[0][:, at].astype(F32), code)
        codes[:, at] = code.astype(BF16)
        all_scales = jnp.where(lane == b, scale, all_scales)
    if before:
        all_scales = jnp.where(
            lax.broadcasted_iota(jnp.int32, scales.shape, 0) == 0, before[1][...], all_scales
        )
    scales[...] = all_scales
    mean_sq = jnp.sum(squares, axis=1, keepdims=True) / total.shape[1]
    factor = lax.rsqrt(mean_sq + 1e-05)
    for at in parts(total):
        normed[:, at] = (decoded[:, at] * factor * gain[:, at]).astype(BF16)


def times(rows, weight):
    depth = weight.shape[0] // STEPS
    count = sum(r[0].shape[0] if isinstance(r, tuple) else r.shape[0] for r in rows)
    total = jnp.zeros((count, weight.shape[1]), F32)
    odd = (lax.axis_index("tp") & 1) == 1
    for c in range(STEPS):
        part = pl.ds(c * depth, depth)
        block = [
            jnp.where(odd, r[0][:, part], r[1][:, part]) if isinstance(r, tuple) else r[:, part]
            for r in rows
        ]
        block = jnp.concatenate(block, axis=0)
        total += jnp.dot(block, weight[part], preferred_element_type=F32)
    return total


def placed(n, tokens, values, side, order):
    count = values.shape[0]
    part = count // len(order)
    at = lax.broadcasted_iota(jnp.int32, (tokens, count), 1)
    row = at & (part - 1)
    for k, (which, place) in enumerate(order):
        here = (at >> (part.bit_length() - 1)) == k
        row = row + jnp.where(here, (8 * side + 4 * which + place) * part, 0)
    token = lax.broadcasted_iota(jnp.int32, (tokens, count), 0)
    pick = (owner_token(row, lax.axis_index("tp"), n) == token).astype(F32).astype(BF16)
    return jnp.dot(pick, values.astype(BF16), preferred_element_type=F32)


def first_dots_kernel(n, groups, *refs):
    *rows, weight, codes, scales, out, codes_out, scales_out, sems = refs
    copies = [
        pltpu.make_async_copy(codes, codes_out, sems.at[0]),
        pltpu.make_async_copy(scales, scales_out, sems.at[1]),
    ]
    for copy in copies:
        copy.start()
    *rows, a, b, c, d = rows
    rows += [(a, b), (c, d)]
    values = times(rows, weight)
    total = jnp.zeros(out.shape, F32)
    start = 0
    for ref, (side, order) in zip(rows, groups):
        stop = start + (ref[0] if isinstance(ref, tuple) else ref).shape[0]
        total += placed(n, out.shape[0], values[start:stop], side, order)
        start = stop
    out[...] = total
    for copy in copies:
        copy.wait()


def last_dot_kernel(n, group, rows, before, weight, out):
    values = times([rows], weight)
    out[...] = (before[...] + placed(n, out.shape[0], values, *group)).astype(BF16)


def local_call(kernel, shapes, name, *operands, scratch=()):
    spec = pl.BlockSpec(memory_space=pltpu.VMEM)
    spaces = [space[0] if space else pltpu.VMEM for _, _, *space in shapes]
    return pl.pallas_call(
        kernel,
        out_shape=[
            (space[0] if space else jax.ShapeDtypeStruct)(shape, dtype)
            for shape, dtype, *space in shapes
        ],
        in_specs=[spec] * len(operands),
        out_specs=[pl.BlockSpec(memory_space=space) for space in spaces],
        scratch_shapes=list(scratch),
        compiler_params=pltpu.CompilerParams(vmem_limit_bytes=SMALL_LIMIT),
        cost_estimate=pl.CostEstimate(
            flops=0, bytes_accessed=sum(2 * x.size for x in operands), transcendentals=0
        ),
        name=name,
    )(*operands)


def on_device(residual, queries, key_rows, value_rows, out_weight, norm_gain, q_weight):
    n = lax.axis_size("tp")
    tokens = queries.shape[0]
    D = residual.shape[1]
    levels = late_levels(n)
    square = (6, 2, 4)

    def swap(x, distance):
        return lax.ppermute(x, "tp", [(i, i ^ distance) for i in range(n)])

    def send(x, core, distance):
        return lax.ppermute(x, "tp", [(i, i ^ distance) for i in range(core, n, 2)])

    half, quarter = tokens // 2, tokens // 4
    part, pair = quarter // 4, (2, D)
    gain = norm_gain.reshape(1, D)
    context, weight = attend(n, queries, key_rows, value_rows, out_weight)
    sent = jnp.dot(context[half:], weight, preferred_element_type=F32).astype(BF16)
    got = [swap(sent[:quarter], 1), swap(sent[quarter:], 1)]
    kept = jnp.dot(context[:half], weight, preferred_element_type=F32)

    def reduce(which):
        shapes = [((part, D), F32)] + [((part, D), BF16)] * 3
        kernel = functools.partial(split_kernel, which)
        total, *pieces = local_call(kernel, shapes, f"split{which}", kept, got[which])
        arrived = [swap(piece, distance) for piece, distance in zip(pieces, square)]
        if len(levels) > 1:
            for piece in arrived:
                total = total + piece.astype(F32)
            arrived = []
        for level in levels[:-1]:
            rest = total.shape[0] // 2
            total = total[:rest] + swap(total[rest:].astype(BF16), level).astype(F32)
        kernel = functools.partial(settle_kernel, which)
        shapes = [(pair, F32), (pair, BF16)]
        return local_call(kernel, shapes, f"settle{which}", total, residual, *arrived)

    def widen(held):
        for level in levels[-2::-1]:
            held = jnp.concatenate([held, swap(held, level)], axis=0)
        return held

    sums = [reduce(which) for which in range(2)]
    sums = [(total, swap(turned, levels[-1])) for total, turned in sums]
    shapes = [(pair, BF16), (pair, BF16, pltpu.VMEM), ((2, D // QB), F32, pltpu.VMEM)]
    scratch = [pltpu.VMEM(pair, F32)]
    first = local_call(encode_kernel, shapes, "encode0", *sums[0], gain, scratch=scratch)
    second = local_call(encode_kernel, shapes, "encode1", *sums[1], gain, *first, scratch=scratch)
    held = [widen(first[0]), widen(second[0])]
    diagonal, near, far = square
    lent = send(held[0], 0, 1)
    far_mine, far_other = send(held[0], 1, far), send(lent, 1, far)
    back_other, back_mine = send(far_mine, 1, 1), send(far_other, 1, 1)
    early = [swap(held[0], near), swap(held[0], diagonal), held[0]]
    early = jnp.concatenate(early, axis=0)
    late = [swap(held[1], d) for d in square][::-1] + [held[1]]
    late = jnp.concatenate(late, axis=0)
    early_other = swap(early, 1)
    late, *_ = lax.optimization_barrier((late, early_other, back_mine, back_other))
    late_other = swap(late, 1)
    first_rows, far_rows = [(0, 2), (0, 1), (0, 0)], [(0, 3)]
    last_rows = [(1, 3), (1, 2), (1, 1), (1, 0)]
    groups = [(0, first_rows), (1, first_rows), (0, last_rows), (0, far_rows), (1, far_rows)]
    shape = (tokens, q_weight.shape[1])
    outs = second[1:3]
    shapes = [(shape, F32)] + [(x.shape, x.dtype, pltpu.HBM) for x in outs]
    before, *outs = local_call(
        functools.partial(first_dots_kernel, n, groups),
        shapes,
        "first_dots",
        *(early, early_other, late, far_mine, back_mine, far_other, back_other, q_weight, *outs),
        scratch=[pltpu.SemaphoreType.DMA((2,))],
    )
    kernel = functools.partial(last_dot_kernel, n, (1, last_rows))
    (next_queries,) = local_call(
        kernel, [(shape, BF16)], "last_dot", late_other, before, q_weight
    )
    return (*outs, next_queries)


def solution(mesh):
    in_specs = (
        P(("replica", "tp"), None),
        P("replica", "tp"),
        P("replica", None),
        P("replica", None),
        P("tp", None),
        P(),
        P(None, "tp"),
    )
    out_specs = (P(("replica", "tp"), None), P(("replica", "tp"), None), P("replica", "tp"))
    return jax.shard_map(
        on_device, mesh=mesh, in_specs=in_specs, out_specs=out_specs, check_vma=False
    )
```

```python
import functools

import jax
import jax.numpy as jnp
from jax import lax
from jax.experimental import pallas as pl
from jax.experimental.pallas import tpu as pltpu
from jax.sharding import PartitionSpec as P

HD = 128
QB = 128
EPS = 1e-06
F32 = jnp.float32
BF16 = jnp.bfloat16
PIECES = 4
STEPS = 8
VMEM_LIMIT = 24 << 20
SMALL_LIMIT = 16 << 20


def late_levels(n):
    return [1 << b for b in range(3, n.bit_length() - 1)]


def owner_token(row, device, n):
    bits = [2, 6] + late_levels(n)
    distance = row >> (len(bits) + 1)
    which = (row >> len(bits)) & 1
    block = row ^ which
    for place, bit in enumerate(bits):
        distance = distance ^ (((block >> (len(bits) - 1 - place)) & 1) * bit)
    return ((device ^ distance) << 1) | which


def attend_kernel(
    n, queries, keys, values, weight, context, held, query, key, value, small, large
):
    device = lax.axis_index("tp")
    tokens = queries.shape[0]
    heads = queries.shape[1] // HD
    group = heads * n // (keys.shape[1] // HD)
    copies = [pltpu.make_async_copy(queries, query, small.at[0])]
    for h in range(heads):
        at = pl.ds(pl.multiple_of(lax.div(device * heads + h, group) * HD, HD), HD)
        copies.append(pltpu.make_async_copy(keys.at[:, at], key.at[h], small.at[1 + 2 * h]))
        copies.append(pltpu.make_async_copy(values.at[:, at], value.at[h], small.at[2 + 2 * h]))
    depth = held.shape[0] // PIECES
    late = []
    for c in range(PIECES):
        part = pl.ds(c * depth, depth)
        late.append(pltpu.make_async_copy(weight.at[part], held.at[part], large.at[c]))
    for copy in copies + late:
        copy.start()
    row = lax.broadcasted_iota(jnp.int32, (tokens, tokens), 0)
    col = lax.broadcasted_iota(jnp.int32, (tokens, tokens), 1)
    token = owner_token(row, device, n)
    pick = (token == col).astype(F32).astype(BF16)
    for copy in copies:
        copy.wait()
    ordered = jnp.dot(pick, query[...], preferred_element_type=F32).astype(BF16)
    for h in range(heads):
        scores = lax.dot_general(
            ordered[:, h * HD : (h + 1) * HD],
            key[h],
            (((1,), (1,)), ((), ())),
            preferred_element_type=F32,
        ) / jnp.sqrt(F32(HD))
        scores = jnp.where(col <= token, scores, F32(-1e30))
        weights = jnp.exp(scores - jnp.max(scores, axis=1, keepdims=True))
        probs = (weights / jnp.sum(weights, axis=1, keepdims=True)).astype(BF16)
        context[:, h * HD : (h + 1) * HD] = jnp.dot(
            probs, value[h], preferred_element_type=F32
        ).astype(BF16)
    for copy in late:
        copy.wait()


def in_hbm(*arrays):
    return [pltpu.with_memory_space_constraint(x, pltpu.HBM) for x in arrays]


def attend(n, queries, keys, values, weight):
    tokens = queries.shape[0]
    heads = queries.shape[1] // HD
    whole = pl.BlockSpec(memory_space=pltpu.VMEM)
    return pl.pallas_call(
        functools.partial(attend_kernel, n),
        out_shape=[
            jax.ShapeDtypeStruct(queries.shape, BF16),
            pltpu.VMEM(weight.shape, BF16),
        ],
        in_specs=[pl.BlockSpec(memory_space=pltpu.HBM)] * 4,
        out_specs=[whole] * 2,
        scratch_shapes=[
            pltpu.VMEM(queries.shape, BF16),
            pltpu.VMEM((heads, tokens, HD), BF16),
            pltpu.VMEM((heads, tokens, HD), BF16),
            pltpu.SemaphoreType.DMA((1 + 2 * heads,)),
            pltpu.SemaphoreType.DMA((PIECES,)),
        ],
        compiler_params=pltpu.CompilerParams(vmem_limit_bytes=VMEM_LIMIT),
        cost_estimate=pl.CostEstimate(
            flops=0, bytes_accessed=2 * weight.size, transcendentals=0
        ),
        name="attend",
    )(*in_hbm(queries, keys, values, weight))


def parts(ref):
    width = ref.shape[1] // STEPS
    return [pl.ds(c * width, width) for c in range(STEPS)]


def split_kernel(which, kept, got, own, *pieces):
    rows = got.shape[0]
    part = rows // 4
    for at in parts(got):
        total = kept[which * rows : (which + 1) * rows, at] + got[:, at].astype(F32)
        own[:, at] = total[:part]
        for k, piece in enumerate(pieces, 1):
            piece[:, at] = total[k * part : (k + 1) * part].astype(BF16)


def settle_kernel(which, own, old, *refs):
    *arrived, total, turned = refs
    for at in parts(own):
        value = own[:, at]
        for piece in arrived:
            value = value + piece[:, at].astype(F32)
        row = lax.broadcasted_iota(jnp.int32, value.shape, 0)
        value = value + jnp.where(row == which, old[:, at].astype(F32), F32(0))
        total[:, at] = value
        turned[:, at] = jnp.concatenate([value[1:], value[:1]], axis=0).astype(BF16)


def encode_kernel(total, arrived, gain, *refs):
    if len(refs) > 4:
        first, *before, normed, codes, scales, joint, decoded = refs
    else:
        before, (normed, codes, scales, decoded) = (), refs
    blocks = total.shape[1] // QB
    row = lax.broadcasted_iota(jnp.int32, (total.shape[0], QB), 0)
    lane = lax.broadcasted_iota(jnp.int32, (total.shape[0], blocks), 1)
    all_scales = jnp.zeros(scales.shape, F32)
    squares = jnp.zeros(row.shape, F32)
    for b in range(blocks):
        at = pl.ds(b * QB, QB)
        stream = total[:, at] + arrived[:, at].astype(F32)
        scale = jnp.max(jnp.abs(stream), axis=1, keepdims=True) + EPS
        code = (stream / scale).astype(BF16).astype(F32)
        value = code * scale
        squares += value * value
        decoded[:, at] = value
        if before:
            code = jnp.where(row == 0, before[0][:, at].astype(F32), code)
        codes[:, at] = code.astype(BF16)
        all_scales = jnp.where(lane == b, scale, all_scales)
    if before:
        all_scales = jnp.where(
            lax.broadcasted_iota(jnp.int32, scales.shape, 0) == 0, before[1][...], all_scales
        )
    scales[...] = all_scales
    mean_sq = jnp.sum(squares, axis=1, keepdims=True) / total.shape[1]
    factor = lax.rsqrt(mean_sq + 1e-05)
    for at in parts(total):
        value = decoded[:, at] * factor * gain[:, at]
        normed[:, at] = value.astype(BF16)
        if before:
            joint[:, at] = jnp.concatenate([first[:, at].astype(F32), value], axis=0).astype(BF16)


def times(rows, weight):
    depth = weight.shape[0] // STEPS
    count = sum(r.shape[0] for r in rows)
    total = jnp.zeros((count, weight.shape[1]), F32)
    for c in range(STEPS):
        part = pl.ds(c * depth, depth)
        block = jnp.concatenate([r[:, part] for r in rows], axis=0)
        total += jnp.dot(block, weight[part], preferred_element_type=F32)
    return total


def placed(n, tokens, values, side, order):
    count = values.shape[0]
    part = count // len(order)
    at = lax.broadcasted_iota(jnp.int32, (tokens, count), 1)
    row = at & (part - 1)
    for k, (which, place) in enumerate(order):
        here = (at >> (part.bit_length() - 1)) == k
        row = row + jnp.where(here, (8 * side + 4 * which + place) * part, 0)
    token = lax.broadcasted_iota(jnp.int32, (tokens, count), 0)
    pick = (owner_token(row, lax.axis_index("tp"), n) == token).astype(F32).astype(BF16)
    return jnp.dot(pick, values.astype(BF16), preferred_element_type=F32)


def first_dots_kernel(n, groups, *refs):
    *rows, weight, codes, scales, out, codes_out, scales_out, sems = refs
    copies = [
        pltpu.make_async_copy(codes, codes_out, sems.at[0]),
        pltpu.make_async_copy(scales, scales_out, sems.at[1]),
    ]
    for copy in copies:
        copy.start()
    values = times(rows, weight)
    total = jnp.zeros(out.shape, F32)
    start = 0
    for ref, (side, order) in zip(rows, groups):
        stop = start + ref.shape[0]
        total += placed(n, out.shape[0], values[start:stop], side, order)
        start = stop
    out[...] = total
    for copy in copies:
        copy.wait()


def last_dot_kernel(n, group, rows, before, weight, out):
    values = times([rows], weight)
    out[...] = (before[...] + placed(n, out.shape[0], values, *group)).astype(BF16)


def local_call(kernel, shapes, name, *operands, scratch=()):
    spec = pl.BlockSpec(memory_space=pltpu.VMEM)
    spaces = [space[0] if space else pltpu.VMEM for _, _, *space in shapes]
    return pl.pallas_call(
        kernel,
        out_shape=[
            (space[0] if space else jax.ShapeDtypeStruct)(shape, dtype)
            for shape, dtype, *space in shapes
        ],
        in_specs=[spec] * len(operands),
        out_specs=[pl.BlockSpec(memory_space=space) for space in spaces],
        scratch_shapes=list(scratch),
        compiler_params=pltpu.CompilerParams(vmem_limit_bytes=SMALL_LIMIT),
        cost_estimate=pl.CostEstimate(
            flops=0, bytes_accessed=sum(2 * x.size for x in operands), transcendentals=0
        ),
        name=name,
    )(*operands)


def on_device(residual, queries, key_rows, value_rows, out_weight, norm_gain, q_weight):
    n = lax.axis_size("tp")
    tokens = queries.shape[0]
    D = residual.shape[1]
    levels = late_levels(n)
    square = (6, 2, 4)

    def swap(x, distance):
        return lax.ppermute(x, "tp", [(i, i ^ distance) for i in range(n)])

    half, quarter = tokens // 2, tokens // 4
    part, pair = quarter // 4, (2, D)
    gain = norm_gain.reshape(1, D)
    context, weight = attend(n, queries, key_rows, value_rows, out_weight)
    sent = jnp.dot(context[half:], weight, preferred_element_type=F32).astype(BF16)
    kept = jnp.dot(context[:half], weight, preferred_element_type=F32)
    got = [swap(sent[:quarter], 1)]
    kept, sent = lax.optimization_barrier((kept, sent))
    got.append(swap(sent[quarter:], 1))

    def reduce(which):
        shapes = [((part, D), F32)] + [((part, D), BF16)] * 3
        kernel = functools.partial(split_kernel, which)
        total, *pieces = local_call(kernel, shapes, f"split{which}", kept, got[which])
        arrived = [swap(piece, distance) for piece, distance in zip(pieces, square)]
        if len(levels) > 1:
            for piece in arrived:
                total = total + piece.astype(F32)
            arrived = []
        for level in levels[:-1]:
            rest = total.shape[0] // 2
            total = total[:rest] + swap(total[rest:].astype(BF16), level).astype(F32)
        kernel = functools.partial(settle_kernel, which)
        shapes = [(pair, F32), (pair, BF16)]
        return local_call(kernel, shapes, f"settle{which}", total, residual, *arrived)

    def widen(held):
        for level in levels[-2::-1]:
            held = jnp.concatenate([held, swap(held, level)], axis=0)
        return held

    sums = [reduce(which) for which in range(2)]
    sums = [(total, swap(turned, levels[-1])) for total, turned in sums]
    shapes = [(pair, BF16), (pair, BF16, pltpu.VMEM), ((2, D // QB), F32, pltpu.VMEM)]
    scratch = [pltpu.VMEM(pair, F32)]
    first = local_call(encode_kernel, shapes, "encode0", *sums[0], gain, scratch=scratch)
    shapes.append(((4, D), BF16))
    second = local_call(encode_kernel, shapes, "encode1", *sums[1], gain, *first, scratch=scratch)
    held = [widen(first[0]), widen(second[0])]
    joint = second[3] if len(levels) == 1 else jnp.concatenate(held, axis=0)
    diagonal, near, far = square
    early = [swap(held[0], near), swap(held[0], diagonal), held[0]]
    early = jnp.concatenate(early, axis=0)
    both = swap(joint, far)
    late = [swap(held[1], near), swap(held[1], diagonal), held[1]]
    late = jnp.concatenate(late, axis=0)
    early_other = swap(early, 1)
    late, _ = lax.optimization_barrier((late, early_other))
    both_other, late_other = swap(both, 1), swap(late, 1)
    orders = [(0, 2), (0, 1), (0, 0)], [(1, 2), (1, 1), (1, 0)], [(0, 3), (1, 3)]
    groups = [(side, order) for order in orders for side in range(2)]
    shape = (tokens, q_weight.shape[1])
    outs = second[1:3]
    shapes = [(shape, F32)] + [(x.shape, x.dtype, pltpu.HBM) for x in outs]
    before, *outs = local_call(
        functools.partial(first_dots_kernel, n, groups[:-1]),
        shapes,
        "first_dots",
        *(early, early_other, late, late_other, both, q_weight, *outs),
        scratch=[pltpu.SemaphoreType.DMA((2,))],
    )
    kernel = functools.partial(last_dot_kernel, n, groups[-1])
    (next_queries,) = local_call(
        kernel, [(shape, BF16)], "last_dot", both_other, before, q_weight
    )
    return (*outs, next_queries)


def solution(mesh):
    in_specs = (
        P(("replica", "tp"), None),
        P("replica", "tp"),
        P("replica", None),
        P("replica", None),
        P("tp", None),
        P(),
        P(None, "tp"),
    )
    out_specs = (P(("replica", "tp"), None), P(("replica", "tp"), None), P("replica", "tp"))
    return jax.shard_map(
        on_device, mesh=mesh, in_specs=in_specs, out_specs=out_specs, check_vma=False
    )
```

```python
import functools

import jax
import jax.numpy as jnp
from jax import lax
from jax.experimental import pallas as pl
from jax.experimental.pallas import tpu as pltpu
from jax.sharding import PartitionSpec as P

HD = 128
QB = 128
EPS = 1e-06
F32 = jnp.float32
BF16 = jnp.bfloat16
PIECES = 4
STEPS = 8
VMEM_LIMIT = 24 << 20
SMALL_LIMIT = 16 << 20


def late_levels(n):
    return [1 << b for b in range(3, n.bit_length() - 1)]


def owner_token(row, device, n):
    bits = [2, 6] + late_levels(n)
    distance = row >> (len(bits) + 1)
    which = (row >> len(bits)) & 1
    block = row ^ which
    for place, bit in enumerate(bits):
        distance = distance ^ (((block >> (len(bits) - 1 - place)) & 1) * bit)
    return ((device ^ distance) << 1) | which


def attend_kernel(
    n, queries, keys, values, weight, context, held, query, key, value, small, large
):
    device = lax.axis_index("tp")
    tokens = queries.shape[0]
    heads = queries.shape[1] // HD
    group = heads * n // (keys.shape[1] // HD)
    copies = [pltpu.make_async_copy(queries, query, small.at[0])]
    for h in range(heads):
        at = pl.ds(pl.multiple_of(lax.div(device * heads + h, group) * HD, HD), HD)
        copies.append(pltpu.make_async_copy(keys.at[:, at], key.at[h], small.at[1 + 2 * h]))
        copies.append(pltpu.make_async_copy(values.at[:, at], value.at[h], small.at[2 + 2 * h]))
    depth = held.shape[0] // PIECES
    late = []
    for c in range(PIECES):
        part = pl.ds(c * depth, depth)
        late.append(pltpu.make_async_copy(weight.at[part], held.at[part], large.at[c]))
    for copy in copies + late:
        copy.start()
    row = lax.broadcasted_iota(jnp.int32, (tokens, tokens), 0)
    col = lax.broadcasted_iota(jnp.int32, (tokens, tokens), 1)
    token = owner_token(row, device, n)
    pick = (token == col).astype(F32).astype(BF16)
    for copy in copies:
        copy.wait()
    ordered = jnp.dot(pick, query[...], preferred_element_type=F32).astype(BF16)
    for h in range(heads):
        scores = lax.dot_general(
            ordered[:, h * HD : (h + 1) * HD],
            key[h],
            (((1,), (1,)), ((), ())),
            preferred_element_type=F32,
        ) / jnp.sqrt(F32(HD))
        scores = jnp.where(col <= token, scores, F32(-1e30))
        weights = jnp.exp(scores - jnp.max(scores, axis=1, keepdims=True))
        probs = (weights / jnp.sum(weights, axis=1, keepdims=True)).astype(BF16)
        context[:, h * HD : (h + 1) * HD] = jnp.dot(
            probs, value[h], preferred_element_type=F32
        ).astype(BF16)
    for copy in late:
        copy.wait()


def in_hbm(*arrays):
    return [pltpu.with_memory_space_constraint(x, pltpu.HBM) for x in arrays]


def attend(n, queries, keys, values, weight):
    tokens = queries.shape[0]
    heads = queries.shape[1] // HD
    whole = pl.BlockSpec(memory_space=pltpu.VMEM)
    return pl.pallas_call(
        functools.partial(attend_kernel, n),
        out_shape=[
            jax.ShapeDtypeStruct(queries.shape, BF16),
            pltpu.VMEM(weight.shape, BF16),
        ],
        in_specs=[pl.BlockSpec(memory_space=pltpu.HBM)] * 4,
        out_specs=[whole] * 2,
        scratch_shapes=[
            pltpu.VMEM(queries.shape, BF16),
            pltpu.VMEM((heads, tokens, HD), BF16),
            pltpu.VMEM((heads, tokens, HD), BF16),
            pltpu.SemaphoreType.DMA((1 + 2 * heads,)),
            pltpu.SemaphoreType.DMA((PIECES,)),
        ],
        compiler_params=pltpu.CompilerParams(vmem_limit_bytes=VMEM_LIMIT),
        cost_estimate=pl.CostEstimate(
            flops=0, bytes_accessed=2 * weight.size, transcendentals=0
        ),
        name="attend",
    )(*in_hbm(queries, keys, values, weight))


def parts(ref):
    width = ref.shape[1] // STEPS
    return [pl.ds(c * width, width) for c in range(STEPS)]


def split_kernel(which, kept, got, own, *pieces):
    rows = got.shape[0]
    part = rows // 4
    for at in parts(got):
        total = kept[which * rows : (which + 1) * rows, at] + got[:, at].astype(F32)
        own[:, at] = total[:part]
        for k, piece in enumerate(pieces, 1):
            piece[:, at] = total[k * part : (k + 1) * part].astype(BF16)


def settle_kernel(which, own, old, *refs):
    *arrived, total, turned = refs
    for at in parts(own):
        value = own[:, at]
        for piece in arrived:
            value = value + piece[:, at].astype(F32)
        row = lax.broadcasted_iota(jnp.int32, value.shape, 0)
        value = value + jnp.where(row == which, old[:, at].astype(F32), F32(0))
        total[:, at] = value
        turned[:, at] = jnp.concatenate([value[1:], value[:1]], axis=0).astype(BF16)


def encode_kernel(total, arrived, gain, *refs):
    if len(refs) > 4:
        first, *before, normed, codes, scales, joint, decoded = refs
    else:
        before, (normed, codes, scales, decoded) = (), refs
    blocks = total.shape[1] // QB
    row = lax.broadcasted_iota(jnp.int32, (total.shape[0], QB), 0)
    lane = lax.broadcasted_iota(jnp.int32, (total.shape[0], blocks), 1)
    all_scales = jnp.zeros(scales.shape, F32)
    squares = jnp.zeros(row.shape, F32)
    for b in range(blocks):
        at = pl.ds(b * QB, QB)
        stream = total[:, at] + arrived[:, at].astype(F32)
        scale = jnp.max(jnp.abs(stream), axis=1, keepdims=True) + EPS
        code = (stream / scale).astype(BF16).astype(F32)
        value = code * scale
        squares += value * value
        decoded[:, at] = value
        if before:
            code = jnp.where(row == 0, before[0][:, at].astype(F32), code)
        codes[:, at] = code.astype(BF16)
        all_scales = jnp.where(lane == b, scale, all_scales)
    if before:
        all_scales = jnp.where(
            lax.broadcasted_iota(jnp.int32, scales.shape, 0) == 0, before[1][...], all_scales
        )
    scales[...] = all_scales
    mean_sq = jnp.sum(squares, axis=1, keepdims=True) / total.shape[1]
    factor = lax.rsqrt(mean_sq + 1e-05)
    for at in parts(total):
        value = decoded[:, at] * factor * gain[:, at]
        normed[:, at] = value.astype(BF16)
        if before:
            joint[:, at] = jnp.concatenate([first[:, at].astype(F32), value], axis=0).astype(BF16)


def times(rows, weight):
    depth = weight.shape[0] // STEPS
    count = sum(r.shape[0] for r in rows)
    total = jnp.zeros((count, weight.shape[1]), F32)
    for c in range(STEPS):
        part = pl.ds(c * depth, depth)
        block = jnp.concatenate([r[:, part] for r in rows], axis=0)
        total += jnp.dot(block, weight[part], preferred_element_type=F32)
    return total


def placed(n, tokens, values, side, order):
    count = values.shape[0]
    part = count // len(order)
    at = lax.broadcasted_iota(jnp.int32, (tokens, count), 1)
    row = at & (part - 1)
    for k, (which, place) in enumerate(order):
        here = (at >> (part.bit_length() - 1)) == k
        row = row + jnp.where(here, (8 * side + 4 * which + place) * part, 0)
    token = lax.broadcasted_iota(jnp.int32, (tokens, count), 0)
    pick = (owner_token(row, lax.axis_index("tp"), n) == token).astype(F32).astype(BF16)
    return jnp.dot(pick, values.astype(BF16), preferred_element_type=F32)


def first_dots_kernel(n, groups, *refs):
    *rows, weight, codes, scales, out, codes_out, scales_out, sems = refs
    copies = [
        pltpu.make_async_copy(codes, codes_out, sems.at[0]),
        pltpu.make_async_copy(scales, scales_out, sems.at[1]),
    ]
    for copy in copies:
        copy.start()
    values = times(rows, weight)
    total = jnp.zeros(out.shape, F32)
    start = 0
    for ref, (side, order) in zip(rows, groups):
        stop = start + ref.shape[0]
        total += placed(n, out.shape[0], values[start:stop], side, order)
        start = stop
    out[...] = total
    for copy in copies:
        copy.wait()


def last_dot_kernel(n, group, rows, before, weight, out):
    values = times([rows], weight)
    out[...] = (before[...] + placed(n, out.shape[0], values, *group)).astype(BF16)


def local_call(kernel, shapes, name, *operands, scratch=()):
    spec = pl.BlockSpec(memory_space=pltpu.VMEM)
    spaces = [space[0] if space else pltpu.VMEM for _, _, *space in shapes]
    return pl.pallas_call(
        kernel,
        out_shape=[
            (space[0] if space else jax.ShapeDtypeStruct)(shape, dtype)
            for shape, dtype, *space in shapes
        ],
        in_specs=[spec] * len(operands),
        out_specs=[pl.BlockSpec(memory_space=space) for space in spaces],
        scratch_shapes=list(scratch),
        compiler_params=pltpu.CompilerParams(vmem_limit_bytes=SMALL_LIMIT),
        cost_estimate=pl.CostEstimate(
            flops=0, bytes_accessed=sum(2 * x.size for x in operands), transcendentals=0
        ),
        name=name,
    )(*operands)


def on_device(residual, queries, key_rows, value_rows, out_weight, norm_gain, q_weight):
    n = lax.axis_size("tp")
    tokens = queries.shape[0]
    D = residual.shape[1]
    levels = late_levels(n)
    square = (6, 2, 4)

    def swap(x, distance):
        return lax.ppermute(x, "tp", [(i, i ^ distance) for i in range(n)])

    half, quarter = tokens // 2, tokens // 4
    part, pair = quarter // 4, (2, D)
    gain = norm_gain.reshape(1, D)
    context, weight = attend(n, queries, key_rows, value_rows, out_weight)
    sent = jnp.dot(context[half:], weight, preferred_element_type=F32).astype(BF16)
    kept = jnp.dot(context[:half], weight, preferred_element_type=F32)
    got = [swap(sent[:quarter], 1)]
    kept, sent = lax.optimization_barrier((kept, sent))
    got.append(swap(sent[quarter:], 1))

    def reduce(which):
        shapes = [((part, D), F32)] + [((part, D), BF16)] * 3
        kernel = functools.partial(split_kernel, which)
        total, *pieces = local_call(kernel, shapes, f"split{which}", kept, got[which])
        arrived = [swap(piece, distance) for piece, distance in zip(pieces, square)]
        if len(levels) > 1:
            for piece in arrived:
                total = total + piece.astype(F32)
            arrived = []
        for level in levels[:-1]:
            rest = total.shape[0] // 2
            total = total[:rest] + swap(total[rest:].astype(BF16), level).astype(F32)
        kernel = functools.partial(settle_kernel, which)
        shapes = [(pair, F32), (pair, BF16)]
        return local_call(kernel, shapes, f"settle{which}", total, residual, *arrived)

    def widen(held):
        for level in levels[-2::-1]:
            held = jnp.concatenate([held, swap(held, level)], axis=0)
        return held

    sums = [reduce(which) for which in range(2)]
    sums = [(total, swap(turned, levels[-1])) for total, turned in sums]
    shapes = [(pair, BF16), (pair, BF16, pltpu.VMEM), ((2, D // QB), F32, pltpu.VMEM)]
    scratch = [pltpu.VMEM(pair, F32)]
    first = local_call(encode_kernel, shapes, "encode0", *sums[0], gain, scratch=scratch)
    shapes.append(((4, D), BF16))
    second = local_call(encode_kernel, shapes, "encode1", *sums[1], gain, *first, scratch=scratch)
    held = [widen(first[0]), widen(second[0])]
    joint = second[3] if len(levels) == 1 else jnp.concatenate(held, axis=0)
    diagonal, near, far = square
    early = [swap(held[0], near), swap(held[0], diagonal), held[0]]
    early = jnp.concatenate(early, axis=0)
    both = swap(joint, far)
    late = [swap(held[1], diagonal), swap(held[1], near), held[1]]
    late = jnp.concatenate(late, axis=0)
    early_other = swap(early, 1)
    late, _ = lax.optimization_barrier((late, early_other))
    both_other, late_other = swap(both, 1), swap(late, 1)
    orders = [(0, 2), (0, 1), (0, 0)], [(1, 1), (1, 2), (1, 0)], [(0, 3), (1, 3)]
    groups = [(side, order) for order in orders for side in range(2)]
    shape = (tokens, q_weight.shape[1])
    outs = second[1:3]
    shapes = [(shape, F32)] + [(x.shape, x.dtype, pltpu.HBM) for x in outs]
    before, *outs = local_call(
        functools.partial(first_dots_kernel, n, groups[:-1]),
        shapes,
        "first_dots",
        *(early, early_other, late, late_other, both, q_weight, *outs),
        scratch=[pltpu.SemaphoreType.DMA((2,))],
    )
    kernel = functools.partial(last_dot_kernel, n, groups[-1])
    (next_queries,) = local_call(
        kernel, [(shape, BF16)], "last_dot", both_other, before, q_weight
    )
    return (*outs, next_queries)


def solution(mesh):
    in_specs = (
        P(("replica", "tp"), None),
        P("replica", "tp"),
        P("replica", None),
        P("replica", None),
        P("tp", None),
        P(),
        P(None, "tp"),
    )
    out_specs = (P(("replica", "tp"), None), P(("replica", "tp"), None), P("replica", "tp"))
    return jax.shard_map(
        on_device, mesh=mesh, in_specs=in_specs, out_specs=out_specs, check_vma=False
    )
```

```python
import functools

import jax
import jax.numpy as jnp
from jax import lax
from jax.experimental import pallas as pl
from jax.experimental.pallas import tpu as pltpu
from jax.sharding import PartitionSpec as P

HD = 128
QB = 128
EPS = 1e-06
F32 = jnp.float32
BF16 = jnp.bfloat16
PIECES = 2
STEPS = 8
VMEM_LIMIT = 24 << 20
SMALL_LIMIT = 16 << 20


def late_levels(n):
    return [1 << b for b in range(3, n.bit_length() - 1)]


def owner_token(row, device, n):
    bits = [2, 6] + late_levels(n)
    distance = row >> (len(bits) + 1)
    which = (row >> len(bits)) & 1
    block = row ^ which
    for place, bit in enumerate(bits):
        distance = distance ^ (((block >> (len(bits) - 1 - place)) & 1) * bit)
    return ((device ^ distance) << 1) | which


def attend_kernel(
    n, queries, keys, values, weight, context, held, query, key, value, small, large
):
    device = lax.axis_index("tp")
    tokens = queries.shape[0]
    heads = queries.shape[1] // HD
    group = heads * n // (keys.shape[1] // HD)
    copies = [pltpu.make_async_copy(queries, query, small.at[0])]
    for h in range(heads):
        at = pl.ds(pl.multiple_of(lax.div(device * heads + h, group) * HD, HD), HD)
        copies.append(pltpu.make_async_copy(keys.at[:, at], key.at[h], small.at[1 + 2 * h]))
        copies.append(pltpu.make_async_copy(values.at[:, at], value.at[h], small.at[2 + 2 * h]))
    depth = held.shape[0] // PIECES
    late = []
    for c in range(PIECES):
        part = pl.ds(c * depth, depth)
        late.append(pltpu.make_async_copy(weight.at[part], held.at[part], large.at[c]))
    for copy in copies + late:
        copy.start()
    row = lax.broadcasted_iota(jnp.int32, (tokens, tokens), 0)
    col = lax.broadcasted_iota(jnp.int32, (tokens, tokens), 1)
    token = owner_token(row, device, n)
    pick = (token == col).astype(F32).astype(BF16)
    for copy in copies:
        copy.wait()
    ordered = jnp.dot(pick, query[...], preferred_element_type=F32).astype(BF16)
    for h in range(heads):
        scores = lax.dot_general(
            ordered[:, h * HD : (h + 1) * HD],
            key[h],
            (((1,), (1,)), ((), ())),
            preferred_element_type=F32,
        ) / jnp.sqrt(F32(HD))
        scores = jnp.where(col <= token, scores, F32(-1e30))
        weights = jnp.exp(scores - jnp.max(scores, axis=1, keepdims=True))
        probs = (weights / jnp.sum(weights, axis=1, keepdims=True)).astype(BF16)
        context[:, h * HD : (h + 1) * HD] = jnp.dot(
            probs, value[h], preferred_element_type=F32
        ).astype(BF16)
    for copy in late:
        copy.wait()


def in_hbm(*arrays):
    return [pltpu.with_memory_space_constraint(x, pltpu.HBM) for x in arrays]


def attend(n, queries, keys, values, weight):
    tokens = queries.shape[0]
    heads = queries.shape[1] // HD
    whole = pl.BlockSpec(memory_space=pltpu.VMEM)
    return pl.pallas_call(
        functools.partial(attend_kernel, n),
        out_shape=[
            jax.ShapeDtypeStruct(queries.shape, BF16),
            pltpu.VMEM(weight.shape, BF16),
        ],
        in_specs=[pl.BlockSpec(memory_space=pltpu.HBM)] * 4,
        out_specs=[whole] * 2,
        scratch_shapes=[
            pltpu.VMEM(queries.shape, BF16),
            pltpu.VMEM((heads, tokens, HD), BF16),
            pltpu.VMEM((heads, tokens, HD), BF16),
            pltpu.SemaphoreType.DMA((1 + 2 * heads,)),
            pltpu.SemaphoreType.DMA((PIECES,)),
        ],
        compiler_params=pltpu.CompilerParams(vmem_limit_bytes=VMEM_LIMIT),
        cost_estimate=pl.CostEstimate(
            flops=0, bytes_accessed=2 * weight.size, transcendentals=0
        ),
        name="attend",
    )(*in_hbm(queries, keys, values, weight))


def parts(ref):
    width = ref.shape[1] // STEPS
    return [pl.ds(c * width, width) for c in range(STEPS)]


def split_kernel(which, kept, got, own, *pieces):
    rows = got.shape[0]
    part = rows // 4
    for at in parts(got):
        total = kept[which * rows : (which + 1) * rows, at] + got[:, at].astype(F32)
        own[:, at] = total[:part]
        for k, piece in enumerate(pieces, 1):
            piece[:, at] = total[k * part : (k + 1) * part].astype(BF16)


def settle_kernel(which, own, old, *refs):
    *arrived, total, turned = refs
    for at in parts(own):
        value = own[:, at]
        for piece in arrived:
            value = value + piece[:, at].astype(F32)
        row = lax.broadcasted_iota(jnp.int32, value.shape, 0)
        value = value + jnp.where(row == which, old[:, at].astype(F32), F32(0))
        total[:, at] = value
        turned[:, at] = jnp.concatenate([value[1:], value[:1]], axis=0).astype(BF16)


def encode_kernel(total, arrived, gain, *refs):
    if len(refs) > 4:
        first, *before, normed, codes, scales, joint, decoded = refs
    else:
        before, (normed, codes, scales, decoded) = (), refs
    blocks = total.shape[1] // QB
    row = lax.broadcasted_iota(jnp.int32, (total.shape[0], QB), 0)
    lane = lax.broadcasted_iota(jnp.int32, (total.shape[0], blocks), 1)
    all_scales = jnp.zeros(scales.shape, F32)
    squares = jnp.zeros(row.shape, F32)
    for b in range(blocks):
        at = pl.ds(b * QB, QB)
        stream = total[:, at] + arrived[:, at].astype(F32)
        scale = jnp.max(jnp.abs(stream), axis=1, keepdims=True) + EPS
        code = (stream / scale).astype(BF16).astype(F32)
        value = code * scale
        squares += value * value
        decoded[:, at] = value
        if before:
            code = jnp.where(row == 0, before[0][:, at].astype(F32), code)
        codes[:, at] = code.astype(BF16)
        all_scales = jnp.where(lane == b, scale, all_scales)
    if before:
        all_scales = jnp.where(
            lax.broadcasted_iota(jnp.int32, scales.shape, 0) == 0, before[1][...], all_scales
        )
    scales[...] = all_scales
    mean_sq = jnp.sum(squares, axis=1, keepdims=True) / total.shape[1]
    factor = lax.rsqrt(mean_sq + 1e-05)
    for at in parts(total):
        value = decoded[:, at] * factor * gain[:, at]
        normed[:, at] = value.astype(BF16)
        if before:
            joint[:, at] = jnp.concatenate([first[:, at].astype(F32), value], axis=0).astype(BF16)


def times(rows, weight):
    depth = weight.shape[0] // STEPS
    count = sum(r.shape[0] for r in rows)
    total = jnp.zeros((count, weight.shape[1]), F32)
    for c in range(STEPS):
        part = pl.ds(c * depth, depth)
        block = jnp.concatenate([r[:, part] for r in rows], axis=0)
        total += jnp.dot(block, weight[part], preferred_element_type=F32)
    return total


def placed(n, tokens, values, side, order):
    count = values.shape[0]
    part = count // len(order)
    at = lax.broadcasted_iota(jnp.int32, (tokens, count), 1)
    row = at & (part - 1)
    for k, (which, place) in enumerate(order):
        here = (at >> (part.bit_length() - 1)) == k
        row = row + jnp.where(here, (8 * side + 4 * which + place) * part, 0)
    token = lax.broadcasted_iota(jnp.int32, (tokens, count), 0)
    pick = (owner_token(row, lax.axis_index("tp"), n) == token).astype(F32).astype(BF16)
    return jnp.dot(pick, values.astype(BF16), preferred_element_type=F32)


def first_dots_kernel(n, groups, *refs):
    *rows, weight, codes, scales, out, codes_out, scales_out, sems = refs
    copies = [
        pltpu.make_async_copy(codes, codes_out, sems.at[0]),
        pltpu.make_async_copy(scales, scales_out, sems.at[1]),
    ]
    for copy in copies:
        copy.start()
    values = times(rows, weight)
    total = jnp.zeros(out.shape, F32)
    start = 0
    for ref, (side, order) in zip(rows, groups):
        stop = start + ref.shape[0]
        total += placed(n, out.shape[0], values[start:stop], side, order)
        start = stop
    out[...] = total
    for copy in copies:
        copy.wait()


def last_dot_kernel(n, group, rows, before, weight, out):
    values = times([rows], weight)
    out[...] = (before[...] + placed(n, out.shape[0], values, *group)).astype(BF16)


def local_call(kernel, shapes, name, *operands, scratch=()):
    spec = pl.BlockSpec(memory_space=pltpu.VMEM)
    spaces = [space[0] if space else pltpu.VMEM for _, _, *space in shapes]
    return pl.pallas_call(
        kernel,
        out_shape=[
            (space[0] if space else jax.ShapeDtypeStruct)(shape, dtype)
            for shape, dtype, *space in shapes
        ],
        in_specs=[spec] * len(operands),
        out_specs=[pl.BlockSpec(memory_space=space) for space in spaces],
        scratch_shapes=list(scratch),
        compiler_params=pltpu.CompilerParams(vmem_limit_bytes=SMALL_LIMIT),
        cost_estimate=pl.CostEstimate(
            flops=0, bytes_accessed=sum(2 * x.size for x in operands), transcendentals=0
        ),
        name=name,
    )(*operands)


def on_device(residual, queries, key_rows, value_rows, out_weight, norm_gain, q_weight):
    n = lax.axis_size("tp")
    tokens = queries.shape[0]
    D = residual.shape[1]
    levels = late_levels(n)
    square = (6, 2, 4)

    def swap(x, distance):
        return lax.ppermute(x, "tp", [(i, i ^ distance) for i in range(n)])

    half, quarter = tokens // 2, tokens // 4
    part, pair = quarter // 4, (2, D)
    gain = norm_gain.reshape(1, D)
    context, weight = attend(n, queries, key_rows, value_rows, out_weight)
    sent = jnp.dot(context[half:], weight, preferred_element_type=F32).astype(BF16)
    kept = jnp.dot(context[:half], weight, preferred_element_type=F32)
    got = [swap(sent[:quarter], 1)]
    kept, sent = lax.optimization_barrier((kept, sent))
    got.append(swap(sent[quarter:], 1))

    def reduce(which):
        shapes = [((part, D), F32)] + [((part, D), BF16)] * 3
        kernel = functools.partial(split_kernel, which)
        total, *pieces = local_call(kernel, shapes, f"split{which}", kept, got[which])
        arrived = [swap(piece, distance) for piece, distance in zip(pieces, square)]
        if len(levels) > 1:
            for piece in arrived:
                total = total + piece.astype(F32)
            arrived = []
        for level in levels[:-1]:
            rest = total.shape[0] // 2
            total = total[:rest] + swap(total[rest:].astype(BF16), level).astype(F32)
        kernel = functools.partial(settle_kernel, which)
        shapes = [(pair, F32), (pair, BF16)]
        return local_call(kernel, shapes, f"settle{which}", total, residual, *arrived)

    def widen(held):
        for level in levels[-2::-1]:
            held = jnp.concatenate([held, swap(held, level)], axis=0)
        return held

    sums = [reduce(which) for which in range(2)]
    sums = [(total, swap(turned, levels[-1])) for total, turned in sums]
    shapes = [(pair, BF16), (pair, BF16, pltpu.VMEM), ((2, D // QB), F32, pltpu.VMEM)]
    scratch = [pltpu.VMEM(pair, F32)]
    first = local_call(encode_kernel, shapes, "encode0", *sums[0], gain, scratch=scratch)
    shapes.append(((4, D), BF16))
    second = local_call(encode_kernel, shapes, "encode1", *sums[1], gain, *first, scratch=scratch)
    held = [widen(first[0]), widen(second[0])]
    joint = second[3] if len(levels) == 1 else jnp.concatenate(held, axis=0)
    diagonal, far, near = square
    early = [swap(held[0], near), swap(held[0], diagonal), held[0]]
    early = jnp.concatenate(early, axis=0)
    both = swap(joint, far)
    late = [swap(held[1], near), swap(held[1], diagonal), held[1]]
    late = jnp.concatenate(late, axis=0)
    early_other = swap(early, 1)
    late, _ = lax.optimization_barrier((late, early_other))
    both_other, late_other = swap(both, 1), swap(late, 1)
    orders = [(0, 3), (0, 1), (0, 0)], [(1, 3), (1, 1), (1, 0)], [(0, 2), (1, 2)]
    groups = [(side, order) for order in orders for side in range(2)]
    shape = (tokens, q_weight.shape[1])
    outs = second[1:3]
    shapes = [(shape, F32)] + [(x.shape, x.dtype, pltpu.HBM) for x in outs]
    before, *outs = local_call(
        functools.partial(first_dots_kernel, n, groups[:-1]),
        shapes,
        "first_dots",
        *(early, early_other, late, late_other, both, q_weight, *outs),
        scratch=[pltpu.SemaphoreType.DMA((2,))],
    )
    kernel = functools.partial(last_dot_kernel, n, groups[-1])
    (next_queries,) = local_call(
        kernel, [(shape, BF16)], "last_dot", both_other, before, q_weight
    )
    return (*outs, next_queries)


def solution(mesh):
    in_specs = (
        P(("replica", "tp"), None),
        P("replica", "tp"),
        P("replica", None),
        P("replica", None),
        P("tp", None),
        P(),
        P(None, "tp"),
    )
    out_specs = (P(("replica", "tp"), None), P(("replica", "tp"), None), P("replica", "tp"))
    return jax.shard_map(
        on_device, mesh=mesh, in_specs=in_specs, out_specs=out_specs, check_vma=False
    )
```
